32 devices in a mesh: dp: 8 (over z, x), section: 4 (over y, core).
Axes of the slice: x: 2, y: 2, z: 4, core: 2. Of those that a mesh axis runs over, the one named last changes fastest.
Arguments:
- tiles: bfloat16 [32, 128, 1536], P('dp'), may hold values from -6 to 6
- slide_ids: int32 [32, 128], P('dp'), may hold values from 0 to 2, never falling along the last dimension, each value on 1 to 64 neighbouring positions
- coords: int32 [2, 32, 128], P(None, 'dp'), may hold values from 0 to 255
- known: int32 [32, 3, 18], P('dp'), may hold values from 0 to 1
- labels: int32 [32, 3, 18], P('dp'), may hold values 0 or 1
- mats: float32 [4, 3, 768, 3072], P('section', None, 'dp')
- mats_m: float32 [4, 3, 768, 3072], P('section', None, 'dp'), may hold values from -5.722046e-06 to 5.722046e-06
- mats_v: float32 [4, 3, 768, 3072], P('section', None, 'dp'), may hold values from 4.455824e-12 to 1.7789412e-11
- gains: float32 [4, 2, 768], P('section')
- gains_m: float32 [4, 2, 768], P('section'), may hold values from -2.2888184e-05 to 2.2888184e-05
- gains_v: float32 [4, 2, 768], P('section'), may hold values from 7.129319e-11 to 2.846306e-10
- final_gain: float32 [768], P('section'), may hold values from 0.5 to 1.5
- fgain_m: float32 [768], P('section'), may hold values from -2.2888184e-05 to 2.2888184e-05
- fgain_v: float32 [768], P('section'), may hold values from 7.129319e-11 to 2.846306e-10
- w_in: float32 [1536, 768], P('section'), may hold values from -0.15625 to 0.15625
- win_m: float32 [1536, 768], P('section'), may hold values from -5.722046e-06 to 5.722046e-06
- win_v: float32 [1536, 768], P('section'), may hold values from 4.455824e-12 to 1.7789412e-11
- head: float32 [768, 18], P('section'), may hold values from -0.21875 to 0.21875
- head_m: float32 [768, 18], P('section'), may hold values from -5.722046e-06 to 5.722046e-06
- head_v: float32 [768, 18], P('section'), may hold values from 4.455824e-12 to 1.7789412e-11
Outputs:
- grad_norm: float32 [], replicated
- loss_sum: float32 [], replicated
- known_count: float32 [], replicated
- mats_m_new: float32 [4, 3, 768, 3072], P('section', None, 'dp')
- mats_v_new: float32 [4, 3, 768, 3072], P('section', None, 'dp')
- mats_new: float32 [4, 3, 768, 3072], P('section', None, 'dp')
- gains_m_new: float32 [4, 2, 768], P('section')
- gains_v_new: float32 [4, 2, 768], P('section')
- gains_new: float32 [4, 2, 768], P('section')
- fgain_m_new: float32 [768], P('section')
- fgain_v_new: float32 [768], P('section')
- fgain_new: float32 [768], P('section')
- win_m_new: float32 [1536, 768], P('section')
- win_v_new: float32 [1536, 768], P('section')
- win_new: float32 [1536, 768], P('section')
- head_m_new: float32 [768, 18], P('section')
- head_v_new: float32 [768, 18], P('section')
- head_new: float32 [768, 18], P('section')
The draws below stay inside these ranges and needn't reach their ends.
Inputs may be any that keep to these rules, and one draw needn't show every extreme that they name: `slide_ids`: within a pack slide numbers never fall; each of the 3 slides has 1 to 64 tiles.
All inputs are finite; a program needn't handle non-finite values. No bound on the sum of `labels` on one device may be relied on, other than what follows from the above.
Results may differ from the reference program's by a relative error of at most 0.015.
Values may be sent and summed in bfloat16 or wider, within the bound.
No kernel may reach another device: no remote copies, remote signals or barrier semaphores. Data moves between devices by JAX's collectives and lax.ppermute only.
A program may use at most 576 MiB of HBM per device.

```python
import math
import jax
import jax.numpy as jnp
import numpy as np
from jax import lax

D = 768
HEADS = 16
FF = 3072
IN = 1536
GENES = 18
MB_TOK = 128
SLIDES = 3
STEP = 10
HD = 48
SECTIONS = 4
PACKS = 32
PARAMS = 29511936


def draw_mats(key, part):
    key = jax.random.fold_in(key, 11)
    shape = (SECTIONS, 3, D, FF)
    base = jax.random.normal(key, shape, jnp.float32)
    column = jnp.arange(FF)
    attn = jnp.where(column < 3 * D, (2.0 * D) ** (-0.5), 4.0 * D ** (-0.5))
    scale = jnp.stack([attn, jnp.full((FF,), D ** (-0.5)), jnp.full((FF,), 1.5 * FF ** (-0.5))])
    return base * scale[None, :, None, :]


def draw_gains(key, part):
    key = jax.random.fold_in(key, 12)
    feature = jnp.arange(D, dtype=jnp.float32) / (D - 1)
    depth = jnp.arange(SECTIONS, dtype=jnp.float32)
    noise = jax.random.uniform(key, (SECTIONS, 2, D), jnp.float32, 0.85, 1.15)
    base = 0.6 * 3.0 ** feature
    return base[None, None, :] * (1.0 + 0.25 * depth)[:, None, None] * noise


def draw_known(key, part):
    key = jax.random.fold_in(key, 13)
    pack = jnp.arange(PACKS, dtype=jnp.int32)
    limit = 20 + 60 * pack // max(PACKS - 1, 1)
    roll = jax.random.randint(key, (PACKS, SLIDES, GENES), 0, 100)
    return (roll < limit[:, None, None]).astype(jnp.int32)


def set_ends(result, rng, smallest, largest):
    longest = result.shape.index(max(result.shape))
    spots = []
    for shift in (0, 1):
        where = [jax.random.randint(jax.random.fold_in(rng, axis), (), 0, length) for axis, length in enumerate(result.shape)]
        where[longest] = (where[longest] + shift) % result.shape[longest]
        spots.append(tuple(where))
    return result.at[spots[0]].set(smallest).at[spots[1]].set(largest)


def steps_of(rng, dims, cuts, low, high):
    level = 1.0
    for position, parts in cuts:
        draws = jax.random.uniform(jax.random.fold_in(jax.random.fold_in(rng, 6), position), (parts,), jnp.float32, low / len(cuts), high / len(cuts))
        level = level * jnp.repeat(jnp.exp(draws), dims[position] // parts).reshape((-1,) + (1,) * (len(dims) - 1 - position))
    return level


def length_profile(number_of, total, reach, lean):
    loads = [(1 << 20) // math.isqrt(rank ** lean) + 1 for rank in range(2, number_of + 1)]
    spare, given = total - reach - (number_of - 1), [1] * (number_of - 1)
    while spare > 0:
        free = [i for i in range(number_of - 1) if given[i] < reach]
        pool, budget = sum([loads[i] for i in free]), spare
        for i in free:
            extra = min(reach - given[i], max(1, budget * loads[i] // pool), spare)
            given[i] = given[i] + extra
            spare = spare - extra
    return np.array([reach] + given)


def ragged_sizes(own_key, count, total, most, slope):
    if count == 2:
        one = jax.random.randint(own_key, (), max(1, total - most), min(most, total - 1) + 1)
        return jnp.stack([one, total - one])
    lengths = jnp.asarray(length_profile(count, total, most, slope), jnp.int32)
    twos = (count - 1) // 2
    giver, taker = lengths[1:1 + 2 * twos:2], lengths[2:2 + 2 * twos:2]
    margin = jnp.minimum(giver - 1, most - taker)
    moved = jax.random.randint(jax.random.fold_in(own_key, 1), (twos,), 0, 1 << 20) % (margin + 1)
    lengths = lengths.at[1:1 + 2 * twos:2].set(giver - moved).at[2:2 + 2 * twos:2].set(taker + moved)
    return lengths[jax.random.permutation(jax.random.fold_in(own_key, 2), count)]


def gaussian(stream_key, shape, width, most, pieces=(), held_as=jnp.bfloat16):
    result = width * jax.random.normal(stream_key, shape, jnp.float32)
    if pieces:
        result = result * steps_of(stream_key, shape, pieces, -0.22, 0.18)
    return jnp.clip(result, -most, most).astype(held_as)


def setup_inputs(seed: int = 0) -> dict:
    key_of = jax.random.split(jax.random.key(seed), 21)
    return {
        "tiles": gaussian(key_of[0], (PACKS, MB_TOK, IN), 1.0, 6.0, ((0, 8),)),
        "slide_ids": jax.vmap(lambda own: jnp.searchsorted(jnp.cumsum(ragged_sizes(own, SLIDES, MB_TOK, MB_TOK // 2, 2)), jnp.arange(MB_TOK), side="right"))(jax.random.split(key_of[1], PACKS)).reshape((PACKS, MB_TOK)).astype(jnp.int32),
        "coords": set_ends(jax.random.randint(key_of[2], (2, PACKS, MB_TOK), 0, 256), jax.random.fold_in(key_of[2], 1), 0, 255).astype(jnp.int32),
        "known": draw_known(jax.random.fold_in(key_of[20], 71), 0),
        "labels": set_ends((jax.random.randint(key_of[4], (PACKS, SLIDES, GENES), 0, 3) < 1).astype(jnp.int32), jax.random.fold_in(key_of[4], 1), 0, 1),
        "mats": draw_mats(jax.random.fold_in(key_of[20], 71), 0),
        "mats_m": gaussian(key_of[6], (SECTIONS, 3, D, FF), (0.111 * 0.05 / PARAMS ** 0.5), 5.7220458984375e-06, ((0, 4), (2, 8)), jnp.float32),
        "mats_v": jnp.clip(jnp.exp(math.log(1.7789412304347607e-11) - 1.3843914 * jax.random.uniform(key_of[7], (SECTIONS, 3, D, FF), jnp.float32) ** steps_of(key_of[7], (SECTIONS, 3, D, FF), ((0, 4), (2, 8)), -0.2, 0.2)), 4.4558241645009655e-12, 1.7789412304347607e-11),
        "gains": draw_gains(jax.random.fold_in(key_of[20], 71), 0),
        "gains_m": gaussian(key_of[9], (SECTIONS, 2, D), (0.111 * 0.2 / PARAMS ** 0.5), 2.288818359375e-05, ((0, 4),), jnp.float32),
        "gains_v": jnp.clip(jnp.exp(math.log(2.846305968695617e-10) - 1.3843914 * jax.random.uniform(key_of[10], (SECTIONS, 2, D), jnp.float32) ** steps_of(key_of[10], (SECTIONS, 2, D), ((0, 4),), -0.2, 0.2)), 7.129318663201545e-11, 2.846305968695617e-10),
        "final_gain": jnp.clip(1.0 + 0.1 * jax.random.normal(key_of[11], (D,), jnp.float32), 0.5, 1.5),
        "fgain_m": gaussian(key_of[12], (D,), (0.111 * 0.2 / PARAMS ** 0.5), 2.288818359375e-05, ((0, 4),), jnp.float32),
        "fgain_v": jnp.clip(jnp.exp(math.log(2.846305968695617e-10) - 1.3843914 * jax.random.uniform(key_of[13], (D,), jnp.float32) ** steps_of(key_of[13], (D,), ((0, 4),), -0.2, 0.2)), 7.129318663201545e-11, 2.846305968695617e-10),
        "w_in": gaussian(key_of[14], (IN, D), IN ** -0.5, 0.15625, ((0, 4),), jnp.float32),
        "win_m": gaussian(key_of[15], (IN, D), (0.111 * 0.05 / PARAMS ** 0.5), 5.7220458984375e-06, ((0, 4),), jnp.float32),
        "win_v": jnp.clip(jnp.exp(math.log(1.7789412304347607e-11) - 1.3843914 * jax.random.uniform(key_of[16], (IN, D), jnp.float32) ** steps_of(key_of[16], (IN, D), ((0, 4),), -0.2, 0.2)), 4.4558241645009655e-12, 1.7789412304347607e-11),
        "head": gaussian(key_of[17], (D, GENES), D ** -0.5, 0.21875, ((0, 4),), jnp.float32),
        "head_m": gaussian(key_of[18], (D, GENES), (0.111 * 0.05 / PARAMS ** 0.5), 5.7220458984375e-06, ((0, 4),), jnp.float32),
        "head_v": jnp.clip(jnp.exp(math.log(1.7789412304347607e-11) - 1.3843914 * jax.random.uniform(key_of[19], (D, GENES), jnp.float32) ** steps_of(key_of[19], (D, GENES), ((0, 4),), -0.2, 0.2)), 4.4558241645009655e-12, 1.7789412304347607e-11),
    }


EPS_NORM = 1e-05
CLIP = 0.05
BETA_ONE = 0.9
BETA_TWO = 0.95
ADAM_EPS = 1e-08
RATE = 0.06
RATE_GAIN = 1.0
DECAY = 0.1
RATIOS = (1, 2, 4, 8, 16)

@jax.custom_vjp
def low(v):
    return lax.optimization_barrier(v.astype(jnp.bfloat16)).astype(jnp.float32)

@jax.custom_vjp
def low_back(v):
    return v

def low_keep(v):
    return (low(v), None)

def low_pass(kept, grad):
    return (grad,)

def back_keep(v):
    return (v, None)

def back_low(kept, grad):
    return (low(grad),)
low.defvjp(low_keep, low_pass)
low_back.defvjp(back_keep, back_low)

def hdot(left, right):
    return jnp.dot(left, right, precision=lax.Precision.HIGHEST, preferred_element_type=jnp.float32)

def layer_norm(value, gain):
    mean = lax.optimization_barrier(jnp.mean(value, -1, keepdims=True))
    centred = value - mean
    var = lax.optimization_barrier(jnp.mean(centred * centred, -1, keepdims=True))
    return centred * lax.rsqrt(var + EPS_NORM) * gain

def position_table(coord):
    quarter = D // 4
    freq = jnp.exp(-jnp.log(10000.0) * jnp.arange(quarter, dtype=jnp.float32) / quarter)
    along = coord[0].astype(jnp.float32)[:, None] * freq
    across = coord[1].astype(jnp.float32)[:, None] * freq
    return jnp.concatenate([jnp.sin(along), jnp.cos(along), jnp.sin(across), jnp.cos(across)], axis=1)

def score_bias(slide_row):
    place = jnp.arange(MB_TOK, dtype=jnp.int32)
    heads = jnp.arange(HEADS, dtype=jnp.int32)
    mult = jnp.zeros((HEADS, MB_TOK, MB_TOK), jnp.float32)
    for ratio in RATIOS:
        hit = (place[None, :] % ratio == heads[:, None] % ratio).astype(jnp.float32)
        mult = mult + hit[:, :, None] * hit[:, None, :]
    same = slide_row[:, None] == slide_row[None, :]
    return jnp.where(same[None], jnp.log(mult), -1000000000.0)

def layer(x, mat, gain, bias):
    tok = x.shape[0]
    wide = mat[0]
    a_low = low(layer_norm(x, gain[0]))
    qkv = low(low_back(hdot(a_low, wide[:, :3 * D])))
    query = qkv[:, :D].reshape(tok, HEADS, HD)
    keys = qkv[:, D:2 * D].reshape(tok, HEADS, HD)
    vals = qkv[:, 2 * D:].reshape(tok, HEADS, HD)
    scores = jnp.einsum('thd,shd->hts', query, keys, precision=lax.Precision.HIGHEST) * HD ** (-0.5) + bias
    scores = low_back(scores)
    prob = jax.nn.softmax(scores, axis=-1)
    attended = jnp.einsum('hts,shd->thd', low(prob), vals, precision=lax.Precision.HIGHEST).reshape(tok, D)
    attended = low(low_back(attended))
    middle = x + low_back(hdot(attended, wide[:, 3 * D:]))
    b_low = low(layer_norm(middle, gain[1]))
    upper = low_back(hdot(b_low, mat[1]))
    hidden = low(jax.nn.gelu(upper))
    return middle + low_back(hdot(hidden, mat[2].T))

def pack_loss(params, tile, slide_row, coord, known_row, label_row):
    mats_w, gains_w, fgain_w, in_w, head_w = params
    bias = score_bias(slide_row)
    x = low_back(hdot(tile, in_w) + position_table(coord))
    for index in range(SECTIONS):
        x = layer(x, mats_w[index], gains_w[index], bias)
        if index + 1 < SECTIONS:
            x = low(low_back(x))
    member = (slide_row[None, :] == jnp.arange(SLIDES, dtype=jnp.int32)[:, None]).astype(jnp.float32)
    pooled = hdot(member, x) / lax.optimization_barrier(jnp.sum(member, 1, keepdims=True))
    normed = low(layer_norm(pooled, fgain_w))
    logits = low_back(hdot(normed, head_w))
    terms = jnp.logaddexp(0.0, logits) - label_row * logits
    return jnp.sum(known_row * terms)

def adam(weight, grad, first, second, rate, decay):
    first = BETA_ONE * first + (1.0 - BETA_ONE) * grad
    second = BETA_TWO * second + (1.0 - BETA_TWO) * grad * grad
    mhat = first / (1.0 - BETA_ONE ** STEP)
    vhat = second / (1.0 - BETA_TWO ** STEP)
    return (first, second, weight - rate * (mhat / (jnp.sqrt(vhat) + ADAM_EPS) + decay * weight))

def reference(tiles, slide_ids, coords, known, labels, mats, mats_m, mats_v, gains, gains_m, gains_v, final_gain, fgain_m, fgain_v, w_in, win_m, win_v, head, head_m, head_v):
    known_f = known.astype(jnp.float32)
    count = jnp.maximum(jnp.sum(known_f), 1.0)
    items = (tiles.astype(jnp.float32), slide_ids, jnp.moveaxis(coords, 1, 0), known_f, labels.astype(jnp.float32))
    step_fn = jax.checkpoint(pack_loss)

    def objective(params):
        mats_w, gains_w, fgain_w, in_w, head_w = params
        lowered = (low(mats_w), gains_w, fgain_w, low(in_w), low(head_w))

        def one(total, item):
            return (total + step_fn(lowered, *item), None)
        total, _ = lax.scan(one, jnp.zeros((), jnp.float32), items)
        return (total / count, total)
    params = (mats, gains, final_gain, w_in, head)
    loss, pull, loss_sum = jax.vjp(objective, params, has_aux=True)
    grads = pull(jnp.ones((), jnp.float32))[0]
    squares = sum((jnp.sum(g * g) for g in grads))
    grad_norm = jnp.sqrt(squares)
    factor = CLIP / jnp.maximum(grad_norm, CLIP)
    g_mats, g_gains, g_fgain, g_in, g_head = [g * factor for g in grads]
    mats_out = adam(mats, g_mats, mats_m, mats_v, RATE, DECAY)
    gains_out = adam(gains, g_gains, gains_m, gains_v, RATE_GAIN, 0.0)
    fgain_out = adam(final_gain, g_fgain, fgain_m, fgain_v, RATE_GAIN, 0.0)
    in_out = adam(w_in, g_in, win_m, win_v, RATE, DECAY)
    head_out = adam(head, g_head, head_m, head_v, RATE, DECAY)
    return (grad_norm, loss_sum, count, mats_out[0], mats_out[1], mats_out[2], gains_out[0], gains_out[1], gains_out[2], fgain_out[0], fgain_out[1], fgain_out[2], in_out[0], in_out[1], in_out[2], head_out[0], head_out[1], head_out[2])
```

```python
import functools

import jax
import jax.numpy as jnp
from jax import lax
from jax.experimental import pallas as pl
from jax.experimental.pallas import tpu as pltpu
from jax.sharding import PartitionSpec as P

HEADS = 16
STEP = 10


EPS_NORM = 1e-05
CLIP = 0.05
BETA_ONE = 0.9
BETA_TWO = 0.95
ADAM_EPS = 1e-08
RATE = 0.06
RATE_GAIN = 1.0
DECAY = 0.1
RATIOS = (1, 2, 4, 8, 16)

def shifted(block, axis, distance):
    devices = range(lax.axis_size(axis))
    route = [(i - distance, i) for i in devices if i - distance in devices]
    return lax.ppermute(block, axis, route)


def inner(left, right):
    return lax.dot_general(
        left, right, (((0,), (0,)), ((), ())), preferred_element_type=jnp.float32
    )


def position_table(coord, width):
    quarter = width // 4
    freq = jnp.exp(-jnp.log(10000.0) * jnp.arange(quarter, dtype=jnp.float32) / quarter)
    along = coord[0].astype(jnp.float32)[:, None] * freq
    across = coord[1].astype(jnp.float32)[:, None] * freq
    return jnp.concatenate(
        [jnp.sin(along), jnp.cos(along), jnp.sin(across), jnp.cos(across)], axis=1
    )


def log_mult(heads, tok):
    place = jnp.arange(tok, dtype=jnp.int32)
    head_idx = jnp.arange(heads, dtype=jnp.int32)
    mult = jnp.zeros((heads, tok, tok), jnp.float32)
    for ratio in RATIOS:
        hit = (place[None, :] % ratio == head_idx[:, None] % ratio).astype(jnp.float32)
        mult = mult + hit[:, :, None] * hit[:, None, :]
    return jnp.log(mult)


NN = (((1,), (0,)), ((), ()))
NT = (((1,), (1,)), ((), ()))
TN = (((0,), (0,)), ((), ()))
LANES = 128
BF = jnp.bfloat16
F32 = jnp.float32


def mm(left, right, dims=NN):
    return lax.dot_general(left, right, dims, preferred_element_type=F32)


def norm_parts(value):
    mean = jnp.mean(value, -1, keepdims=True)
    centred = value - mean
    var = jnp.mean(centred * centred, -1, keepdims=True)
    inv = lax.rsqrt(var + EPS_NORM)
    return centred * inv, inv


def norm_back(dvalue, gain, hat, inv):
    dhat = dvalue * gain
    return inv * (
        dhat
        - jnp.mean(dhat, -1, keepdims=True)
        - hat * jnp.mean(dhat * hat, -1, keepdims=True)
    )


def window(head, size):
    low = head * size // LANES * LANES
    high = -(-(head + 1) * size // LANES) * LANES
    return low, high


def placed_rows(ref, head, size):
    low, high = window(head, size)
    before, after = head * size - low, high - (head + 1) * size
    tok = ref.shape[1]
    parts = [ref[head * size : (head + 1) * size, :]]
    if before:
        parts = [jnp.zeros((before, tok), ref.dtype)] + parts
    if after:
        parts = parts + [jnp.zeros((after, tok), ref.dtype)]
    return jnp.concatenate(parts, axis=0) if len(parts) > 1 else parts[0]


def same_slide(ids_ref, pick):
    tok = ids_ref.shape[1]
    row = jnp.broadcast_to(ids_ref[pl.ds(pick, 1), :].astype(F32), (tok, tok))
    return row, row.T


def forward_kernel(
    heads, slides, scal, ids, gain, fgain, head_w, known, label, count,
    x0_h, rc_h, lm_h, wa_h, w1_h, w2_h, *rest
):
    fresh = rest[0]
    n_buf = 13
    rest = rest[1:] if fresh else rest[1 + n_buf :]
    send_h = rest[0]
    (x_b, qkv_b, lse_b, att_b, mid_b, gp_b, hid_b, a_b, b_b, dl_b, nl_b, dlog_b, side_b) = rest[1 : 1 + n_buf]
    (x_v, lm_v, wa, w1, w2, qkv_v, lse_v, att_v, mid_v, gp_v, hid_v, a_v, b_v, o_v, send_v,
     q_t, v_t, o_t, pool_v, nl_v, dlog_v, side_v, sin, sout) = rest[1 + n_buf :]
    valid, pick, first, last = scal[0], scal[1], scal[2], scal[3]
    tok, width = x_v.shape
    size = width // heads
    scale = size ** (-0.5)

    @pl.when(valid == 1)
    def _():
        weights = [
            pltpu.make_async_copy(wa_h.at[:, : 3 * width], wa.at[:, : 3 * width], sin.at[1]),
            pltpu.make_async_copy(lm_h, lm_v, sin.at[2]),
            pltpu.make_async_copy(wa_h.at[:, 3 * width :], wa.at[:, 3 * width :], sin.at[3]),
            pltpu.make_async_copy(w1_h, w1, sin.at[4]),
            pltpu.make_async_copy(w2_h, w2, sin.at[5]),
        ]
        from_table = pltpu.make_async_copy(x0_h.at[pick], x_v, sin.at[0])
        from_wire = pltpu.make_async_copy(rc_h, x_v, sin.at[0])

        @pl.when(first == 1)
        def _():
            from_table.start()

        @pl.when(first != 1)
        def _():
            from_wire.start()

        for c in weights:
            c.start()
        outs = []

        def emit(src, dst):
            c = pltpu.make_async_copy(src, dst, sout.at[len(outs)])
            c.start()
            outs.append(c)

        row, col = same_slide(ids, pick)
        same = row == col

        @pl.when(first == 1)
        def _():
            from_table.wait()

        @pl.when(first != 1)
        def _():
            from_wire.wait()

        emit(x_v, x_b.at[pick])
        x = x_v[...].astype(F32)
        hat, _ = norm_parts(x)
        a_v[...] = (hat * gain[0:1, :]).astype(BF)
        emit(a_v, a_b.at[pick])
        weights[0].wait()
        qkv_v[...] = mm(a_v[...], wa[:, : 3 * width]).astype(BF)
        emit(qkv_v, qkv_b.at[pick])
        q_t[...] = qkv_v[:, :width].T
        v_t[...] = qkv_v[:, 2 * width :].T
        weights[1].wait()
        for h in range(heads):
            low, high = window(h, size)
            s = mm(qkv_v[:, width + low : width + high], placed_rows(q_t, h, size)) * scale
            s = s + jnp.where(same, lm_v[h], -1000000000.0)
            top = jnp.max(s, 0, keepdims=True)
            e = jnp.exp(s - top)
            total = jnp.sum(e, 0, keepdims=True)
            lse_v[h : h + 1, :] = top + jnp.log(total)
            o = mm(v_t[h * size : (h + 1) * size, :], e.astype(BF))
            o_t[h * size : (h + 1) * size, :] = o * (1.0 / total)
        att_v[...] = o_t[...].T.astype(BF)
        emit(lse_v, lse_b.at[pick])
        emit(att_v, att_b.at[pick])
        weights[2].wait()
        middle = x + mm(att_v[...], wa[:, 3 * width :])
        mid_v[...] = middle
        emit(mid_v, mid_b.at[pick])
        hat, _ = norm_parts(middle)
        b_v[...] = (hat * gain[1:2, :]).astype(BF)
        emit(b_v, b_b.at[pick])
        weights[3].wait()
        ff = w1.shape[1]
        part = ff // 4
        for j in range(4):
            cols = slice(j * part, (j + 1) * part)
            up = mm(b_v[...], w1[:, cols])
            square = up * up
            sig = 1.0 / (1.0 + jnp.exp(up * (-1.5957691216057308 - 0.07135481627159852 * square)))
            act = up * sig
            hid_v[:, cols] = act.astype(BF)
            slope = 1.5957691216057308 + 0.21406444881478 * square
            gp_v[:, cols] = sig + act * (1.0 - sig) * slope
        emit(gp_v, gp_b.at[pick])
        emit(hid_v, hid_b.at[pick])
        weights[4].wait()
        out = mid_v[...] + mm(hid_v[...], w2[...], NT)
        send_v[...] = out.astype(BF)
        emit(send_v, send_h)

        @pl.when(last == 1)
        def _():
            o_v[...] = out
            pool_v[...] = jnp.zeros_like(pool_v)
            inverse = []
            for s in range(slides):
                inside = (col == float(s)).astype(F32)
                inverse.append(1.0 / jnp.sum(inside, 0, keepdims=True))
                parts = []
                for j in range(width // LANES):
                    parts.append(
                        jnp.sum(o_v[:, j * LANES : (j + 1) * LANES] * inside, 0, keepdims=True) * inverse[s]
                    )
                pool_v[s : s + 1, :] = jnp.concatenate(parts, axis=1)
            hat, inv = norm_parts(pool_v[...])
            low_n = (hat * fgain[...]).astype(BF)
            nl_v[...] = low_n
            logits = mm(low_n, head_w[...])
            kn = known[pick]
            lb = label[pick]
            tail = jnp.exp(-jnp.abs(logits))
            soft = jnp.maximum(logits, 0.0) + jnp.log(1.0 + tail)
            terms = kn * (soft - lb * logits)
            gate = jnp.where(logits >= 0.0, 1.0, tail) / (1.0 + tail)
            dlog = (kn * (gate - lb) / count[0, 0]).astype(BF)
            dlog_v[...] = dlog
            d_n = mm(dlog, head_w[...], NT)
            side_v[...] = jnp.zeros_like(side_v)
            side_v[0:1, :] = jnp.sum(d_n * hat, 0, keepdims=True)
            side_v[1:2, 0:LANES] = jnp.sum(terms, 0, keepdims=True)
            d_pool = norm_back(d_n, fgain[...], hat, inv)
            pool_v[...] = d_pool
            for j in range(width // LANES):
                lanes = slice(j * LANES, (j + 1) * LANES)
                acc = jnp.zeros((tok, LANES), F32)
                for s in range(slides):
                    acc = acc + jnp.where(col == float(s), pool_v[s : s + 1, lanes] * inverse[s], 0.0)
                o_v[:, lanes] = acc
            tails = [
                pltpu.make_async_copy(o_v, dl_b.at[pick], sin.at[0]),
                pltpu.make_async_copy(nl_v, nl_b.at[pick], sin.at[1]),
                pltpu.make_async_copy(dlog_v, dlog_b.at[pick], sin.at[2]),
                pltpu.make_async_copy(side_v, side_b.at[pick], sin.at[3]),
            ]
            for c in tails:
                c.start()
            for c in tails:
                c.wait()

        for c in outs:
            c.wait()


def backward_kernel(
    heads, scal, ids, gain, rc_h, dl_b, lm_h, wa_h, w1_h, w2_h,
    x_b, qkv_b, lse_b, mid_b, gp_b, *rest
):
    fresh = rest[0]
    n_buf = 5
    rest = rest[1:] if fresh else rest[1 + n_buf :]
    send_h = rest[0]
    (dbr_b, dup_b, dat_b, dqkv_b, gg_b) = rest[1 : 1 + n_buf]
    (rc_v, dl_v, lm_v, wa, w1, w2, x_v, qkv_v, lse_v, mid_v, gp_v,
     dbr_v, dup_v, dat_v, dqkv_v, gg_v, send_v, dm_v, q_t, k_t, do_v, do_t, dq_t, p_v, ds_v, sin, sout) = rest[1 + n_buf :]
    valid, pick, last = scal[0], scal[1], scal[3]
    tok, width = x_v.shape
    size = width // heads
    scale = size ** (-0.5)
    per = 8

    @pl.when(valid == 1)
    def _():
        from_wire = pltpu.make_async_copy(rc_h, rc_v, sin.at[0])
        from_head = pltpu.make_async_copy(dl_b.at[pick], dl_v, sin.at[0])

        @pl.when(last == 1)
        def _():
            from_head.start()

        @pl.when(last != 1)
        def _():
            from_wire.start()

        loads = [
            pltpu.make_async_copy(w2_h, w2, sin.at[1]),
            pltpu.make_async_copy(gp_b.at[pick], gp_v, sin.at[2]),
            pltpu.make_async_copy(w1_h, w1, sin.at[3]),
            pltpu.make_async_copy(mid_b.at[pick], mid_v, sin.at[4]),
            pltpu.make_async_copy(qkv_b.at[pick], qkv_v, sin.at[5]),
            pltpu.make_async_copy(wa_h.at[:, 3 * width :], wa.at[:, 3 * width :], sin.at[6]),
            pltpu.make_async_copy(lse_b.at[pick], lse_v, sin.at[7]),
            pltpu.make_async_copy(lm_h, lm_v, sin.at[8]),
            pltpu.make_async_copy(wa_h.at[:, : 3 * width], wa.at[:, : 3 * width], sin.at[9]),
            pltpu.make_async_copy(x_b.at[pick], x_v, sin.at[10]),
        ]
        for c in loads:
            c.start()
        outs = []

        def emit(src, dst):
            c = pltpu.make_async_copy(src, dst, sout.at[len(outs)])
            c.start()
            outs.append(c)

        row, col = same_slide(ids, pick)
        same = row == col

        @pl.when(last == 1)
        def _():
            from_head.wait()

        @pl.when(last != 1)
        def _():
            from_wire.wait()
            dl_v[...] = rc_v[...].astype(F32)

        dbr_v[...] = dl_v[...].astype(BF)
        emit(dbr_v, dbr_b.at[pick])
        loads[0].wait()
        loads[1].wait()
        ff = w1.shape[1]
        part = ff // 4
        for j in range(4):
            cols = slice(j * part, (j + 1) * part)
            dup_v[:, cols] = (mm(dbr_v[...], w2[:, cols]) * gp_v[:, cols]).astype(BF)
        emit(dup_v, dup_b.at[pick])
        loads[2].wait()
        d_b = mm(dup_v[...], w1[...], NT)
        loads[3].wait()
        hat, inv = norm_parts(mid_v[...])
        gg_v[1:2, :] = jnp.sum(d_b * hat, 0, keepdims=True)
        d_mid = dl_v[...] + norm_back(d_b, gain[1:2, :], hat, inv)
        dm_v[...] = d_mid
        dat_v[...] = d_mid.astype(BF)
        emit(dat_v, dat_b.at[pick])
        loads[4].wait()
        q_t[...] = qkv_v[:, :width].T
        k_t[...] = qkv_v[:, width : 2 * width].T
        loads[5].wait()
        do_v[...] = mm(dat_v[...], wa[:, 3 * width :], NT).astype(BF)
        do_t[...] = do_v[...].T
        loads[6].wait()
        loads[7].wait()
        lane = lax.broadcasted_iota(jnp.int32, (tok, LANES), 1)
        for group in range(heads // per):
            for i in range(per):
                h = group * per + i
                low, high = window(h, size)
                s = mm(qkv_v[:, width + low : width + high], placed_rows(q_t, h, size)) * scale
                s = s + jnp.where(same, lm_v[h], -1000000000.0)
                p = jnp.exp(s - lse_v[h : h + 1, :])
                dp = mm(qkv_v[:, 2 * width + low : 2 * width + high], placed_rows(do_t, h, size))
                inner_sum = jnp.sum(dp * p, 0, keepdims=True)
                ds = (p * (dp - inner_sum)).astype(BF)
                p_v[:, i * tok : (i + 1) * tok] = p.astype(BF)
                ds_v[:, i * tok : (i + 1) * tok] = ds
                dq_t[h * size : (h + 1) * size, :] = mm(k_t[h * size : (h + 1) * size, :], ds) * scale
            base = group * per * size
            for block in range(base // LANES, (base + per * size) // LANES):
                left = block * LANES
                inside = [
                    i for i in range(per)
                    if (group * per + i) * size < left + LANES and (group * per + i + 1) * size > left
                ]
                spans = slice(inside[0] * tok, (inside[-1] + 1) * tok)
                q_parts, o_parts = [], []
                for i in inside:
                    start = (group * per + i) * size - left
                    keep = (lane >= start) & (lane < start + size)
                    q_parts.append(jnp.where(keep, qkv_v[:, left : left + LANES], jnp.zeros((), BF)))
                    o_parts.append(jnp.where(keep, do_v[:, left : left + LANES], jnp.zeros((), BF)))
                dk = mm(ds_v[:, spans], jnp.concatenate(q_parts, axis=0)) * scale
                dv = mm(p_v[:, spans], jnp.concatenate(o_parts, axis=0))
                dqkv_v[:, width + left : width + left + LANES] = dk.astype(BF)
                dqkv_v[:, 2 * width + left : 2 * width + left + LANES] = dv.astype(BF)
        dqkv_v[:, :width] = dq_t[...].T.astype(BF)
        emit(dqkv_v, dqkv_b.at[pick])
        loads[8].wait()
        d_a = mm(dqkv_v[...], wa[:, : 3 * width], NT)
        loads[9].wait()
        hat, inv = norm_parts(x_v[...].astype(F32))
        gg_v[0:1, :] = jnp.sum(d_a * hat, 0, keepdims=True)
        emit(gg_v, gg_b.at[pick])
        send_v[...] = (dm_v[...] + norm_back(d_a, gain[0:1, :], hat, inv)).astype(BF)
        emit(send_v, send_h)
        for c in outs:
            c.wait()


def spec_any():
    return pl.BlockSpec(memory_space=pl.ANY)


def spec_vmem():
    return pl.BlockSpec(memory_space=pltpu.VMEM)


def forward_call(heads, slides, scal, ids, gain, fgain, head_w, known, label, count, x0, received, lm, wa, w1, w2, bufs):
    micro, tok, width = x0.shape
    ff = w1.shape[1]
    rows = known.shape[1]
    shapes = [
        ((tok, width), BF), ((tok, 3 * width), BF), ((heads, tok), F32), ((tok, width), BF),
        ((tok, width), F32), ((tok, ff), F32), ((tok, ff), BF), ((tok, width), BF), ((tok, width), BF),
        ((tok, width), F32), ((rows, width), BF), ((rows, LANES), BF), ((8, width), F32),
    ]
    fresh = bufs is None
    given = [] if fresh else list(bufs)
    vm = lambda index: pltpu.VMEM(*shapes[index])
    n_in = 14
    out = pl.pallas_call(
        functools.partial(forward_body, heads, slides, fresh),
        out_shape=[jax.ShapeDtypeStruct((tok, width), BF)]
        + [jax.ShapeDtypeStruct((micro,) + s, d) for s, d in shapes],
        in_specs=[pl.BlockSpec(memory_space=pltpu.SMEM)]
        + [spec_vmem()] * 6
        + [pl.BlockSpec(memory_space=pltpu.SMEM)]
        + [spec_any()] * (6 + len(given)),
        out_specs=[spec_any()] * (1 + len(shapes)),
        input_output_aliases={n_in + i: 1 + i for i in range(len(given))},
        scratch_shapes=[
            vm(0), pltpu.VMEM(lm.shape, F32), pltpu.VMEM(wa.shape, BF), pltpu.VMEM(w1.shape, BF),
            pltpu.VMEM(w2.shape, BF), vm(1), vm(2), vm(3), vm(4), vm(5), vm(6), vm(7), vm(8),
            pltpu.VMEM((tok, width), F32), vm(0),
            pltpu.VMEM((width, tok), BF), pltpu.VMEM((width, tok), BF), pltpu.VMEM((width, tok), F32),
            pltpu.VMEM((rows, width), F32), vm(10), vm(11), vm(12),
            pltpu.SemaphoreType.DMA((6,)), pltpu.SemaphoreType.DMA((10,)),
        ],
        compiler_params=pltpu.CompilerParams(vmem_limit_bytes=48 << 20),
        name="layer_forward",
    )(scal, ids, gain, fgain, head_w, known, label, count, x0, received, lm, wa, w1, w2, *given)
    return out[0], out[1:]


def backward_call(heads, scal, ids, gain, received, records, lm, wa, w1, w2, bufs):
    x_b, qkv_b, lse_b, mid_b, gp_b, dl_b = records
    micro, tok, width = x_b.shape
    ff = w1.shape[1]
    shapes = [((tok, width), BF), ((tok, ff), BF), ((tok, width), BF), ((tok, 3 * width), BF), ((8, width), F32)]
    fresh = bufs is None
    given = [] if fresh else list(bufs)
    n_in = 14
    out = pl.pallas_call(
        functools.partial(backward_body, heads, fresh),
        out_shape=[jax.ShapeDtypeStruct((tok, width), BF)]
        + [jax.ShapeDtypeStruct((micro,) + s, d) for s, d in shapes],
        in_specs=[pl.BlockSpec(memory_space=pltpu.SMEM)] + [spec_vmem()] * 2 + [spec_any()] * (11 + len(given)),
        out_specs=[spec_any()] * (1 + len(shapes)),
        input_output_aliases={n_in + i: 1 + i for i in range(len(given))},
        scratch_shapes=[
            pltpu.VMEM((tok, width), BF), pltpu.VMEM((tok, width), F32), pltpu.VMEM(lm.shape, F32),
            pltpu.VMEM(wa.shape, BF), pltpu.VMEM(w1.shape, BF), pltpu.VMEM(w2.shape, BF),
            pltpu.VMEM((tok, width), BF), pltpu.VMEM((tok, 3 * width), BF), pltpu.VMEM((heads, tok), F32),
            pltpu.VMEM((tok, width), F32), pltpu.VMEM((tok, ff), F32),
        ]
        + [pltpu.VMEM(s, d) for s, d in shapes]
        + [
            pltpu.VMEM((tok, width), BF), pltpu.VMEM((tok, width), F32),
            pltpu.VMEM((width, tok), BF), pltpu.VMEM((width, tok), BF),
            pltpu.VMEM((tok, width), BF), pltpu.VMEM((width, tok), BF), pltpu.VMEM((width, tok), F32),
            pltpu.VMEM((tok, 8 * tok), BF), pltpu.VMEM((tok, 8 * tok), BF),
            pltpu.SemaphoreType.DMA((11,)), pltpu.SemaphoreType.DMA((6,)),
        ],
        compiler_params=pltpu.CompilerParams(vmem_limit_bytes=48 << 20),
        name="layer_backward",
    )(scal, ids, gain, received, dl_b, lm, wa, w1, w2, x_b, qkv_b, lse_b, mid_b, gp_b, *given)
    return out[0], out[1:]


def forward_body(heads, slides, fresh, *refs):
    forward_kernel(heads, slides, *refs[:14], fresh, *refs[14:])


def backward_body(heads, fresh, *refs):
    backward_kernel(heads, *refs[:14], fresh, *refs[14:])


def adam(weight, grad, first, second, rate, decay):
    first = BETA_ONE * first + (1.0 - BETA_ONE) * grad
    second = BETA_TWO * second + (1.0 - BETA_TWO) * grad * grad
    mhat = first / (1.0 - BETA_ONE**STEP)
    vhat = second / (1.0 - BETA_TWO**STEP)
    return (first, second, weight - rate * (mhat / (jnp.sqrt(vhat) + ADAM_EPS) + decay * weight))


def per_device(
    tiles,
    slide_ids,
    coords,
    known,
    labels,
    mats,
    mats_m,
    mats_v,
    gains,
    gains_m,
    gains_v,
    final_gain,
    fgain_m,
    fgain_v,
    w_in,
    win_m,
    win_v,
    head,
    head_m,
    head_v,
):
    sections = lax.axis_size("section")
    section = lax.axis_index("section")
    first_dp = (lax.axis_index("dp") == 0).astype(jnp.float32)
    micro, tok = slide_ids.shape
    heads = HEADS
    slides, genes = known.shape[1:]
    wide = lax.all_gather(mats[0].astype(BF), "dp", axis=1, tiled=True)
    in_low = lax.all_gather(w_in.astype(BF), "section", axis=0, tiled=True)
    head_low = lax.all_gather(head.astype(BF), "section", axis=0, tiled=True)
    full_fgain = lax.all_gather(final_gain, "section", axis=0, tiled=True)
    gain = gains[0]
    width = wide.shape[1]
    known_f = known.astype(jnp.float32)
    labels_f = labels.astype(jnp.float32)
    count = jnp.maximum(lax.psum(jnp.sum(known_f), "dp"), 1.0)
    ticks = micro + sections - 1
    wa, w1, w2 = wide[0], wide[1], wide[2]
    lm = log_mult(heads, tok)
    pad = ((0, 0), (0, 16 - slides), (0, LANES - genes))
    known_p = jnp.pad(known_f, pad)
    labels_p = jnp.pad(labels_f, pad)
    head_p = jnp.pad(head_low, ((0, 0), (0, LANES - genes)))
    table = jax.vmap(lambda c: position_table(c, width), in_axes=1)(coords)
    x0 = (
        jnp.dot(tiles.reshape(micro * tok, -1), in_low, preferred_element_type=F32).reshape(
            micro, tok, width
        )
        + table
    ).astype(BF)

    def scalars(index):
        valid = (index >= 0) & (index < micro)
        return jnp.stack(
            [valid, jnp.clip(index, 0, micro - 1), section == 0, section == sections - 1]
        ).astype(jnp.int32)

    received = jnp.zeros((tok, width), BF)
    bufs = None
    for tick in range(ticks):
        send, bufs = forward_call(
            heads, slides, scalars(tick - section), slide_ids, gain, full_fgain[None, :], head_p,
            known_p, labels_p, count.reshape(1, 1), x0, received, lm, wa, w1, w2, bufs,
        )
        if tick + 1 < ticks:
            received = shifted(send, "section", 1)
    (x_b, qkv_b, lse_b, att_b, mid_b, gp_b, hid_b, a_b, b_b, dl_b, nl_b, dlog_b, side_b) = bufs
    records = (x_b, qkv_b, lse_b, mid_b, gp_b, dl_b)
    incoming = jnp.zeros((tok, width), BF)
    bufs = None
    sends = []
    for tick in range(ticks):
        send, bufs = backward_call(
            heads, scalars(tick - (sections - 1 - section)), slide_ids, gain, incoming, records,
            lm, wa, w1, w2, bufs,
        )
        sends.append(send)
        if tick + 1 < ticks:
            incoming = shifted(send, "section", -1)
    dbr_b, dup_b, dat_b, dqkv_b, gg_b = bufs
    flat = lambda v: v.reshape((-1, v.shape[-1]))
    grad_down = inner(flat(dbr_b), flat(hid_b)).astype(BF)
    grad_up = inner(flat(b_b), flat(dup_b)).astype(BF)
    grad_attn = jnp.concatenate(
        [inner(flat(a_b), flat(dqkv_b)).astype(BF), inner(flat(att_b), flat(dat_b)).astype(BF)], axis=1
    )
    grad_wide = jnp.stack([grad_attn, grad_up, grad_down])
    grad_gain = jnp.sum(gg_b, 0)[:2]
    on_first = section == 0
    on_last = section == sections - 1
    d_first = jnp.stack(sends[sections - 1 :])
    grad_in = inner(flat(tiles), flat(d_first))
    grad_in = jnp.where(on_first, grad_in, 0.0).astype(BF)
    grad_head = jnp.where(on_last, inner(flat(nl_b), flat(dlog_b)), 0.0)[:, :genes]
    side = jnp.where(on_last, jnp.sum(side_b, 0), 0.0)
    grad_fgain = side[0]
    loss_local = jnp.sum(side[1, :LANES])
    shard_wide = lax.psum_scatter(grad_wide, "dp", scatter_dimension=1, tiled=True).astype(F32)[None]
    part_in = lax.psum(
        lax.psum_scatter(grad_in, "section", scatter_dimension=0, tiled=True).astype(F32), "dp"
    )
    sum_gain, sum_head, sum_fgain = lax.psum((grad_gain, grad_head, grad_fgain), "dp")
    part_head, part_fgain = (
        lax.psum_scatter(sum_head, "section", scatter_dimension=0, tiled=True),
        lax.psum_scatter(sum_fgain, "section", scatter_dimension=0, tiled=True),
    )
    squares = jnp.sum(shard_wide * shard_wide) + first_dp * (
        jnp.sum(sum_gain * sum_gain)
        + jnp.sum(part_in * part_in)
        + jnp.sum(part_head * part_head)
        + jnp.sum(part_fgain * part_fgain)
    )
    total_sq, loss_sum = lax.psum((squares, loss_local), ("dp", "section"))
    grad_norm = jnp.sqrt(total_sq)
    factor = CLIP / jnp.maximum(grad_norm, CLIP)
    mats_out = adam(mats, shard_wide * factor, mats_m, mats_v, RATE, DECAY)
    gains_out = adam(gains, sum_gain[None] * factor, gains_m, gains_v, RATE_GAIN, 0.0)
    fgain_out = adam(final_gain, part_fgain * factor, fgain_m, fgain_v, RATE_GAIN, 0.0)
    in_out = adam(w_in, part_in * factor, win_m, win_v, RATE, DECAY)
    head_out = adam(head, part_head * factor, head_m, head_v, RATE, DECAY)
    return (
        grad_norm,
        loss_sum,
        count,
        mats_out[0],
        mats_out[1],
        mats_out[2],
        gains_out[0],
        gains_out[1],
        gains_out[2],
        fgain_out[0],
        fgain_out[1],
        fgain_out[2],
        in_out[0],
        in_out[1],
        in_out[2],
        head_out[0],
        head_out[1],
        head_out[2],
    )


def solution(mesh):
    placed = (
        P("dp", None, None),
        P("dp", None),
        P(None, "dp", None),
        P("dp", None, None),
        P("dp", None, None),
        P("section", None, "dp", None),
        P("section", None, "dp", None),
        P("section", None, "dp", None),
        P("section", None, None),
        P("section", None, None),
        P("section", None, None),
        P("section"),
        P("section"),
        P("section"),
        P("section", None),
        P("section", None),
        P("section", None),
        P("section", None),
        P("section", None),
        P("section", None),
    )
    return jax.shard_map(
        per_device,
        mesh=mesh,
        in_specs=placed,
        out_specs=(
            P(),
            P(),
            P(),
            P("section", None, "dp", None),
            P("section", None, "dp", None),
            P("section", None, "dp", None),
            P("section", None, None),
            P("section", None, None),
            P("section", None, None),
            P("section"),
            P("section"),
            P("section"),
            P("section", None),
            P("section", None),
            P("section", None),
            P("section", None),
            P("section", None),
            P("section", None),
        ),
        check_vma=False,
    )
```

```python
import functools

import jax
import jax.numpy as jnp
from jax import lax
from jax.experimental import pallas as pl
from jax.experimental.pallas import tpu as pltpu
from jax.sharding import PartitionSpec as P

HEADS = 16
STEP = 10


EPS_NORM = 1e-05
CLIP = 0.05
BETA_ONE = 0.9
BETA_TWO = 0.95
ADAM_EPS = 1e-08
RATE = 0.06
RATE_GAIN = 1.0
DECAY = 0.1
RATIOS = (1, 2, 4, 8, 16)

def moved(block, route):
    dp, sections = lax.axis_size("dp"), lax.axis_size("section")
    pairs = []
    for d in range(dp):
        for s in range(sections):
            target = route(d, s)
            if target is not None:
                pairs.append((d * sections + s, target[0] * sections + target[1]))
    return lax.ppermute(block, ("dp", "section"), pairs)


def flip_dp(bit):
    return lambda d, s: (d ^ bit, s)


def flip_section(bit):
    return lambda d, s: (d, s ^ bit)


def spread_sum(value):
    dp, sections = lax.axis_size("dp"), lax.axis_size("section")
    flips = [(0, 1 << k) for k in range(sections.bit_length() - 1)]
    flips += [(1 << k, 0) for k in range(dp.bit_length() - 1)]
    if len(flips) % 2:
        d, s = flips.pop(0)
        value = value + moved(value, lambda i, j: (i ^ d, j ^ s))
    while flips:
        (d0, s0), (d1, s1) = flips.pop(0), flips.pop(0)
        first = moved(value, lambda i, j: (i ^ d0, j ^ s0))
        second = moved(value, lambda i, j: (i ^ d1, j ^ s1))
        third = moved(value, lambda i, j: (i ^ d0 ^ d1, j ^ s0 ^ s1))
        value = (value + first) + (second + third)
    return value


def dp_sum(value):
    dp = lax.axis_size("dp")
    bit = 1
    while bit < dp:
        value = value + moved(value, flip_dp(bit))
        bit *= 2
    return value


def inner(left, right):
    return lax.dot_general(
        left, right, (((0,), (0,)), ((), ())), preferred_element_type=jnp.float32
    )


def position_table(coord, width):
    quarter = width // 4
    freq = jnp.exp(-jnp.log(10000.0) * jnp.arange(quarter, dtype=jnp.float32) / quarter)
    along = coord[0].astype(jnp.float32)[:, None] * freq
    across = coord[1].astype(jnp.float32)[:, None] * freq
    return jnp.concatenate(
        [jnp.sin(along), jnp.cos(along), jnp.sin(across), jnp.cos(across)], axis=1
    )


def log_mult(heads, tok):
    place = jnp.arange(tok, dtype=jnp.int32)
    head_idx = jnp.arange(heads, dtype=jnp.int32)
    mult = jnp.zeros((heads, tok, tok), jnp.float32)
    for ratio in RATIOS:
        hit = (place[None, :] % ratio == head_idx[:, None] % ratio).astype(jnp.float32)
        mult = mult + hit[:, :, None] * hit[:, None, :]
    return jnp.log(mult)


NN = (((1,), (0,)), ((), ()))
NT = (((1,), (1,)), ((), ()))
TN = (((0,), (0,)), ((), ()))
LANES = 128
BF = jnp.bfloat16
F32 = jnp.float32


def mm(left, right, dims=NN):
    return lax.dot_general(left, right, dims, preferred_element_type=F32)


def norm_parts(value):
    mean = jnp.mean(value, -1, keepdims=True)
    centred = value - mean
    var = jnp.mean(centred * centred, -1, keepdims=True)
    inv = lax.rsqrt(var + EPS_NORM)
    return centred * inv, inv


def norm_back(dvalue, gain, hat, inv):
    dhat = dvalue * gain
    return inv * (
        dhat
        - jnp.mean(dhat, -1, keepdims=True)
        - hat * jnp.mean(dhat * hat, -1, keepdims=True)
    )


def window(head, size):
    low = head * size // LANES * LANES
    high = -(-(head + 1) * size // LANES) * LANES
    return low, high


def placed_rows(ref, head, size):
    low, high = window(head, size)
    before, after = head * size - low, high - (head + 1) * size
    tok = ref.shape[1]
    parts = [ref[head * size : (head + 1) * size, :]]
    if before:
        parts = [jnp.zeros((before, tok), ref.dtype)] + parts
    if after:
        parts = parts + [jnp.zeros((after, tok), ref.dtype)]
    return jnp.concatenate(parts, axis=0) if len(parts) > 1 else parts[0]


def same_slide(ids_ref, pick):
    tok = ids_ref.shape[1]
    row = jnp.broadcast_to(ids_ref[pl.ds(pick, 1), :].astype(F32), (tok, tok))
    return row, row.T


def forward_kernel(
    heads, slides, shrink, scal, ids, gain, fgain, head_w, known, label,
    x0, rc, lm_v, wqkv, wo, w1, w2t, wqkv_t, wo_t, w1_t, w2, *rest
):
    fresh = rest[0]
    n_buf = 13
    rest = rest[1:] if fresh else rest[1 + n_buf :]
    send_h = rest[0]
    (x_b, qkv_b, lse_b, att_b, mid_b, gp_b, hid_b, a_b, b_b, dl_b, nl_b, dlog_b, side_b) = rest[1 : 1 + n_buf]
    (x_v, qkv_v, lse_v, att_v, mid_v, gp_v, hid_v, a_v, b_v, o_v,
     q_t, v_t, o_t, pool_v, nl_v, dlog_v, side_v, sin, sout) = rest[1 + n_buf :]
    valid, pick, first, last = scal[0], scal[1], scal[2], scal[3]
    tok, width = x_v.shape
    size = width // heads
    scale = size ** (-0.5)

    @pl.when(valid == 1)
    def _():
        @pl.when(first == 1)
        def _():
            x_v[...] = x0[pick]

        @pl.when(first != 1)
        def _():
            x_v[...] = rc[...]

        outs = []

        def emit(src, dst):
            c = pltpu.make_async_copy(src, dst, sout.at[len(outs)])
            c.start()
            outs.append(c)

        row, col = same_slide(ids, pick)
        same = row == col

        emit(x_v, x_b.at[pick])
        x = x_v[...].astype(F32)
        hat, _ = norm_parts(x)
        a_v[...] = (hat * gain[0:1, :]).astype(BF)
        emit(a_v, a_b.at[pick])
        qkv_v[...] = mm(a_v[...], wqkv[...]).astype(BF)
        emit(qkv_v, qkv_b.at[pick])
        q_t[...] = qkv_v[:, :width].T
        v_t[...] = qkv_v[:, 2 * width :].T
        for h in range(heads):
            low, high = window(h, size)
            s = mm(qkv_v[:, width + low : width + high], placed_rows(q_t, h, size)) * scale
            s = s + jnp.where(same, lm_v[h], -1000000000.0)
            top = jnp.max(s, 0, keepdims=True)
            e = jnp.exp(s - top)
            total = jnp.sum(e, 0, keepdims=True)
            lse_v[h : h + 1, :] = top + jnp.log(total)
            o = mm(v_t[h * size : (h + 1) * size, :], e.astype(BF))
            o_t[h * size : (h + 1) * size, :] = o * (1.0 / total)
        att_v[...] = o_t[...].T.astype(BF)
        emit(lse_v, lse_b.at[pick])
        emit(att_v, att_b.at[pick])
        middle = x + mm(att_v[...], wo[...])
        mid_v[...] = middle
        emit(mid_v, mid_b.at[pick])
        hat, _ = norm_parts(middle)
        b_v[...] = (hat * gain[1:2, :]).astype(BF)
        emit(b_v, b_b.at[pick])
        ff = w1.shape[1]
        part = ff // 4
        for j in range(4):
            cols = slice(j * part, (j + 1) * part)
            up = mm(b_v[...], w1[:, cols])
            square = up * up
            sig = 1.0 / (1.0 + jnp.exp(up * (-1.5957691216057308 - 0.07135481627159852 * square)))
            act = up * sig
            hid_v[:, cols] = act.astype(BF)
            slope = 1.5957691216057308 + 0.21406444881478 * square
            gp_v[:, cols] = sig + act * (1.0 - sig) * slope
        emit(gp_v, gp_b.at[pick])
        emit(hid_v, hid_b.at[pick])
        out = mid_v[...] + mm(hid_v[...], w2t[...])
        send_h[...] = out.astype(BF)

        @pl.when(last == 1)
        def _():
            o_v[...] = out
            pool_v[...] = jnp.zeros_like(pool_v)
            inverse = []
            for s in range(slides):
                inside = (col == float(s)).astype(F32)
                inverse.append(1.0 / jnp.sum(inside, 0, keepdims=True))
                parts = []
                for j in range(width // LANES):
                    parts.append(
                        jnp.sum(o_v[:, j * LANES : (j + 1) * LANES] * inside, 0, keepdims=True) * inverse[s]
                    )
                pool_v[s : s + 1, :] = jnp.concatenate(parts, axis=1)
            hat, inv = norm_parts(pool_v[...])
            low_n = (hat * fgain[...]).astype(BF)
            nl_v[...] = low_n
            logits = mm(low_n, head_w[...])
            kn = known[pick]
            lb = label[pick]
            tail = jnp.exp(-jnp.abs(logits))
            soft = jnp.maximum(logits, 0.0) + jnp.log(1.0 + tail)
            terms = kn * (soft - lb * logits)
            gate = jnp.where(logits >= 0.0, 1.0, tail) / (1.0 + tail)
            dlog = (kn * (gate - lb) * shrink).astype(BF)
            dlog_v[...] = dlog
            d_n = mm(dlog, head_w[...], NT)
            side_v[...] = jnp.zeros_like(side_v)
            side_v[0:1, :] = jnp.sum(d_n * hat, 0, keepdims=True)
            side_v[1:2, 0:LANES] = jnp.sum(terms, 0, keepdims=True)
            d_pool = norm_back(d_n, fgain[...], hat, inv)
            pool_v[...] = d_pool
            for j in range(width // LANES):
                lanes = slice(j * LANES, (j + 1) * LANES)
                acc = jnp.zeros((tok, LANES), F32)
                for s in range(slides):
                    acc = acc + jnp.where(col == float(s), pool_v[s : s + 1, lanes] * inverse[s], 0.0)
                o_v[:, lanes] = acc
            tails = [
                pltpu.make_async_copy(o_v, dl_b.at[pick], sin.at[0]),
                pltpu.make_async_copy(nl_v, nl_b.at[pick], sin.at[1]),
                pltpu.make_async_copy(dlog_v, dlog_b.at[pick], sin.at[2]),
                pltpu.make_async_copy(side_v, side_b.at[pick], sin.at[3]),
            ]
            for c in tails:
                c.start()
            for c in tails:
                c.wait()

        for c in outs:
            c.wait()


def backward_kernel(
    heads, scal, ids, gain, rc_v, dl_b, lm_v, wqkv_t, wo_t, w1_t, w2,
    x_b, qkv_b, lse_b, mid_b, gp_b, *rest
):
    fresh = rest[0]
    n_buf = 5
    rest = rest[1:] if fresh else rest[1 + n_buf :]
    send_h = rest[0]
    (dbr_b, dup_b, dat_b, dqkv_b, gg_b) = rest[1 : 1 + n_buf]
    (dl_v, x_v, qkv_v, lse_v, mid_v, gp_v,
     dbr_v, dup_v, dat_v, dqkv_v, gg_v, dm_v, q_t, k_t, do_v, do_t, dq_t, p_v, ds_v, sin, sout) = rest[1 + n_buf :]
    valid, pick, last = scal[0], scal[1], scal[3]
    tok, width = x_v.shape
    size = width // heads
    scale = size ** (-0.5)
    per = 8

    @pl.when(valid == 1)
    def _():
        from_head = pltpu.make_async_copy(dl_b.at[pick], dl_v, sin.at[0])

        @pl.when(last == 1)
        def _():
            from_head.start()

        loads = [
            pltpu.make_async_copy(gp_b.at[pick], gp_v, sin.at[1]),
            pltpu.make_async_copy(mid_b.at[pick], mid_v, sin.at[2]),
            pltpu.make_async_copy(qkv_b.at[pick], qkv_v, sin.at[3]),
            pltpu.make_async_copy(lse_b.at[pick], lse_v, sin.at[4]),
            pltpu.make_async_copy(x_b.at[pick], x_v, sin.at[5]),
        ]
        for c in loads:
            c.start()
        outs = []

        def emit(src, dst):
            c = pltpu.make_async_copy(src, dst, sout.at[len(outs)])
            c.start()
            outs.append(c)

        row, col = same_slide(ids, pick)
        same = row == col

        @pl.when(last == 1)
        def _():
            from_head.wait()

        @pl.when(last != 1)
        def _():
            dl_v[...] = rc_v[...].astype(F32)

        dbr_v[...] = dl_v[...].astype(BF)
        emit(dbr_v, dbr_b.at[pick])
        loads[0].wait()
        ff = w2.shape[1]
        part = ff // 4
        for j in range(4):
            cols = slice(j * part, (j + 1) * part)
            dup_v[:, cols] = (mm(dbr_v[...], w2[:, cols]) * gp_v[:, cols]).astype(BF)
        emit(dup_v, dup_b.at[pick])
        d_b = mm(dup_v[...], w1_t[...])
        loads[1].wait()
        hat, inv = norm_parts(mid_v[...])
        gg_v[1:2, :] = jnp.sum(d_b * hat, 0, keepdims=True)
        d_mid = dl_v[...] + norm_back(d_b, gain[1:2, :], hat, inv)
        dm_v[...] = d_mid
        dat_v[...] = d_mid.astype(BF)
        emit(dat_v, dat_b.at[pick])
        loads[2].wait()
        q_t[...] = qkv_v[:, :width].T
        k_t[...] = qkv_v[:, width : 2 * width].T
        do_v[...] = mm(dat_v[...], wo_t[...]).astype(BF)
        do_t[...] = do_v[...].T
        loads[3].wait()
        lane = lax.broadcasted_iota(jnp.int32, (tok, LANES), 1)
        for group in range(heads // per):
            for i in range(per):
                h = group * per + i
                low, high = window(h, size)
                s = mm(qkv_v[:, width + low : width + high], placed_rows(q_t, h, size)) * scale
                s = s + jnp.where(same, lm_v[h], -1000000000.0)
                p = jnp.exp(s - lse_v[h : h + 1, :])
                dp = mm(qkv_v[:, 2 * width + low : 2 * width + high], placed_rows(do_t, h, size))
                inner_sum = jnp.sum(dp * p, 0, keepdims=True)
                ds = (p * (dp - inner_sum)).astype(BF)
                p_v[:, i * tok : (i + 1) * tok] = p.astype(BF)
                ds_v[:, i * tok : (i + 1) * tok] = ds
                dq_t[h * size : (h + 1) * size, :] = mm(k_t[h * size : (h + 1) * size, :], ds) * scale
            base = group * per * size
            for block in range(base // LANES, (base + per * size) // LANES):
                left = block * LANES
                inside = [
                    i for i in range(per)
                    if (group * per + i) * size < left + LANES and (group * per + i + 1) * size > left
                ]
                spans = slice(inside[0] * tok, (inside[-1] + 1) * tok)
                q_parts, o_parts = [], []
                for i in inside:
                    start = (group * per + i) * size - left
                    keep = (lane >= start) & (lane < start + size)
                    q_parts.append(jnp.where(keep, qkv_v[:, left : left + LANES], jnp.zeros((), BF)))
                    o_parts.append(jnp.where(keep, do_v[:, left : left + LANES], jnp.zeros((), BF)))
                dk = mm(ds_v[:, spans], jnp.concatenate(q_parts, axis=0)) * scale
                dv = mm(p_v[:, spans], jnp.concatenate(o_parts, axis=0))
                dqkv_v[:, width + left : width + left + LANES] = dk.astype(BF)
                dqkv_v[:, 2 * width + left : 2 * width + left + LANES] = dv.astype(BF)
        dqkv_v[:, :width] = dq_t[...].T.astype(BF)
        emit(dqkv_v, dqkv_b.at[pick])
        d_a = mm(dqkv_v[...], wqkv_t[...])
        loads[4].wait()
        hat, inv = norm_parts(x_v[...].astype(F32))
        gg_v[0:1, :] = jnp.sum(d_a * hat, 0, keepdims=True)
        emit(gg_v, gg_b.at[pick])
        send_h[...] = (dm_v[...] + norm_back(d_a, gain[0:1, :], hat, inv)).astype(BF)
        for c in outs:
            c.wait()


def spec_any():
    return pl.BlockSpec(memory_space=pltpu.HBM)


def spec_vmem():
    return pl.BlockSpec(memory_space=pltpu.VMEM)


def resident(value):
    return pltpu.with_memory_space_constraint(value, pltpu.VMEM)


def in_hbm(value):
    return pltpu.with_memory_space_constraint(value, pltpu.HBM)


def after(value, *others):
    return lax.optimization_barrier((value, *others))[0]


def load_body(counts, cuts, offsets, *refs):
    pieces, rest = refs[: sum(counts)], refs[sum(counts) :]
    n_out = sum(len(c) for c in cuts)
    straight, turned, sems = rest[:n_out], rest[n_out : 2 * n_out], rest[-1]
    copies, first, base = [], 0, 0
    for count, cut in zip(counts, cuts):
        mine = []
        for i in range(first, first + count):
            rows = pl.ds(pl.multiple_of(offsets[i], 16), pieces[i].shape[0])
            for j, (low, high) in enumerate(cut):
                copy = pltpu.make_async_copy(
                    pieces[i].at[:, low:high],
                    straight[base + j].at[rows, :],
                    sems.at[len(copies) * sum(counts) * 2 + len(mine)],
                )
                copy.start()
                mine.append(copy)
        copies.append(mine)
        first, base = first + count, base + len(cut)
    base = 0
    for mine, cut in zip(copies, cuts):
        for copy in mine:
            copy.wait()
        for j in range(base, base + len(cut)):
            step = 256

            def turn(index, carry):
                here = pl.ds(pl.multiple_of(index * step, step), step)
                turned[j][:, here] = straight[j][here, :].T
                return carry

            lax.fori_loop(0, straight[j].shape[0] // step, turn, 0)
        base += len(cut)


def load_weights(groups, cuts):
    counts = [len(pieces) for pieces, _ in groups]
    rows = sum(piece.shape[0] for piece in groups[0][0])
    sizes = [high - low for cut in cuts for low, high in cut]
    pieces = [in_hbm(piece) for group, _ in groups for piece in group]
    offsets = jnp.stack([start for _, starts in groups for start in starts]).astype(jnp.int32)
    return pl.pallas_call(
        functools.partial(load_body, counts, cuts),
        out_shape=[pltpu.VMEM((rows, n), BF) for n in sizes] + [pltpu.VMEM((n, rows), BF) for n in sizes],
        in_specs=[pl.BlockSpec(memory_space=pltpu.SMEM)]
        + [pl.BlockSpec(memory_space=pl.ANY)] * len(pieces),
        out_specs=[spec_vmem()] * (2 * len(sizes)),
        scratch_shapes=[pltpu.SemaphoreType.DMA((len(groups) * sum(counts) * 2,))],
        compiler_params=pltpu.CompilerParams(vmem_limit_bytes=8 << 20),
        name="load_weights",
    )(offsets, *pieces)


def weight_grad_body(pairs, rows, order, *refs):
    lefts, rights = refs[:pairs], refs[pairs : 2 * pairs]
    send, keep, turned, ordered, grad, left_v, right_v, sin, sout = refs[2 * pairs :]
    step = 768
    width = turned.shape[0]
    half = width // 2
    ins, outs, col = [], [], 0
    for n, (left, right) in enumerate(zip(lefts, rights)):
        ins.append(pltpu.make_async_copy(left, left_v.at[n], sin.at[len(ins)]))
        for start in range(0, right.shape[1], step):
            ins.append(
                pltpu.make_async_copy(
                    right.at[:, start : start + step],
                    right_v.at[:, col : col + step],
                    sin.at[len(ins)],
                )
            )
            col += step
    for copy in ins:
        copy.start()
    at, col = 0, 0
    for n, right in enumerate(rights):
        ins[at].wait()
        at += 1
        turned[...] = left_v[n].T
        for k in range(width // rows):
            here = pl.ds(pl.multiple_of(order[k] * rows, 16), rows)
            ordered[k * rows : (k + 1) * rows, :] = turned[here, :]
        for start in range(0, right.shape[1], step):
            ins[at].wait()
            at += 1
            cols = slice(col, col + step)
            for part, target in ((slice(0, half), send), (slice(half, width), keep)):
                grad[part, cols] = mm(ordered[part, :], right_v[:, cols]).astype(BF)
                copy = pltpu.make_async_copy(
                    grad.at[part, cols], target.at[:, cols], sout.at[len(outs)]
                )
                copy.start()
                outs.append(copy)
            col += step
    for copy in outs:
        copy.wait()


def weight_grad(order, pairs, rows):
    lefts, rights = [p[0] for p in pairs], [p[1] for p in pairs]
    tok, width = lefts[0].shape
    cols = sum(r.shape[1] for r in rights)
    half = pltpu.HBM((width // 2, cols), BF)
    n = len(pairs)
    return pl.pallas_call(
        functools.partial(weight_grad_body, n, rows),
        out_shape=[half, half],
        in_specs=[pl.BlockSpec(memory_space=pltpu.SMEM)] + [spec_any()] * (2 * n),
        out_specs=[spec_any()] * 2,
        scratch_shapes=[
            pltpu.VMEM((width, tok), BF), pltpu.VMEM((width, tok), BF), pltpu.VMEM((width, cols), BF),
            pltpu.VMEM((n, tok, width), BF), pltpu.VMEM((tok, cols), BF),
            pltpu.SemaphoreType.DMA((n + cols // 768,)), pltpu.SemaphoreType.DMA((2 * (cols // 768),)),
        ],
        compiler_params=pltpu.CompilerParams(vmem_limit_bytes=24 << 20),
        cost_estimate=pl.CostEstimate(
            flops=2 * tok * width * cols, bytes_accessed=3 * width * cols, transcendentals=0
        ),
        name="weight_grad",
    )(order, *[in_hbm(v) for v in lefts], *[in_hbm(v) for v in rights])


def forward_call(heads, slides, shrink, scal, ids, gain, fgain, head_w, known, label, x0, received, lm, weights, bufs):
    micro, tok, width = x0.shape
    ff = weights[2].shape[1]
    rows = known.shape[1]
    shapes = [
        ((tok, width), BF), ((tok, 3 * width), BF), ((heads, tok), F32), ((tok, width), BF),
        ((tok, width), F32), ((tok, ff), F32), ((tok, ff), BF), ((tok, width), BF), ((tok, width), BF),
        ((tok, width), F32), ((rows, width), BF), ((rows, LANES), BF), ((8, width), F32),
    ]
    fresh = bufs is None
    given = [] if fresh else list(bufs)
    vm = lambda index: pltpu.VMEM(*shapes[index])
    n_in = 18
    out = pl.pallas_call(
        functools.partial(forward_body, heads, slides, shrink, fresh),
        out_shape=[pltpu.VMEM((tok, width), BF)]
        + [pltpu.HBM((micro,) + s, d) for s, d in shapes],
        in_specs=[pl.BlockSpec(memory_space=pltpu.SMEM)]
        + [spec_vmem()] * 17
        + [spec_any()] * len(given),
        out_specs=[spec_vmem()] + [spec_any()] * len(shapes),
        input_output_aliases={n_in + i: 1 + i for i in range(len(given))},
        scratch_shapes=[
            vm(0), vm(1), vm(2), vm(3), vm(4), vm(5), vm(6), vm(7), vm(8),
            pltpu.VMEM((tok, width), F32),
            pltpu.VMEM((width, tok), BF), pltpu.VMEM((width, tok), BF), pltpu.VMEM((width, tok), F32),
            pltpu.VMEM((rows, width), F32), vm(10), vm(11), vm(12),
            pltpu.SemaphoreType.DMA((4,)), pltpu.SemaphoreType.DMA((9,)),
        ],
        compiler_params=pltpu.CompilerParams(vmem_limit_bytes=14 << 20),
        cost_estimate=pl.CostEstimate(flops=7 << 30, bytes_accessed=8 << 20, transcendentals=1 << 20),
        name="layer_forward",
    )(
        scal, ids, gain, fgain, head_w, known, label, resident(x0), received, resident(lm),
        *[resident(w) for w in weights], *[in_hbm(b) for b in given],
    )
    return out[0], out[1:]


def backward_call(heads, scal, ids, gain, received, records, lm, weights, bufs):
    x_b, qkv_b, lse_b, mid_b, gp_b, dl_b = records
    micro, tok, width = x_b.shape
    ff = weights[3].shape[1]
    shapes = [((tok, width), BF), ((tok, ff), BF), ((tok, width), BF), ((tok, 3 * width), BF), ((8, width), F32)]
    fresh = bufs is None
    given = [] if fresh else list(bufs)
    n_in = 15
    out = pl.pallas_call(
        functools.partial(backward_body, heads, fresh),
        out_shape=[pltpu.VMEM((tok, width), BF)]
        + [pltpu.HBM((micro,) + s, d) for s, d in shapes],
        in_specs=[pl.BlockSpec(memory_space=pltpu.SMEM)] + [spec_vmem()] * 3 + [spec_any()]
        + [spec_vmem()] * 5 + [spec_any()] * (5 + len(given)),
        out_specs=[spec_vmem()] + [spec_any()] * len(shapes),
        input_output_aliases={n_in + i: 1 + i for i in range(len(given))},
        scratch_shapes=[
            pltpu.VMEM((tok, width), F32),
            pltpu.VMEM((tok, width), BF), pltpu.VMEM((tok, 3 * width), BF), pltpu.VMEM((heads, tok), F32),
            pltpu.VMEM((tok, width), F32), pltpu.VMEM((tok, ff), F32),
        ]
        + [pltpu.VMEM(s, d) for s, d in shapes]
        + [
            pltpu.VMEM((tok, width), F32),
            pltpu.VMEM((width, tok), BF), pltpu.VMEM((width, tok), BF),
            pltpu.VMEM((tok, width), BF), pltpu.VMEM((width, tok), BF), pltpu.VMEM((width, tok), F32),
            pltpu.VMEM((tok, 8 * tok), BF), pltpu.VMEM((tok, 8 * tok), BF),
            pltpu.SemaphoreType.DMA((6,)), pltpu.SemaphoreType.DMA((6,)),
        ],
        compiler_params=pltpu.CompilerParams(vmem_limit_bytes=14 << 20),
        cost_estimate=pl.CostEstimate(flops=10 << 30, bytes_accessed=8 << 20, transcendentals=1 << 20),
        name="layer_backward",
    )(
        scal, ids, gain, received, in_hbm(dl_b), resident(lm), *[resident(w) for w in weights],
        *[in_hbm(b) for b in (x_b, qkv_b, lse_b, mid_b, gp_b)], *[in_hbm(b) for b in given],
    )
    return out[0], out[1:]


def forward_body(heads, slides, shrink, fresh, *refs):
    forward_kernel(heads, slides, shrink, *refs[:18], fresh, *refs[18:])


def backward_body(heads, fresh, *refs):
    backward_kernel(heads, *refs[:15], fresh, *refs[15:])


def adam(weight, grad, first, second, rate, decay):
    first = BETA_ONE * first + (1.0 - BETA_ONE) * grad
    second = BETA_TWO * second + (1.0 - BETA_TWO) * grad * grad
    mhat = first / (1.0 - BETA_ONE**STEP)
    vhat = second / (1.0 - BETA_TWO**STEP)
    return (first, second, weight - rate * (mhat / (jnp.sqrt(vhat) + ADAM_EPS) + decay * weight))


def per_device(
    tiles,
    slide_ids,
    coords,
    known,
    labels,
    mats,
    mats_m,
    mats_v,
    gains,
    gains_m,
    gains_v,
    final_gain,
    fgain_m,
    fgain_v,
    w_in,
    win_m,
    win_v,
    head,
    head_m,
    head_v,
):
    sections = lax.axis_size("section")
    dp = lax.axis_size("dp")
    section = lax.axis_index("section")
    dp_index = lax.axis_index("dp")
    near = dp // 2
    side_of, place = dp_index // near, dp_index % near
    row_of, core = section // 2, section % 2
    stage = 2 * row_of + (side_of ^ row_of)
    micro, tok = slide_ids.shape
    heads = HEADS
    slides, genes = known.shape[1:]
    width = w_in.shape[1]
    rows, wide_cols = mats.shape[2:]
    direct = dp == 8 and sections == 4 and rows % 32 == 0

    def join(side, place, row, core):
        return side * near + place, row * 2 + core

    def layer_turn(d, s):
        side, at, row, c = d // near, d % near, s // 2, s % 2
        target = join(c ^ row, at, row, side ^ row)
        return None if target == (d, s) else target

    def pack_turn(d, s):
        side, at, row, c = d // near, d % near, s // 2, s % 2
        target = join(c, at, row, side)
        return None if target == (d, s) else target

    own_layer = side_of == (core ^ row_of)
    own_packs = side_of == core

    def slot(flip_c, flip_m):
        return (core ^ flip_c ^ row_of) * near + (place ^ flip_m)

    groups = [
        [
            (side * near + m) * sections + row * 2 + (half ^ row)
            for half in range(2)
            for m in range(near)
        ]
        for side in range(2)
        for row in range(sections // 2)
    ]

    def to_next(distance, tick):
        def route(d, s):
            side, at, row, c = d // near, d % near, s // 2, s % 2
            here = 2 * row + (side ^ row)
            goal = here + distance
            pack = tick - 2 * (here if distance > 0 else sections - 1 - here)
            if not (0 <= goal < sections and 0 <= pack < micro):
                return None
            return join((goal % 2) ^ (goal // 2), at, goal // 2, c)

        return route

    def gather_all(blocks, early, ready):
        owns, got = [], None
        for n, block in enumerate(blocks):
            got = moved(block if got is None else after(block, got), layer_turn)
            if n:
                got = lax.optimization_barrier((got, owns[-1], early[n - 1]))[0]
            owns.append(after(jnp.where(own_layer, block, got)))
        if not direct:
            return [
                (
                    [
                        lax.all_gather(
                            own, ("dp", "section"), axis=0, tiled=True, axis_index_groups=groups
                        )
                    ],
                    [jnp.zeros((), jnp.int32)],
                )
                for own in owns
            ]
        out = []
        for n, own in enumerate(owns):
            side = moved(own, flip_dp(1))
            over = moved(own, flip_dp(2))
            if n == 0:
                side, over = lax.optimization_barrier((side, over, ready, owns[1]))[:2]
            if n == 1:
                side, over = lax.optimization_barrier((side, over, owns[2]))[:2]
            far = moved(side, flip_dp(2)) if n == 1 else moved(over, flip_dp(1))
            pieces, starts = [], []
            for flip_m, piece in enumerate((own, side, over, far)):
                pieces += [piece, moved(piece, flip_section(1))]
                starts += [slot(0, flip_m) * rows, slot(1, flip_m) * rows]
            out.append((pieces, starts))
        return out

    def scatter_all(grads):
        order = jnp.stack([slot(1 - k // 4, k % 4) for k in range(8)]).astype(jnp.int32)
        if not direct:
            outs = []
            for pairs in grads:
                grad = jnp.concatenate([inner(l, r).astype(BF) for l, r in pairs], axis=1)
                own = lax.psum_scatter(
                    grad, ("dp", "section"), scatter_dimension=0, tiled=True, axis_index_groups=groups
                )
                outs.append(jnp.where(own_layer, own, moved(own, layer_turn)).astype(F32))
            return outs, outs[:1] * 4
        kept, got = [], []
        for pairs in grads:
            send, keep = weight_grad(order, pairs, rows)
            kept.append(keep.reshape(4, rows, wide_cols))
            got.append(moved(send, flip_section(1)).reshape(4, rows, wide_cols))

        def both(n, m):
            return kept[n][m].astype(F32) + got[n][m].astype(F32)

        fars = []
        for n in range(3):
            if n:
                got[n] = after(got[n], fars[-1])
            fars.append(after(both(n, 3).astype(BF)))
        sides, overs = [], []
        for n in range(3):
            far = moved(fars[n], flip_dp(2) if n == 1 else flip_dp(1))
            if n:
                far = after(far, overs[-1])
            extra = far.astype(F32)
            side = both(n, 1) + (extra if n == 1 else 0.0)
            over = both(n, 2) + (0.0 if n == 1 else extra)
            side, over = lax.optimization_barrier((side.astype(BF), over.astype(BF)))
            sides.append(side)
            overs.append(over)
        outs, last = [], None
        for n in range(3):
            side, over = moved(sides[n], flip_dp(1)), moved(overs[n], flip_dp(2))
            if last is not None:
                side, over = lax.optimization_barrier((side, over, last))[:2]
            last = after((both(n, 0) + side.astype(F32) + over.astype(F32)).astype(BF))
            outs.append((last, moved(last, layer_turn)))
        marks = (overs[2], outs[0][0], outs[1][0], outs[2][0])
        return [jnp.where(own_layer, total, away).astype(F32) for total, away in outs], marks

    def over_section(block):
        other_row = moved(block, flip_section(2))
        pair = jnp.stack([block, other_row])
        other_core = moved(pair, flip_section(1))
        whole = jnp.zeros((sections,) + block.shape, block.dtype)
        for part, flip in ((block, 0), (other_row, 2), (other_core[0], 1), (other_core[1], 3)):
            whole = lax.dynamic_update_slice(
                whole, part[None], (section ^ flip,) + (0,) * block.ndim
            )
        return whole.reshape((sections * block.shape[0],) + block.shape[1:])

    got = moved(gains[0], layer_turn)
    gain = jnp.where(own_layer, gains[0], got)
    home = jnp.concatenate(
        [slide_ids, known.reshape(micro, -1), labels.reshape(micro, -1)], axis=1
    )
    home = jnp.where(own_packs, home, moved(home, pack_turn))
    ids = home[:, :tok]
    marks = home[:, tok:].reshape(micro, 2, slides, genes).astype(F32)
    in_low = over_section(w_in.astype(BF))
    table = jax.vmap(lambda c: position_table(c, width), in_axes=1)(coords)
    x0 = (
        jnp.dot(tiles.reshape(micro * tok, -1), in_low, preferred_element_type=F32).reshape(
            micro, tok, width
        )
        + table
    ).astype(BF)

    def to_first(d, s):
        return (d - near, s) if d >= near and s == 1 else None

    def to_home(d, s):
        return (d + near, s) if d < near and s == 1 else None

    ends = over_section(
        jnp.concatenate(
            [head, final_gain[:, None], jnp.zeros((head.shape[0], LANES - genes - 1), F32)], axis=1
        )
    )
    full_fgain = ends[:, genes][None, :]
    head_p = ends.astype(BF)
    slots = micro * dp * slides * genes
    shrink = 0.5 ** (slots - 1).bit_length()
    x0 = after(x0)
    cuts = (((0, 3 * width), (3 * width, wide_cols)), ((0, wide_cols),), ((0, wide_cols),))
    gathered = gather_all(
        [mats[0, n].astype(BF) for n in range(3)], (ends, x0), x0
    )
    x0 = jnp.where(core == 0, x0, moved(x0, to_first))
    x0, lm, ids, gain, gathered = lax.optimization_barrier(
        (x0, log_mult(heads, tok), ids, gain, gathered)
    )
    wqkv, wo, w1, w2, wqkv_t, wo_t, w1_t, w2_t = load_weights(gathered, cuts)
    ticks = micro + 2 * (sections - 1)
    late = 2 * (sections - 1)
    pad = ((0, 0), (0, 16 - slides), (0, LANES - genes))
    known_p = jnp.pad(marks[:, 0], pad)
    labels_p = jnp.pad(marks[:, 1], pad)
    def scalars(index):
        valid = (index >= 0) & (index < micro)
        return jnp.stack(
            [valid, jnp.clip(index, 0, micro - 1), stage == 0, stage == sections - 1]
        ).astype(jnp.int32)

    arrived = [jnp.zeros((tok, width), BF)] * 2
    bufs = None
    for tick in range(ticks):
        end_args = (full_fgain, head_p, known_p, labels_p)
        send, bufs = forward_call(
            heads, slides, shrink, scalars(tick - 2 * stage), ids, gain, *end_args, x0, arrived[tick], lm,
            (wqkv, wo, w1, w2_t, wqkv_t, wo_t, w1_t, w2), bufs,
        )
        arrived.append(moved(send, to_next(1, tick)) if tick + 2 < ticks else None)
    (x_b, qkv_b, lse_b, att_b, mid_b, gp_b, hid_b, a_b, b_b, dl_b, nl_b, dlog_b, side_b) = bufs
    records = (x_b, qkv_b, lse_b, mid_b, gp_b, dl_b)
    arrived = [jnp.zeros((tok, width), BF)] * 2
    bufs = None
    sends = []
    for tick in range(ticks):
        send, bufs = backward_call(
            heads, scalars(tick - 2 * (sections - 1 - stage)), ids, gain, arrived[tick], records,
            lm, (wqkv_t, wo_t, w1_t, w2), bufs,
        )
        sends.append(send)
        arrived.append(moved(send, to_next(-1, tick)) if tick + 2 < ticks else None)
    dbr_b, dup_b, dat_b, dqkv_b, gg_b = bufs
    nl_b, dlog_b, side_b = lax.optimization_barrier((nl_b, dlog_b, side_b, sends[-1]))[:3]
    flat = lambda v: v.reshape((-1, v.shape[-1]))
    (grad_down, grad_up, grad_attn), marks_done = scatter_all(
        [
            [(flat(dbr_b), flat(hid_b))],
            [(flat(b_b), flat(dup_b))],
            [(flat(a_b), flat(dqkv_b)), (flat(att_b), flat(dat_b))],
        ]
    )
    keep_own = (stage == 0) & (core == 0)
    take_far = (row_of == 0) & (side_of == 1) & (core == 1)
    d_parts = []
    for send in sends[late:]:
        far = moved(send, to_home)
        d_parts.append(jnp.where(keep_own, send, jnp.where(take_far, far, jnp.zeros((), BF))))
    d_first = jnp.stack(d_parts)
    d_first = d_first + moved(d_first, flip_section(2))
    d_first = d_first + moved(d_first, flip_section(1))
    in_rows = w_in.shape[0]
    mine = lax.dynamic_slice_in_dim(flat(tiles), section * in_rows, in_rows, 1)
    piece = inner(mine, flat(d_first)).astype(BF)
    bits = [1 << k for k in range(dp.bit_length() - 1)]
    size = in_rows
    for n, bit in enumerate(bits):
        size //= 2
        up = (dp_index // bit) % 2
        if n < 3:
            piece = after(piece, marks_done[n])
        keep = lax.dynamic_slice_in_dim(piece, up * size, size, 0)
        away = lax.dynamic_slice_in_dim(piece, (1 - up) * size, size, 0)
        piece = (keep.astype(F32) + moved(away, flip_dp(bit)).astype(F32)).astype(BF)
    part_in = after(piece, marks_done[3])
    for bit in reversed(bits):
        up = (dp_index // bit) % 2 == 1
        other = moved(part_in, flip_dp(bit))
        part_in = jnp.concatenate([jnp.where(up, other, part_in), jnp.where(up, part_in, other)])
    part_in = part_in.astype(F32)
    on_last = stage == sections - 1
    grad_head = jnp.where(on_last, inner(flat(nl_b), flat(dlog_b)), 0.0)[:, :genes]
    side = jnp.where(on_last, jnp.sum(side_b, 0), 0.0)
    seen = jnp.pad(jnp.sum(marks[:, 0]).reshape(1), (0, LANES - 1))
    small = jnp.concatenate(
        [jnp.sum(gg_b, 0)[:2].reshape(-1), seen, side[0], grad_head.reshape(-1), side[1, :LANES]]
    )
    small = small + moved(small, flip_section(1))
    bit = 1
    while bit < near:
        small = small + moved(small, flip_dp(bit))
        bit *= 2
    n_gain = 2 * width
    layer_gain, ends = small[:n_gain].reshape(2, width), small[n_gain + LANES :]
    count = jnp.maximum(small[n_gain], 1.0)
    sum_gain = jnp.where(own_layer, layer_gain, moved(layer_gain, layer_turn))

    def from_last(side_to, row_to):
        last_row = sections // 2 - 1
        last_side = 1 ^ last_row

        def route(d, s):
            if d // near != last_side or s // 2 != last_row:
                return None
            return join(side_to, d % near, row_to, s % 2)

        return None if (side_to, row_to) == (last_side, last_row) else moved(ends, route)

    ends = jnp.where(on_last, ends, 0.0)
    for side_to in range(2):
        for row_to in range(sections // 2):
            got = from_last(side_to, row_to)
            ends = ends if got is None else ends + got
    sum_fgain = ends[:width]
    sum_head = ends[width : width + width * genes].reshape(width, genes)
    loss_sum = jnp.sum(ends[width + width * genes :])
    part = width // sections
    part_head = lax.dynamic_slice_in_dim(sum_head, section * part, part, 0)
    part_fgain = lax.dynamic_slice_in_dim(sum_fgain, section * part, part, 0)
    shards = (grad_attn, grad_up, grad_down)
    lead = (place == 0) & (core == 0)
    squares = (
        sum(jnp.sum(g * g) for g in shards)
        + jnp.sum(jnp.square(piece.astype(F32)))
        + jnp.where(lead, jnp.sum(layer_gain * layer_gain), 0.0)
        + jnp.where(lead & on_last, jnp.sum(sum_fgain * sum_fgain) + jnp.sum(sum_head * sum_head), 0.0)
    )
    total_sq = spread_sum(squares.reshape(1, 1))[0, 0]
    shard_wide = jnp.stack(shards)[None]
    grow = 1.0 / (shrink * count)
    grad_norm = jnp.sqrt(total_sq) * grow
    factor = CLIP / jnp.maximum(grad_norm, CLIP) * grow
    mats_out = adam(mats, shard_wide * factor, mats_m, mats_v, RATE, DECAY)
    gains_out = adam(gains, sum_gain[None] * factor, gains_m, gains_v, RATE_GAIN, 0.0)
    fgain_out = adam(final_gain, part_fgain * factor, fgain_m, fgain_v, RATE_GAIN, 0.0)
    in_out = adam(w_in, part_in * factor, win_m, win_v, RATE, DECAY)
    head_out = adam(head, part_head * factor, head_m, head_v, RATE, DECAY)
    return (
        grad_norm,
        loss_sum,
        count,
        mats_out[0],
        mats_out[1],
        mats_out[2],
        gains_out[0],
        gains_out[1],
        gains_out[2],
        fgain_out[0],
        fgain_out[1],
        fgain_out[2],
        in_out[0],
        in_out[1],
        in_out[2],
        head_out[0],
        head_out[1],
        head_out[2],
    )


def solution(mesh):
    placed = (
        P("dp", None, None),
        P("dp", None),
        P(None, "dp", None),
        P("dp", None, None),
        P("dp", None, None),
        P("section", None, "dp", None),
        P("section", None, "dp", None),
        P("section", None, "dp", None),
        P("section", None, None),
        P("section", None, None),
        P("section", None, None),
        P("section"),
        P("section"),
        P("section"),
        P("section", None),
        P("section", None),
        P("section", None),
        P("section", None),
        P("section", None),
        P("section", None),
    )
    return jax.shard_map(
        per_device,
        mesh=mesh,
        in_specs=placed,
        out_specs=(
            P(),
            P(),
            P(),
            P("section", None, "dp", None),
            P("section", None, "dp", None),
            P("section", None, "dp", None),
            P("section", None, None),
            P("section", None, None),
            P("section", None, None),
            P("section"),
            P("section"),
            P("section"),
            P("section", None),
            P("section", None),
            P("section", None),
            P("section", None),
            P("section", None),
            P("section", None),
        ),
        check_vma=False,
    )
```

```python
import functools

import jax
import jax.numpy as jnp
from jax import lax
from jax.experimental import pallas as pl
from jax.experimental.pallas import tpu as pltpu
from jax.sharding import PartitionSpec as P

HEADS = 16
STEP = 10


EPS_NORM = 1e-05
CLIP = 0.05
BETA_ONE = 0.9
BETA_TWO = 0.95
ADAM_EPS = 1e-08
RATE = 0.06
RATE_GAIN = 1.0
DECAY = 0.1
RATIOS = (1, 2, 4, 8, 16)

def moved(block, route):
    dp, sections = lax.axis_size("dp"), lax.axis_size("section")
    pairs = []
    for d in range(dp):
        for s in range(sections):
            target = route(d, s)
            if target is not None:
                pairs.append((d * sections + s, target[0] * sections + target[1]))
    return lax.ppermute(block, ("dp", "section"), pairs)


def flip_dp(bit):
    return lambda d, s: (d ^ bit, s)


def flip_section(bit):
    return lambda d, s: (d, s ^ bit)


def spread_sum(value):
    dp, sections = lax.axis_size("dp"), lax.axis_size("section")
    for k in range(sections.bit_length() - 1):
        value = value + moved(value, flip_section(1 << k))
    for k in range(dp.bit_length() - 1):
        value = value + moved(value, flip_dp(1 << k))
    return value


def inner(left, right):
    return lax.dot_general(
        left, right, (((0,), (0,)), ((), ())), preferred_element_type=jnp.float32
    )


def position_table(coord, width):
    quarter = width // 4
    freq = jnp.exp(-jnp.log(10000.0) * jnp.arange(quarter, dtype=jnp.float32) / quarter)
    along = coord[0].astype(jnp.float32)[:, None] * freq
    across = coord[1].astype(jnp.float32)[:, None] * freq
    return jnp.concatenate(
        [jnp.sin(along), jnp.cos(along), jnp.sin(across), jnp.cos(across)], axis=1
    )


def log_mult(heads, tok):
    place = jnp.arange(tok, dtype=jnp.int32)
    head_idx = jnp.arange(heads, dtype=jnp.int32)
    mult = jnp.zeros((heads, tok, tok), jnp.float32)
    for ratio in RATIOS:
        hit = (place[None, :] % ratio == head_idx[:, None] % ratio).astype(jnp.float32)
        mult = mult + hit[:, :, None] * hit[:, None, :]
    return jnp.log(mult)


NN = (((1,), (0,)), ((), ()))
NT = (((1,), (1,)), ((), ()))
TN = (((0,), (0,)), ((), ()))
LANES = 128
BF = jnp.bfloat16
F32 = jnp.float32


def mm(left, right, dims=NN):
    return lax.dot_general(left, right, dims, preferred_element_type=F32)


def norm_parts(value):
    mean = jnp.mean(value, -1, keepdims=True)
    centred = value - mean
    var = jnp.mean(centred * centred, -1, keepdims=True)
    inv = lax.rsqrt(var + EPS_NORM)
    return centred * inv, inv


def norm_back(dvalue, gain, hat, inv):
    dhat = dvalue * gain
    return inv * (
        dhat
        - jnp.mean(dhat, -1, keepdims=True)
        - hat * jnp.mean(dhat * hat, -1, keepdims=True)
    )


def window(head, size):
    low = head * size // LANES * LANES
    high = -(-(head + 1) * size // LANES) * LANES
    return low, high


def placed_rows(ref, head, size):
    low, high = window(head, size)
    before, after = head * size - low, high - (head + 1) * size
    tok = ref.shape[1]
    parts = [ref[head * size : (head + 1) * size, :]]
    if before:
        parts = [jnp.zeros((before, tok), ref.dtype)] + parts
    if after:
        parts = parts + [jnp.zeros((after, tok), ref.dtype)]
    return jnp.concatenate(parts, axis=0) if len(parts) > 1 else parts[0]


def same_slide(ids_ref, pick):
    tok = ids_ref.shape[1]
    row = jnp.broadcast_to(ids_ref[pl.ds(pick, 1), :].astype(F32), (tok, tok))
    return row, row.T


def forward_kernel(
    heads, slides, shrink, scal, ids, gain, fgain, head_w, known, label,
    x0, rc, lm_v, wqkv, wo, w1, w2t, wqkv_t, wo_t, w1_t, w2, *rest
):
    fresh = rest[0]
    n_buf = 13
    rest = rest[1:] if fresh else rest[1 + n_buf :]
    send_h = rest[0]
    (x_b, qkv_b, lse_b, att_b, mid_b, gp_b, hid_b, a_b, b_b, dl_b, nl_b, dlog_b, side_b) = rest[1 : 1 + n_buf]
    (x_v, qkv_v, lse_v, att_v, mid_v, gp_v, hid_v, a_v, b_v, o_v,
     q_t, v_t, o_t, pool_v, nl_v, dlog_v, side_v, sin, sout) = rest[1 + n_buf :]
    valid, pick, first, last = scal[0], scal[1], scal[2], scal[3]
    tok, width = x_v.shape
    size = width // heads
    scale = size ** (-0.5)

    @pl.when(valid == 1)
    def _():
        @pl.when(first == 1)
        def _():
            x_v[...] = x0[pick]

        @pl.when(first != 1)
        def _():
            x_v[...] = rc[...]

        outs = []

        def emit(src, dst):
            c = pltpu.make_async_copy(src, dst, sout.at[len(outs)])
            c.start()
            outs.append(c)

        row, col = same_slide(ids, pick)
        same = row == col

        emit(x_v, x_b.at[pick])
        x = x_v[...].astype(F32)
        hat, _ = norm_parts(x)
        a_v[...] = (hat * gain[0:1, :]).astype(BF)
        emit(a_v, a_b.at[pick])
        qkv_v[...] = mm(a_v[...], wqkv[...]).astype(BF)
        emit(qkv_v, qkv_b.at[pick])
        q_t[...] = qkv_v[:, :width].T
        v_t[...] = qkv_v[:, 2 * width :].T
        for h in range(heads):
            low, high = window(h, size)
            s = mm(qkv_v[:, width + low : width + high], placed_rows(q_t, h, size)) * scale
            s = s + jnp.where(same, lm_v[h], -1000000000.0)
            top = jnp.max(s, 0, keepdims=True)
            e = jnp.exp(s - top)
            total = jnp.sum(e, 0, keepdims=True)
            lse_v[h : h + 1, :] = top + jnp.log(total)
            o = mm(v_t[h * size : (h + 1) * size, :], e.astype(BF))
            o_t[h * size : (h + 1) * size, :] = o * (1.0 / total)
        att_v[...] = o_t[...].T.astype(BF)
        emit(lse_v, lse_b.at[pick])
        emit(att_v, att_b.at[pick])
        middle = x + mm(att_v[...], wo[...])
        mid_v[...] = middle
        emit(mid_v, mid_b.at[pick])
        hat, _ = norm_parts(middle)
        b_v[...] = (hat * gain[1:2, :]).astype(BF)
        emit(b_v, b_b.at[pick])
        ff = w1.shape[1]
        part = ff // 4
        for j in range(4):
            cols = slice(j * part, (j + 1) * part)
            up = mm(b_v[...], w1[:, cols])
            square = up * up
            sig = 1.0 / (1.0 + jnp.exp(up * (-1.5957691216057308 - 0.07135481627159852 * square)))
            act = up * sig
            hid_v[:, cols] = act.astype(BF)
            slope = 1.5957691216057308 + 0.21406444881478 * square
            gp_v[:, cols] = sig + act * (1.0 - sig) * slope
        emit(gp_v, gp_b.at[pick])
        emit(hid_v, hid_b.at[pick])
        out = mid_v[...] + mm(hid_v[...], w2t[...])
        send_h[...] = out.astype(BF)

        @pl.when(last == 1)
        def _():
            o_v[...] = out
            pool_v[...] = jnp.zeros_like(pool_v)
            inverse = []
            for s in range(slides):
                inside = (col == float(s)).astype(F32)
                inverse.append(1.0 / jnp.sum(inside, 0, keepdims=True))
                parts = []
                for j in range(width // LANES):
                    parts.append(
                        jnp.sum(o_v[:, j * LANES : (j + 1) * LANES] * inside, 0, keepdims=True) * inverse[s]
                    )
                pool_v[s : s + 1, :] = jnp.concatenate(parts, axis=1)
            hat, inv = norm_parts(pool_v[...])
            low_n = (hat * fgain[...]).astype(BF)
            nl_v[...] = low_n
            logits = mm(low_n, head_w[...])
            kn = known[pick]
            lb = label[pick]
            tail = jnp.exp(-jnp.abs(logits))
            soft = jnp.maximum(logits, 0.0) + jnp.log(1.0 + tail)
            terms = kn * (soft - lb * logits)
            gate = jnp.where(logits >= 0.0, 1.0, tail) / (1.0 + tail)
            dlog = (kn * (gate - lb) * shrink).astype(BF)
            dlog_v[...] = dlog
            d_n = mm(dlog, head_w[...], NT)
            side_v[...] = jnp.zeros_like(side_v)
            side_v[0:1, :] = jnp.sum(d_n * hat, 0, keepdims=True)
            side_v[1:2, 0:LANES] = jnp.sum(terms, 0, keepdims=True)
            d_pool = norm_back(d_n, fgain[...], hat, inv)
            pool_v[...] = d_pool
            for j in range(width // LANES):
                lanes = slice(j * LANES, (j + 1) * LANES)
                acc = jnp.zeros((tok, LANES), F32)
                for s in range(slides):
                    acc = acc + jnp.where(col == float(s), pool_v[s : s + 1, lanes] * inverse[s], 0.0)
                o_v[:, lanes] = acc
            tails = [
                pltpu.make_async_copy(o_v, dl_b.at[pick], sin.at[0]),
                pltpu.make_async_copy(nl_v, nl_b.at[pick], sin.at[1]),
                pltpu.make_async_copy(dlog_v, dlog_b.at[pick], sin.at[2]),
                pltpu.make_async_copy(side_v, side_b.at[pick], sin.at[3]),
            ]
            for c in tails:
                c.start()
            for c in tails:
                c.wait()

        for c in outs:
            c.wait()


def backward_kernel(
    heads, scal, ids, gain, rc_v, dl_b, lm_v, wqkv_t, wo_t, w1_t, w2,
    x_b, qkv_b, lse_b, mid_b, gp_b, *rest
):
    fresh = rest[0]
    n_buf = 5
    rest = rest[1:] if fresh else rest[1 + n_buf :]
    send_h = rest[0]
    outs = rest[1 : 1 + n_buf]
    (dl_v, x_v, qkv_v, lse_v, mid_v, gp_v, dm_v, q_t, k_t, do_v, do_t, dq_t, p_v, ds_v, sin) = rest[1 + n_buf :]
    valid, pick, last = scal[0], scal[1], scal[3]
    dbr_v, dup_v, dat_v, dqkv_v, gg_v = [ref.at[pick] for ref in outs]
    tok, width = x_v.shape
    size = width // heads
    scale = size ** (-0.5)
    per = 8

    @pl.when(valid == 1)
    def _():
        from_head = pltpu.make_async_copy(dl_b.at[pick], dl_v, sin.at[0])

        @pl.when(last == 1)
        def _():
            from_head.start()

        loads = [
            pltpu.make_async_copy(gp_b.at[pick], gp_v, sin.at[1]),
            pltpu.make_async_copy(mid_b.at[pick], mid_v, sin.at[2]),
            pltpu.make_async_copy(qkv_b.at[pick], qkv_v, sin.at[3]),
            pltpu.make_async_copy(lse_b.at[pick], lse_v, sin.at[4]),
            pltpu.make_async_copy(x_b.at[pick], x_v, sin.at[5]),
        ]
        for c in loads:
            c.start()
        row, col = same_slide(ids, pick)
        same = row == col

        @pl.when(last == 1)
        def _():
            from_head.wait()

        @pl.when(last != 1)
        def _():
            dl_v[...] = rc_v[...].astype(F32)

        dbr_v[...] = dl_v[...].astype(BF)
        loads[0].wait()
        ff = w2.shape[1]
        part = ff // 4
        for j in range(4):
            cols = slice(j * part, (j + 1) * part)
            dup_v[:, cols] = (mm(dbr_v[...], w2[:, cols]) * gp_v[:, cols]).astype(BF)
        d_b = mm(dup_v[...], w1_t[...])
        loads[1].wait()
        hat, inv = norm_parts(mid_v[...])
        gg_v[1:2, :] = jnp.sum(d_b * hat, 0, keepdims=True)
        d_mid = dl_v[...] + norm_back(d_b, gain[1:2, :], hat, inv)
        dm_v[...] = d_mid
        dat_v[...] = d_mid.astype(BF)
        loads[2].wait()
        q_t[...] = qkv_v[:, :width].T
        k_t[...] = qkv_v[:, width : 2 * width].T
        do_v[...] = mm(dat_v[...], wo_t[...]).astype(BF)
        do_t[...] = do_v[...].T
        loads[3].wait()
        lane = lax.broadcasted_iota(jnp.int32, (tok, LANES), 1)
        for group in range(heads // per):
            for i in range(per):
                h = group * per + i
                low, high = window(h, size)
                s = mm(qkv_v[:, width + low : width + high], placed_rows(q_t, h, size)) * scale
                s = s + jnp.where(same, lm_v[h], -1000000000.0)
                p = jnp.exp(s - lse_v[h : h + 1, :])
                dp = mm(qkv_v[:, 2 * width + low : 2 * width + high], placed_rows(do_t, h, size))
                inner_sum = jnp.sum(dp * p, 0, keepdims=True)
                ds = (p * (dp - inner_sum)).astype(BF)
                p_v[:, i * tok : (i + 1) * tok] = p.astype(BF)
                ds_v[:, i * tok : (i + 1) * tok] = ds
                dq_t[h * size : (h + 1) * size, :] = mm(k_t[h * size : (h + 1) * size, :], ds) * scale
            base = group * per * size
            for block in range(base // LANES, (base + per * size) // LANES):
                left = block * LANES
                inside = [
                    i for i in range(per)
                    if (group * per + i) * size < left + LANES and (group * per + i + 1) * size > left
                ]
                spans = slice(inside[0] * tok, (inside[-1] + 1) * tok)
                q_parts, o_parts = [], []
                for i in inside:
                    start = (group * per + i) * size - left
                    keep = (lane >= start) & (lane < start + size)
                    q_parts.append(jnp.where(keep, qkv_v[:, left : left + LANES], jnp.zeros((), BF)))
                    o_parts.append(jnp.where(keep, do_v[:, left : left + LANES], jnp.zeros((), BF)))
                dk = mm(ds_v[:, spans], jnp.concatenate(q_parts, axis=0)) * scale
                dv = mm(p_v[:, spans], jnp.concatenate(o_parts, axis=0))
                dqkv_v[:, width + left : width + left + LANES] = dk.astype(BF)
                dqkv_v[:, 2 * width + left : 2 * width + left + LANES] = dv.astype(BF)
        dqkv_v[:, :width] = dq_t[...].T.astype(BF)
        d_a = mm(dqkv_v[...], wqkv_t[...])
        loads[4].wait()
        hat, inv = norm_parts(x_v[...].astype(F32))
        gg_v[0:1, :] = jnp.sum(d_a * hat, 0, keepdims=True)
        send_h[...] = (dm_v[...] + norm_back(d_a, gain[0:1, :], hat, inv)).astype(BF)


def spec_any():
    return pl.BlockSpec(memory_space=pltpu.HBM)


def spec_vmem():
    return pl.BlockSpec(memory_space=pltpu.VMEM)


def resident(value):
    return pltpu.with_memory_space_constraint(value, pltpu.VMEM)


def in_hbm(value):
    return pltpu.with_memory_space_constraint(value, pltpu.HBM)


def after(value, *others):
    return lax.optimization_barrier((value, *others))[0]


def load_body(cuts, plans, scal, *refs):
    n_out = sum(len(c) for c in cuts)
    n_in = len(refs) - 2 * n_out - 1
    pieces, straight, turned, sems = (
        refs[:n_in], refs[n_in : n_in + n_out], refs[n_in + n_out : -1], refs[-1]
    )

    def copies_of(chunk, flag):
        base = sum(len(c) for c in cuts[:chunk])
        out = []
        for n, (piece, place, part) in enumerate(plans[flag]):
            src = pieces[piece] if part is None else pieces[piece].at[part]
            src = src.at[chunk]
            rows = pl.ds(pl.multiple_of(scal[1 + place], 16), src.shape[0])
            for j, (low, high) in enumerate(cuts[chunk]):
                out.append(
                    pltpu.make_async_copy(
                        src.at[:, low:high], straight[base + j].at[rows, :], sems.at[chunk, n, j]
                    )
                )
        return out

    for flag in range(2):

        @pl.when(scal[0] == flag)
        def _():
            for chunk in range(len(cuts)):
                for copy in copies_of(chunk, flag):
                    copy.start()

    base = 0
    for chunk, cut in enumerate(cuts):
        for flag in range(2):

            @pl.when(scal[0] == flag)
            def _():
                for copy in copies_of(chunk, flag):
                    copy.wait()

        for j in range(base, base + len(cut)):
            step = 256

            def turn(index, carry):
                here = pl.ds(pl.multiple_of(index * step, step), step)
                turned[j][:, here] = straight[j][here, :].T
                return carry

            lax.fori_loop(0, straight[j].shape[0] // step, turn, 0)
        base += len(cut)


def load_weights(pieces, plans, scal, cuts, rows):
    sizes = [high - low for cut in cuts for low, high in cut]
    most = max(len(plan) for plan in plans)
    return pl.pallas_call(
        functools.partial(load_body, cuts, plans),
        out_shape=[pltpu.VMEM((rows, n), BF) for n in sizes] + [pltpu.VMEM((n, rows), BF) for n in sizes],
        in_specs=[pl.BlockSpec(memory_space=pltpu.SMEM)]
        + [pl.BlockSpec(memory_space=pl.ANY)] * len(pieces),
        out_specs=[spec_vmem()] * (2 * len(sizes)),
        scratch_shapes=[pltpu.SemaphoreType.DMA((len(cuts), most, 2))],
        compiler_params=pltpu.CompilerParams(vmem_limit_bytes=8 << 20),
        name="load_weights",
    )(scal, *[in_hbm(piece) for piece in pieces])


def weight_grads_body(shape, order, *refs):
    rows, micro, tok = shape
    lefts, rights, outs = refs[:4], refs[4:8], refs[8:11]
    turned, ordered, grad, left_v, hid_v, sin, sout = refs[11:]
    loads = [pltpu.make_async_copy(lefts[n], left_v.at[n], sin.at[n]) for n in range(3)]
    wide = pltpu.make_async_copy(rights[3], hid_v, sin.at[3])
    for copy in loads:
        copy.start()
    wide.start()
    taken = ordered.shape[0]
    cuts = (slice(0, rows), slice(rows, taken // 2), slice(taken // 2, taken))
    step = 768
    copies = []
    attn_cols = rights[1].shape[2]
    for chunk, n, col in ((1, 0, 0), (0, 1, 0), (0, 2, attn_cols), (2, 3, 0)):
        if n < 3:
            loads[n].wait()
            left, right = left_v.at[n], rights[n]
        else:
            wide.wait()
            left, right = lefts[3], hid_v
        for p in range(micro):
            turned[:, p * tok : (p + 1) * tok] = left[p].T
        for k in range(taken // rows):
            here = pl.ds(pl.multiple_of(order[k] * rows, 16), rows)
            ordered[k * rows : (k + 1) * rows, :] = turned[here, :]
        for start in range(0, right.shape[2], step):
            block = right[:, :, start : start + step].reshape(micro * tok, step)
            for low in range(0, taken, taken // 2):
                grad[chunk, low : low + taken // 2, col + start : col + start + step] = mm(
                    ordered[low : low + taken // 2, :], block
                ).astype(BF)
        if n == 1:
            continue
        for m, cut in enumerate(cuts):
            copy = pltpu.make_async_copy(grad.at[chunk, cut], outs[m].at[chunk], sout.at[chunk, m])
            copy.start()
            copies.append(copy)
    for copy in copies:
        copy.wait()


def weight_grads(order, lefts, rights, rows):
    micro, tok, width = lefts[0].shape
    cols = rights[0].shape[2]
    taken = order.shape[0] * rows
    return pl.pallas_call(
        functools.partial(weight_grads_body, (rows, micro, tok)),
        out_shape=[pltpu.HBM((3, n, cols), BF) for n in (rows, taken // 2 - rows, taken // 2)],
        in_specs=[pl.BlockSpec(memory_space=pltpu.SMEM)]
        + [spec_any()] * 3 + [spec_vmem()] * 4 + [spec_any()],
        out_specs=[spec_any()] * 3,
        scratch_shapes=[
            pltpu.VMEM((width, micro * tok), BF), pltpu.VMEM((taken, micro * tok), BF),
            pltpu.VMEM((3, taken, cols), BF), pltpu.VMEM((3, micro, tok, width), BF),
            pltpu.VMEM((micro, tok, cols), BF),
            pltpu.SemaphoreType.DMA((4,)), pltpu.SemaphoreType.DMA((3, 3)),
        ],
        compiler_params=pltpu.CompilerParams(vmem_limit_bytes=34 << 20),
        cost_estimate=pl.CostEstimate(
            flops=6 * micro * tok * taken * cols, bytes_accessed=12 * taken * cols, transcendentals=0
        ),
        name="weight_grads",
    )(
        order, *[in_hbm(v) for v in lefts[:3]], resident(lefts[3]),
        *[resident(v) for v in rights[:3]], in_hbm(rights[3]),
    )


def forward_call(heads, slides, shrink, scal, ids, gain, fgain, head_w, known, label, x0, received, lm, weights, bufs):
    micro, tok, width = x0.shape
    ff = weights[2].shape[1]
    rows = known.shape[1]
    shapes = [
        ((tok, width), BF), ((tok, 3 * width), BF), ((heads, tok), F32), ((tok, width), BF),
        ((tok, width), F32), ((tok, ff), F32), ((tok, ff), BF), ((tok, width), BF), ((tok, width), BF),
        ((tok, width), F32), ((rows, width), BF), ((rows, LANES), BF), ((8, width), F32),
    ]
    fresh = bufs is None
    given = [] if fresh else list(bufs)
    vm = lambda index: pltpu.VMEM(*shapes[index])
    n_in = 18
    out = pl.pallas_call(
        functools.partial(forward_body, heads, slides, shrink, fresh),
        out_shape=[pltpu.VMEM((tok, width), BF)]
        + [pltpu.HBM((micro,) + s, d) for s, d in shapes],
        in_specs=[pl.BlockSpec(memory_space=pltpu.SMEM)]
        + [spec_vmem()] * 17
        + [spec_any()] * len(given),
        out_specs=[spec_vmem()] + [spec_any()] * len(shapes),
        input_output_aliases={n_in + i: 1 + i for i in range(len(given))},
        scratch_shapes=[
            vm(0), vm(1), vm(2), vm(3), vm(4), vm(5), vm(6), vm(7), vm(8),
            pltpu.VMEM((tok, width), F32),
            pltpu.VMEM((width, tok), BF), pltpu.VMEM((width, tok), BF), pltpu.VMEM((width, tok), F32),
            pltpu.VMEM((rows, width), F32), vm(10), vm(11), vm(12),
            pltpu.SemaphoreType.DMA((4,)), pltpu.SemaphoreType.DMA((9,)),
        ],
        compiler_params=pltpu.CompilerParams(vmem_limit_bytes=14 << 20),
        cost_estimate=pl.CostEstimate(flops=7 << 30, bytes_accessed=8 << 20, transcendentals=1 << 20),
        name="layer_forward",
    )(
        scal, ids, gain, fgain, head_w, known, label, resident(x0), received, resident(lm),
        *[resident(w) for w in weights], *[in_hbm(b) for b in given],
    )
    return out[0], out[1:]


def backward_call(heads, scal, ids, gain, received, records, lm, weights, bufs):
    x_b, qkv_b, lse_b, mid_b, gp_b, dl_b = records
    micro, tok, width = x_b.shape
    ff = weights[3].shape[1]
    shapes = [((tok, width), BF), ((tok, ff), BF), ((tok, width), BF), ((tok, 3 * width), BF), ((8, width), F32)]
    fresh = bufs is None
    given = [] if fresh else list(bufs)
    n_in = 15
    out = pl.pallas_call(
        functools.partial(backward_body, heads, fresh),
        out_shape=[pltpu.VMEM((tok, width), BF)]
        + [pltpu.VMEM((micro,) + s, d) for s, d in shapes],
        in_specs=[pl.BlockSpec(memory_space=pltpu.SMEM)] + [spec_vmem()] * 3 + [spec_any()]
        + [spec_vmem()] * 5 + [spec_any()] * 5 + [spec_vmem()] * len(given),
        out_specs=[spec_vmem()] * (1 + len(shapes)),
        input_output_aliases={n_in + i: 1 + i for i in range(len(given))},
        scratch_shapes=[
            pltpu.VMEM((tok, width), F32),
            pltpu.VMEM((tok, width), BF), pltpu.VMEM((tok, 3 * width), BF), pltpu.VMEM((heads, tok), F32),
            pltpu.VMEM((tok, width), F32), pltpu.VMEM((tok, ff), F32),
        ]
        + [
            pltpu.VMEM((tok, width), F32),
            pltpu.VMEM((width, tok), BF), pltpu.VMEM((width, tok), BF),
            pltpu.VMEM((tok, width), BF), pltpu.VMEM((width, tok), BF), pltpu.VMEM((width, tok), F32),
            pltpu.VMEM((tok, 8 * tok), BF), pltpu.VMEM((tok, 8 * tok), BF),
            pltpu.SemaphoreType.DMA((6,)),
        ],
        compiler_params=pltpu.CompilerParams(vmem_limit_bytes=14 << 20),
        cost_estimate=pl.CostEstimate(flops=10 << 30, bytes_accessed=8 << 20, transcendentals=1 << 20),
        name="layer_backward",
    )(
        scal, ids, gain, received, in_hbm(dl_b), resident(lm), *[resident(w) for w in weights],
        *[in_hbm(b) for b in (x_b, qkv_b, lse_b, mid_b, gp_b)], *[resident(b) for b in given],
    )
    return out[0], out[1:]


def forward_body(heads, slides, shrink, fresh, *refs):
    forward_kernel(heads, slides, shrink, *refs[:18], fresh, *refs[18:])


def backward_body(heads, fresh, *refs):
    backward_kernel(heads, *refs[:15], fresh, *refs[15:])


def adam(weight, grad, first, second, rate, decay):
    first = BETA_ONE * first + (1.0 - BETA_ONE) * grad
    second = BETA_TWO * second + (1.0 - BETA_TWO) * grad * grad
    mhat = first / (1.0 - BETA_ONE**STEP)
    vhat = second / (1.0 - BETA_TWO**STEP)
    return (first, second, weight - rate * (mhat / (jnp.sqrt(vhat) + ADAM_EPS) + decay * weight))


def per_device(
    tiles,
    slide_ids,
    coords,
    known,
    labels,
    mats,
    mats_m,
    mats_v,
    gains,
    gains_m,
    gains_v,
    final_gain,
    fgain_m,
    fgain_v,
    w_in,
    win_m,
    win_v,
    head,
    head_m,
    head_v,
):
    sections = lax.axis_size("section")
    dp = lax.axis_size("dp")
    section = lax.axis_index("section")
    dp_index = lax.axis_index("dp")
    near = dp // 2
    side_of, place = dp_index // near, dp_index % near
    row_of, core = section // 2, section % 2
    stage = 2 * row_of + (side_of ^ row_of)
    micro, tok = slide_ids.shape
    heads = HEADS
    slides, genes = known.shape[1:]
    width = w_in.shape[1]
    rows, wide_cols = mats.shape[2:]
    direct = dp == 8 and sections == 4 and rows % 32 == 0

    def join(side, place, row, core):
        return side * near + place, row * 2 + core

    def layer_turn(d, s):
        side, at, row, c = d // near, d % near, s // 2, s % 2
        target = join(c ^ row, at, row, side ^ row)
        return None if target == (d, s) else target

    def pack_turn(d, s):
        side, at, row, c = d // near, d % near, s // 2, s % 2
        target = join(c, at, row, side)
        return None if target == (d, s) else target

    own_layer = side_of == (core ^ row_of)
    own_packs = side_of == core

    def slot(flip_c, flip_m):
        return (core ^ flip_c ^ row_of) * near + (place ^ flip_m)

    groups = [
        [
            (side * near + m) * sections + row * 2 + (half ^ row)
            for half in range(2)
            for m in range(near)
        ]
        for side in range(2)
        for row in range(sections // 2)
    ]

    def to_next(distance):
        def route(d, s):
            side, at, row, c = d // near, d % near, s // 2, s % 2
            goal = 2 * row + (side ^ row) + distance
            if not 0 <= goal < sections:
                return None
            return join((goal % 2) ^ (goal // 2), at, goal // 2, c)

        return route

    def some(route, kind):
        def limited(d, s):
            own = d // near == ((s % 2) ^ (s // 2))
            target = route(d, s)
            return target if kind is None or own == kind else None

        return limited

    def gather_all(low, early, late):
        if not direct:
            own = jnp.where(own_layer, low, moved(low, layer_turn))
            full = lax.all_gather(
                own, ("dp", "section"), axis=1, tiled=True, axis_index_groups=groups
            )
            table = early(())
            marks = late(table[0])
            return [full], ([(0, 0, None)], [(0, 0, None)]), jnp.zeros((2,), jnp.int32), table, marks
        half = rows // 2

        def routes(kind):
            return [some(f, kind) for f in (flip_dp(1), flip_dp(2), flip_section(1))]

        x_own, z_own, c_own = routes(True)
        x_got, z_got, c_got = routes(False)
        together = lax.optimization_barrier
        low = low.reshape(3, 2, half, wide_cols).transpose(1, 0, 2, 3)
        got, side, over = together(
            (moved(low, layer_turn), moved(low, x_own), moved(low, z_own))
        )
        table = early(())
        marks = late(got)
        side_got, over_got, far_low, far_high, sent, sent_got, table = together(
            (
                moved(got, x_got), moved(got, z_got), moved(over[0], x_own), moved(side[1], z_own),
                moved(low, c_own), moved(got, c_got), table,
            )
        )
        far_low_got, far_high_got, sent_side, sent_over, sent_low, sent_high, sent_side_got, sent_over_got = together(
            (
                moved(over_got[0], x_got), moved(side_got[1], z_got),
                moved(side, c_own), moved(over, c_own),
                moved(far_low, c_own), moved(far_high, c_own),
                moved(side_got, c_got), moved(over_got, c_got),
            )
        )
        mine_own = [low, side, over, far_low, far_high]
        sent_own = [sent, sent_side, sent_over, sent_low, sent_high]
        mine_got = [got, side_got, over_got, far_low_got, far_high_got]
        sent_got = [
            sent_got, sent_side_got, sent_over_got, moved(far_low_got, c_got), moved(far_high_got, c_got),
        ]
        pieces = mine_own + sent_own + mine_got + sent_got
        def listed(first, place):
            out = []
            for n in range(3):
                out += [(first + n, place + 2 * n + h, h) for h in range(2)]
            return out + [(first + 3 + h, place + 6 + h, None) for h in range(2)]

        plans = (listed(10, 0) + listed(5, 8), listed(0, 0) + listed(15, 8))
        starts = [
            slot(flip_c, m) * rows + start
            for flip_c in range(2)
            for m in range(4)
            for start in (0, half)
        ]
        place_at = jnp.stack([own_layer.astype(jnp.int32)] + starts).astype(jnp.int32)
        return pieces, plans, place_at, table, marks

    def scatter_all(lefts, rights):
        order = jnp.stack([slot(1 - k // 4, (k + 3) % 4) for k in range(8)]).astype(jnp.int32)
        if not direct:
            flat = lambda v: v.reshape((-1, v.shape[-1]))
            grads = [inner(flat(l), flat(r)).astype(BF) for l, r in zip(lefts, rights)]
            outs = []
            for grad in (grads[0], jnp.concatenate(grads[1:3], axis=1), grads[3]):
                own = lax.psum_scatter(
                    grad, ("dp", "section"), scatter_dimension=0, tiled=True, axis_index_groups=groups
                )
                outs.append((own, jnp.where(own_layer, own, moved(own, layer_turn)).astype(F32)))
            squares = sum(jnp.sum(jnp.square(own.astype(F32))) for own, _ in outs)
            mark = outs[0][0]
            held = beside_z(beside_x(beside_early(mark), mark), mark)
            return jnp.stack([outs[n][1] for n in (1, 0, 2)]), settled(*beside_last(held, mark), squares)
        half = rows // 2
        send_far, send_rest, kept = weight_grads(order, lefts, rights, rows)
        got_far = moved(send_far, flip_section(1))
        got_rest = moved(after(send_rest, got_far), flip_section(1))
        kept = kept.reshape(3, 4, rows, wide_cols)
        got_rest = got_rest.reshape(3, 3, rows, wide_cols)

        def both(m, cut=slice(None)):
            other = got_far[:, cut] if m == 0 else got_rest[:, m - 1, cut]
            return kept[:, m, cut].astype(F32) + other.astype(F32)

        far_low, far_high = lax.optimization_barrier(
            (both(0, slice(0, half)).astype(BF), both(0, slice(half, rows)).astype(BF))
        )
        first = beside_early(far_low)
        from_side, from_over = moved(far_low, flip_dp(1)), moved(far_high, flip_dp(2))
        from_side, from_over = lax.optimization_barrier((from_side, from_over))
        low_rows = ((0, 0), (0, rows - half), (0, 0))
        high_rows = ((0, 0), (half, 0), (0, 0))
        side = both(2) + jnp.pad(from_over, high_rows).astype(F32)
        over = both(3) + jnp.pad(from_side, low_rows).astype(F32)
        side, over = lax.optimization_barrier((side.astype(BF), over.astype(BF)))

        def totalled(kind, mark):
            one, two = lax.optimization_barrier(
                (moved(side, some(flip_dp(1), kind)), moved(over, some(flip_dp(2), kind)), mark)
            )[:2]
            return after((both(1) + one.astype(F32) + two.astype(F32)).astype(BF))

        second = beside_x(first, side)
        third = beside_z(second, side)
        total_far = totalled(False, third)
        away = moved(total_far, layer_turn)
        side, over = lax.optimization_barrier((side, over, total_far))[:2]
        total_own = totalled(True, ())
        small, piece = beside_last(third, total_own)
        squares = jnp.where(
            own_layer,
            jnp.sum(jnp.square(total_own.astype(F32))),
            jnp.sum(jnp.square(total_far.astype(F32))),
        )
        ends = settled(small, piece, squares)
        away, ends = lax.optimization_barrier((away, ends))
        return jnp.where(own_layer, total_own, away).astype(F32), ends

    def over_section(block):
        other_row = moved(block, flip_section(3))
        pair = jnp.stack([block, other_row])
        other_core = moved(pair, flip_section(1))
        whole = jnp.zeros((sections,) + block.shape, block.dtype)
        for part, flip in ((block, 0), (other_row, 3), (other_core[0], 1), (other_core[1], 2)):
            whole = lax.dynamic_update_slice(
                whole, part[None], (section ^ flip,) + (0,) * block.ndim
            )
        return whole.reshape((sections * block.shape[0],) + block.shape[1:])

    slots = micro * dp * slides * genes
    shrink = 0.5 ** (slots - 1).bit_length()
    def to_first(d, s):
        return (d - near, s) if d >= near and s < 2 else None

    def to_home(d, s):
        return (d + near, s) if d < near and s < 2 else None

    in_rows = w_in.shape[0]

    def embedded(mark):
        own_part, in_rows = final_gain.shape[0], w_in.shape[0]
        gain_high = final_gain.astype(BF)
        gain_low = (final_gain - gain_high.astype(F32)).astype(BF)
        own_ends = jnp.concatenate([head.astype(BF), gain_high[:, None], gain_low[:, None]], axis=1)
        own_ends = jnp.pad(own_ends, ((0, 0), (0, LANES - genes - 2)))
        extra = own_part * LANES // width
        packed = over_section(
            after(jnp.concatenate([w_in.astype(BF), own_ends.reshape(extra, width)])[None], mark)
        )
        in_low = packed[:, :in_rows].reshape(sections * in_rows, width)
        head_p = packed[:, in_rows:].reshape(sections * own_part, LANES)
        full_fgain = (head_p[:, genes].astype(F32) + head_p[:, genes + 1].astype(F32))[None, :]
        table = jax.vmap(lambda c: position_table(c, width), in_axes=1)(after(coords, mark))
        x0 = (
            jnp.dot(tiles.reshape(micro * tok, -1), in_low, preferred_element_type=F32).reshape(
                micro, tok, width
            )
            + table
        ).astype(BF)

        return x0, head_p, full_fgain

    cuts = (((0, 3 * width), (3 * width, wide_cols)), ((0, wide_cols),), ((0, wide_cols),))
    half_packs = micro // 2

    def mine_of(value):
        return lax.dynamic_slice_in_dim(value, core * half_packs, half_packs, 0)

    def exchanged(x0):
        first, known_in, labels_in = lax.optimization_barrier((slide_ids, known, labels, x0))[:3]
        home = mine_of(
            jnp.concatenate(
                [first, known_in.reshape(micro, -1), labels_in.reshape(micro, -1)], axis=1
            )
        )
        other = moved(home, flip_dp(near))
        lower = side_of == 0
        home = jnp.concatenate([jnp.where(lower, home, other), jnp.where(lower, other, home)])
        gain = jnp.where(own_layer, gains[0], moved(gains[0], flip_section(1)))
        return home, gain

    pieces, plans, place_at, (x0, head_p, full_fgain), (home, gain) = gather_all(
        mats[0].astype(BF), embedded, exchanged
    )
    near_packs = mine_of(x0)
    far_packs = moved(near_packs, to_first)
    x0_near = jnp.concatenate([near_packs, near_packs])
    ids = home[:, :tok]
    marks = home[:, tok:].reshape(micro, 2, slides, genes).astype(F32)
    pad = ((0, 0), (0, 16 - slides), (0, LANES - genes))
    known_p = jnp.pad(marks[:, 0], pad)
    labels_p = jnp.pad(marks[:, 1], pad)
    x0_near, lm, ids, gain, pieces, full_fgain, head_p, known_p, labels_p = lax.optimization_barrier(
        (x0_near, log_mult(heads, tok), ids, gain, pieces, full_fgain, head_p, known_p, labels_p)
    )
    wqkv, wo, w1, w2, wqkv_t, wo_t, w1_t, w2_t = load_weights(pieces, plans, place_at, cuts, width)
    ticks = micro + 2 * (sections - 1)
    late = 2 * (sections - 1)
    def scalars(index):
        valid = (index >= 0) & (index < micro)
        return jnp.stack(
            [valid, jnp.clip(index, 0, micro - 1), stage == 0, stage == sections - 1]
        ).astype(jnp.int32)

    arrived = [jnp.zeros((tok, width), BF)] * 2
    bufs = None
    for tick in range(ticks):
        if tick == half_packs:
            x0_near = jnp.concatenate([near_packs, after(far_packs, send)])
        end_args = (full_fgain, head_p, known_p, labels_p)
        send, bufs = forward_call(
            heads, slides, shrink, scalars(tick - 2 * stage), ids, gain, *end_args, x0_near, arrived[tick], lm,
            (wqkv, wo, w1, w2_t, wqkv_t, wo_t, w1_t, w2), bufs,
        )
        arrived.append(moved(send, to_next(1)) if tick + 2 < ticks else None)
    (x_b, qkv_b, lse_b, att_b, mid_b, gp_b, hid_b, a_b, b_b, dl_b, nl_b, dlog_b, side_b) = bufs
    records = (x_b, qkv_b, lse_b, mid_b, gp_b, dl_b)
    arrived = [jnp.zeros((tok, width), BF)] * 2
    bufs = None
    sends = []
    for tick in range(ticks):
        send, bufs = backward_call(
            heads, scalars(tick - 2 * (sections - 1 - stage)), ids, gain, arrived[tick], records,
            lm, (wqkv_t, wo_t, w1_t, w2), bufs,
        )
        sends.append(send)
        arrived.append(moved(send, to_next(-1)) if tick + 2 < ticks else None)
    dbr_b, dup_b, dat_b, dqkv_b, gg_b = bufs
    nl_b, dlog_b, side_b = lax.optimization_barrier((nl_b, dlog_b, side_b, sends[-1]))[:3]
    flat = lambda v: v.reshape((-1, v.shape[-1]))
    bits = [1 << k for k in range(dp.bit_length() - 1)]
    on_last = stage == sections - 1

    def halved(piece, bit):
        size = piece.shape[0] // 2
        up = (dp_index // bit) % 2
        keep = lax.dynamic_slice_in_dim(piece, up * size, size, 0)
        away = lax.dynamic_slice_in_dim(piece, (1 - up) * size, size, 0)
        return (keep.astype(F32) + moved(away, flip_dp(bit)).astype(F32)).astype(BF)

    d_near = jnp.stack(sends[late : late + half_packs])
    d_far = jnp.stack([moved(send, to_home) for send in sends[late + half_packs :]])
    d_rows = jnp.where(stage == 0, d_near, jnp.where(row_of == 0, d_far, jnp.zeros((), BF)))

    def beside_early(mark):
        rows_in = after(d_rows, mark)
        rows_in = rows_in + moved(rows_in, lambda d, s: (d, s ^ 2) if s < 2 else None)
        other = moved(rows_in, flip_section(1))
        rows_in = jnp.concatenate(
            [jnp.where(core == 0, rows_in, other), jnp.where(core == 0, other, rows_in)]
        )
        mine = lax.dynamic_slice_in_dim(flat(tiles), section * in_rows, in_rows, 1)
        piece = inner(mine, flat(rows_in)).astype(BF)
        grad_head = jnp.where(on_last, inner(flat(nl_b), flat(dlog_b)), 0.0)[:, :genes]
        side = jnp.where(on_last, jnp.sum(side_b, 0), 0.0)
        seen = jnp.pad(jnp.sum(marks[:, 0]).reshape(1), (0, LANES - 1))
        small = jnp.concatenate(
            [jnp.sum(gg_b, 0)[:2].reshape(-1), seen, side[0], grad_head.reshape(-1), side[1, :LANES]]
        )
        return small + moved(small, flip_section(1)), piece

    def folded(held, bit, mark):
        small, piece = lax.optimization_barrier((*held, mark))[:2]
        return small + moved(small, flip_dp(bit)), halved(piece, bit)

    def beside_x(held, mark):
        return folded(held, bits[0], mark)

    def beside_z(held, mark):
        for bit in bits[1:-1]:
            held = folded(held, bit, mark)
        return held

    def beside_last(held, mark):
        small, piece = lax.optimization_barrier((*held, mark))[:2]
        return small, (piece.astype(F32) + moved(piece, flip_dp(bits[-1])).astype(F32)).astype(BF)

    n_gain = 2 * width
    lead = (place == 0) & (core == 0)

    def settled(small, piece, squares):
        layer_gain, ends = small[:n_gain].reshape(2, width), small[n_gain + LANES :]
        count = jnp.maximum(small[n_gain], 1.0)
        own_ends = jnp.where(on_last, ends, 0.0)
        squares = (
            squares
            + 0.5 * jnp.sum(jnp.square(piece.astype(F32)))
            + jnp.where(lead, jnp.sum(layer_gain * layer_gain), 0.0)
            + jnp.where(lead, jnp.sum(own_ends[: width + width * genes] ** 2), 0.0)
        )
        sum_gain = jnp.where(own_layer, layer_gain, moved(layer_gain, flip_dp(near)))
        ends = own_ends + moved(own_ends, flip_section(2))
        ends = ends + moved(ends, flip_dp(near))
        sum_fgain = ends[:width]
        sum_head = ends[width : width + width * genes].reshape(width, genes)
        loss_sum = jnp.sum(ends[width + width * genes :])
        part = width // sections
        part_head = lax.dynamic_slice_in_dim(sum_head, section * part, part, 0)
        part_fgain = lax.dynamic_slice_in_dim(sum_fgain, section * part, part, 0)
        return squares.reshape(1, 1), piece, count, loss_sum, sum_gain, part_head, part_fgain

    shards, (squares, piece, count, loss_sum, sum_gain, part_head, part_fgain) = scatter_all(
        (b_b, a_b, att_b, dbr_b), (dup_b, dqkv_b, dat_b, hid_b)
    )
    total_sq = spread_sum(squares)
    part_in = after(piece, total_sq)
    for bit in reversed(bits[:-1]):
        up = (dp_index // bit) % 2 == 1
        other = moved(part_in, flip_dp(bit))
        part_in = jnp.concatenate([jnp.where(up, other, part_in), jnp.where(up, part_in, other)])
    part_in = part_in.astype(F32)
    total_sq = total_sq[0, 0]
    shard_wide = shards[None]
    grow = 1.0 / (shrink * count)
    grad_norm = jnp.sqrt(total_sq) * grow
    factor = CLIP / jnp.maximum(grad_norm, CLIP) * grow
    mats_out = adam(mats, shard_wide * factor, mats_m, mats_v, RATE, DECAY)
    gains_out = adam(gains, sum_gain[None] * factor, gains_m, gains_v, RATE_GAIN, 0.0)
    fgain_out = adam(final_gain, part_fgain * factor, fgain_m, fgain_v, RATE_GAIN, 0.0)
    in_out = adam(w_in, part_in * factor, win_m, win_v, RATE, DECAY)
    head_out = adam(head, part_head * factor, head_m, head_v, RATE, DECAY)
    return (
        grad_norm,
        loss_sum,
        count,
        mats_out[0],
        mats_out[1],
        mats_out[2],
        gains_out[0],
        gains_out[1],
        gains_out[2],
        fgain_out[0],
        fgain_out[1],
        fgain_out[2],
        in_out[0],
        in_out[1],
        in_out[2],
        head_out[0],
        head_out[1],
        head_out[2],
    )


def solution(mesh):
    placed = (
        P("dp", None, None),
        P("dp", None),
        P(None, "dp", None),
        P("dp", None, None),
        P("dp", None, None),
        P("section", None, "dp", None),
        P("section", None, "dp", None),
        P("section", None, "dp", None),
        P("section", None, None),
        P("section", None, None),
        P("section", None, None),
        P("section"),
        P("section"),
        P("section"),
        P("section", None),
        P("section", None),
        P("section", None),
        P("section", None),
        P("section", None),
        P("section", None),
    )
    return jax.shard_map(
        per_device,
        mesh=mesh,
        in_specs=placed,
        out_specs=(
            P(),
            P(),
            P(),
            P("section", None, "dp", None),
            P("section", None, "dp", None),
            P("section", None, "dp", None),
            P("section", None, None),
            P("section", None, None),
            P("section", None, None),
            P("section"),
            P("section"),
            P("section"),
            P("section", None),
            P("section", None),
            P("section", None),
            P("section", None),
            P("section", None),
            P("section", None),
        ),
        check_vma=False,
    )
```

```python
import functools

import jax
import jax.numpy as jnp
from jax import lax
from jax.experimental import pallas as pl
from jax.experimental.pallas import tpu as pltpu
from jax.sharding import PartitionSpec as P

HEADS = 16
STEP = 10


EPS_NORM = 1e-05
CLIP = 0.05
BETA_ONE = 0.9
BETA_TWO = 0.95
ADAM_EPS = 1e-08
RATE = 0.06
RATE_GAIN = 1.0
DECAY = 0.1
RATIOS = (1, 2, 4, 8, 16)

def moved(block, route):
    dp, sections = lax.axis_size("dp"), lax.axis_size("section")
    pairs = []
    for d in range(dp):
        for s in range(sections):
            target = route(d, s)
            if target is not None:
                pairs.append((d * sections + s, target[0] * sections + target[1]))
    return lax.ppermute(block, ("dp", "section"), pairs)


def flip_dp(bit):
    return lambda d, s: (d ^ bit, s)


def flip_section(bit):
    return lambda d, s: (d, s ^ bit)


def spread_sum(value):
    dp, sections = lax.axis_size("dp"), lax.axis_size("section")
    for k in range(sections.bit_length() - 1):
        value = value + moved(value, flip_section(1 << k))
    for k in range(dp.bit_length() - 1):
        value = value + moved(value, flip_dp(1 << k))
    return value


def inner(left, right):
    return lax.dot_general(
        left, right, (((0,), (0,)), ((), ())), preferred_element_type=jnp.float32
    )


def position_table(coord, width):
    quarter = width // 4
    freq = jnp.exp(-jnp.log(10000.0) * jnp.arange(quarter, dtype=jnp.float32) / quarter)
    along = coord[0].astype(jnp.float32)[:, None] * freq
    across = coord[1].astype(jnp.float32)[:, None] * freq
    return jnp.concatenate(
        [jnp.sin(along), jnp.cos(along), jnp.sin(across), jnp.cos(across)], axis=1
    )


def log_mult(heads, tok):
    place = jnp.arange(tok, dtype=jnp.int32)
    head_idx = jnp.arange(heads, dtype=jnp.int32)
    mult = jnp.zeros((heads, tok, tok), jnp.float32)
    for ratio in RATIOS:
        hit = (place[None, :] % ratio == head_idx[:, None] % ratio).astype(jnp.float32)
        mult = mult + hit[:, :, None] * hit[:, None, :]
    return jnp.log(mult)


NN = (((1,), (0,)), ((), ()))
NT = (((1,), (1,)), ((), ()))
TN = (((0,), (0,)), ((), ()))
LANES = 128
BF = jnp.bfloat16
F32 = jnp.float32


def mm(left, right, dims=NN):
    return lax.dot_general(left, right, dims, preferred_element_type=F32)


def norm_parts(value):
    mean = jnp.mean(value, -1, keepdims=True)
    centred = value - mean
    var = jnp.mean(centred * centred, -1, keepdims=True)
    inv = lax.rsqrt(var + EPS_NORM)
    return centred * inv, inv


def norm_back(dvalue, gain, hat, inv):
    dhat = dvalue * gain
    return inv * (
        dhat
        - jnp.mean(dhat, -1, keepdims=True)
        - hat * jnp.mean(dhat * hat, -1, keepdims=True)
    )


def window(head, size):
    low = head * size // LANES * LANES
    high = -(-(head + 1) * size // LANES) * LANES
    return low, high


def placed_rows(ref, head, size):
    low, high = window(head, size)
    before, after = head * size - low, high - (head + 1) * size
    tok = ref.shape[1]
    parts = [ref[head * size : (head + 1) * size, :]]
    if before:
        parts = [jnp.zeros((before, tok), ref.dtype)] + parts
    if after:
        parts = parts + [jnp.zeros((after, tok), ref.dtype)]
    return jnp.concatenate(parts, axis=0) if len(parts) > 1 else parts[0]


def same_slide(ids_ref, pick):
    tok = ids_ref.shape[1]
    row = jnp.broadcast_to(ids_ref[pl.ds(pick, 1), :].astype(F32), (tok, tok))
    return row, row.T


def forward_kernel(
    heads, slides, shrink, scal, ids, gain, fgain, head_w, known, label,
    x0, rc, lm_v, wqkv, wo, w1, w2t, wqkv_t, wo_t, w1_t, w2, *rest
):
    fresh = rest[0]
    n_buf = 13
    rest = rest[1:] if fresh else rest[1 + n_buf :]
    send_h = rest[0]
    (x_b, qkv_b, lse_b, att_b, mid_b, gp_b, hid_b, a_b, b_b, dl_b, nl_b, dlog_b, side_b) = rest[1 : 1 + n_buf]
    (x_v, qkv_v, lse_v, att_v, mid_v, gp_v, hid_v, a_v, b_v, o_v,
     q_t, v_t, o_t, pool_v, nl_v, dlog_v, side_v, sin, sout) = rest[1 + n_buf :]
    valid, pick, first, last = scal[0], scal[1], scal[2], scal[3]
    tok, width = x_v.shape
    size = width // heads
    scale = size ** (-0.5)

    @pl.when(valid == 1)
    def _():
        @pl.when(first == 1)
        def _():
            x_v[...] = x0[pick]

        @pl.when(first != 1)
        def _():
            x_v[...] = rc[...]

        outs = []

        def emit(src, dst):
            c = pltpu.make_async_copy(src, dst, sout.at[len(outs)])
            c.start()
            outs.append(c)

        row, col = same_slide(ids, pick)
        same = row == col

        emit(x_v, x_b.at[pick])
        x = x_v[...].astype(F32)
        hat, _ = norm_parts(x)
        a_v[...] = (hat * gain[0:1, :]).astype(BF)
        emit(a_v, a_b.at[pick])
        qkv_v[...] = mm(a_v[...], wqkv[...]).astype(BF)
        emit(qkv_v, qkv_b.at[pick])
        q_t[...] = qkv_v[:, :width].T
        v_t[...] = qkv_v[:, 2 * width :].T
        for h in range(heads):
            low, high = window(h, size)
            s = mm(qkv_v[:, width + low : width + high], placed_rows(q_t, h, size)) * scale
            s = s + jnp.where(same, lm_v[h], -1000000000.0)
            top = jnp.max(s, 0, keepdims=True)
            e = jnp.exp(s - top)
            total = jnp.sum(e, 0, keepdims=True)
            lse_v[h : h + 1, :] = top + jnp.log(total)
            o = mm(v_t[h * size : (h + 1) * size, :], e.astype(BF))
            o_t[h * size : (h + 1) * size, :] = o * (1.0 / total)
        att_v[...] = o_t[...].T.astype(BF)
        emit(lse_v, lse_b.at[pick])
        emit(att_v, att_b.at[pick])
        middle = x + mm(att_v[...], wo[...])
        mid_v[...] = middle
        emit(mid_v, mid_b.at[pick])
        hat, _ = norm_parts(middle)
        b_v[...] = (hat * gain[1:2, :]).astype(BF)
        emit(b_v, b_b.at[pick])
        ff = w1.shape[1]
        part = ff // 4
        for j in range(4):
            cols = slice(j * part, (j + 1) * part)
            up = mm(b_v[...], w1[:, cols])
            square = up * up
            sig = 1.0 / (1.0 + jnp.exp(up * (-1.5957691216057308 - 0.07135481627159852 * square)))
            act = up * sig
            hid_v[:, cols] = act.astype(BF)
            slope = 1.5957691216057308 + 0.21406444881478 * square
            gp_v[:, cols] = sig + act * (1.0 - sig) * slope
        emit(gp_v, gp_b.at[pick])
        emit(hid_v, hid_b.at[pick])
        out = mid_v[...] + mm(hid_v[...], w2t[...])
        send_h[...] = out.astype(BF)

        @pl.when(last == 1)
        def _():
            o_v[...] = out
            pool_v[...] = jnp.zeros_like(pool_v)
            inverse = []
            for s in range(slides):
                inside = (col == float(s)).astype(F32)
                inverse.append(1.0 / jnp.sum(inside, 0, keepdims=True))
                parts = []
                for j in range(width // LANES):
                    parts.append(
                        jnp.sum(o_v[:, j * LANES : (j + 1) * LANES] * inside, 0, keepdims=True) * inverse[s]
                    )
                pool_v[s : s + 1, :] = jnp.concatenate(parts, axis=1)
            hat, inv = norm_parts(pool_v[...])
            low_n = (hat * fgain[...]).astype(BF)
            nl_v[...] = low_n
            logits = mm(low_n, head_w[...])
            kn = known[pick]
            lb = label[pick]
            tail = jnp.exp(-jnp.abs(logits))
            soft = jnp.maximum(logits, 0.0) + jnp.log(1.0 + tail)
            terms = kn * (soft - lb * logits)
            gate = jnp.where(logits >= 0.0, 1.0, tail) / (1.0 + tail)
            dlog = (kn * (gate - lb) * shrink).astype(BF)
            dlog_v[...] = dlog
            d_n = mm(dlog, head_w[...], NT)
            side_v[...] = jnp.zeros_like(side_v)
            side_v[0:1, :] = jnp.sum(d_n * hat, 0, keepdims=True)
            side_v[1:2, 0:LANES] = jnp.sum(terms, 0, keepdims=True)
            d_pool = norm_back(d_n, fgain[...], hat, inv)
            pool_v[...] = d_pool
            for j in range(width // LANES):
                lanes = slice(j * LANES, (j + 1) * LANES)
                acc = jnp.zeros((tok, LANES), F32)
                for s in range(slides):
                    acc = acc + jnp.where(col == float(s), pool_v[s : s + 1, lanes] * inverse[s], 0.0)
                o_v[:, lanes] = acc
            tails = [
                pltpu.make_async_copy(o_v, dl_b.at[pick], sin.at[0]),
                pltpu.make_async_copy(nl_v, nl_b.at[pick], sin.at[1]),
                pltpu.make_async_copy(dlog_v, dlog_b.at[pick], sin.at[2]),
                pltpu.make_async_copy(side_v, side_b.at[pick], sin.at[3]),
            ]
            for c in tails:
                c.start()
            for c in tails:
                c.wait()

        for c in outs:
            c.wait()


def backward_kernel(
    heads, scal, ids, gain, rc_v, dl_b, lm_v, wqkv_t, wo_t, w1_t, w2,
    x_b, qkv_b, lse_b, mid_b, gp_b, *rest
):
    fresh = rest[0]
    n_buf = 5
    rest = rest[1:] if fresh else rest[1 + n_buf :]
    send_h = rest[0]
    outs = rest[1 : 1 + n_buf]
    (dl_v, x_v, qkv_v, lse_v, mid_v, gp_v, dm_v, q_t, k_t, do_v, do_t, dq_t, p_v, ds_v, sin) = rest[1 + n_buf :]
    valid, pick, last = scal[0], scal[1], scal[3]
    dbr_v, dup_v, dat_v, dqkv_v, gg_v = [ref.at[pick] for ref in outs]
    tok, width = x_v.shape
    size = width // heads
    scale = size ** (-0.5)
    per = 8

    @pl.when(valid == 1)
    def _():
        from_head = pltpu.make_async_copy(dl_b.at[pick], dl_v, sin.at[0])

        @pl.when(last == 1)
        def _():
            from_head.start()

        loads = [
            pltpu.make_async_copy(gp_b.at[pick], gp_v, sin.at[1]),
            pltpu.make_async_copy(mid_b.at[pick], mid_v, sin.at[2]),
            pltpu.make_async_copy(qkv_b.at[pick], qkv_v, sin.at[3]),
            pltpu.make_async_copy(lse_b.at[pick], lse_v, sin.at[4]),
            pltpu.make_async_copy(x_b.at[pick], x_v, sin.at[5]),
        ]
        for c in loads:
            c.start()
        row, col = same_slide(ids, pick)
        same = row == col

        @pl.when(last == 1)
        def _():
            from_head.wait()

        @pl.when(last != 1)
        def _():
            dl_v[...] = rc_v[...].astype(F32)

        dbr_v[...] = dl_v[...].astype(BF)
        loads[0].wait()
        ff = w2.shape[1]
        part = ff // 4
        for j in range(4):
            cols = slice(j * part, (j + 1) * part)
            dup_v[:, cols] = (mm(dbr_v[...], w2[:, cols]) * gp_v[:, cols]).astype(BF)
        d_b = mm(dup_v[...], w1_t[...])
        loads[1].wait()
        hat, inv = norm_parts(mid_v[...])
        gg_v[1:2, :] = jnp.sum(d_b * hat, 0, keepdims=True)
        d_mid = dl_v[...] + norm_back(d_b, gain[1:2, :], hat, inv)
        dm_v[...] = d_mid
        dat_v[...] = d_mid.astype(BF)
        loads[2].wait()
        q_t[...] = qkv_v[:, :width].T
        k_t[...] = qkv_v[:, width : 2 * width].T
        do_v[...] = mm(dat_v[...], wo_t[...]).astype(BF)
        do_t[...] = do_v[...].T
        loads[3].wait()
        lane = lax.broadcasted_iota(jnp.int32, (tok, LANES), 1)
        for group in range(heads // per):
            for i in range(per):
                h = group * per + i
                low, high = window(h, size)
                s = mm(qkv_v[:, width + low : width + high], placed_rows(q_t, h, size)) * scale
                s = s + jnp.where(same, lm_v[h], -1000000000.0)
                p = jnp.exp(s - lse_v[h : h + 1, :])
                dp = mm(qkv_v[:, 2 * width + low : 2 * width + high], placed_rows(do_t, h, size))
                inner_sum = jnp.sum(dp * p, 0, keepdims=True)
                ds = (p * (dp - inner_sum)).astype(BF)
                p_v[:, i * tok : (i + 1) * tok] = p.astype(BF)
                ds_v[:, i * tok : (i + 1) * tok] = ds
                dq_t[h * size : (h + 1) * size, :] = mm(k_t[h * size : (h + 1) * size, :], ds) * scale
            base = group * per * size
            for block in range(base // LANES, (base + per * size) // LANES):
                left = block * LANES
                inside = [
                    i for i in range(per)
                    if (group * per + i) * size < left + LANES and (group * per + i + 1) * size > left
                ]
                spans = slice(inside[0] * tok, (inside[-1] + 1) * tok)
                q_parts, o_parts = [], []
                for i in inside:
                    start = (group * per + i) * size - left
                    keep = (lane >= start) & (lane < start + size)
                    q_parts.append(jnp.where(keep, qkv_v[:, left : left + LANES], jnp.zeros((), BF)))
                    o_parts.append(jnp.where(keep, do_v[:, left : left + LANES], jnp.zeros((), BF)))
                dk = mm(ds_v[:, spans], jnp.concatenate(q_parts, axis=0)) * scale
                dv = mm(p_v[:, spans], jnp.concatenate(o_parts, axis=0))
                dqkv_v[:, width + left : width + left + LANES] = dk.astype(BF)
                dqkv_v[:, 2 * width + left : 2 * width + left + LANES] = dv.astype(BF)
        dqkv_v[:, :width] = dq_t[...].T.astype(BF)
        d_a = mm(dqkv_v[...], wqkv_t[...])
        loads[4].wait()
        hat, inv = norm_parts(x_v[...].astype(F32))
        gg_v[0:1, :] = jnp.sum(d_a * hat, 0, keepdims=True)
        send_h[...] = (dm_v[...] + norm_back(d_a, gain[0:1, :], hat, inv)).astype(BF)


def spec_any():
    return pl.BlockSpec(memory_space=pltpu.HBM)


def spec_vmem():
    return pl.BlockSpec(memory_space=pltpu.VMEM)


def resident(value):
    return pltpu.with_memory_space_constraint(value, pltpu.VMEM)


def in_hbm(value):
    return pltpu.with_memory_space_constraint(value, pltpu.HBM)


def after(value, *others):
    return lax.optimization_barrier((value, *others))[0]


def load_body(cuts, plans, scal, *refs):
    n_out = sum(len(c) for c in cuts)
    n_in = len(refs) - 2 * n_out - 1
    pieces, straight, turned, sems = (
        refs[:n_in], refs[n_in : n_in + n_out], refs[n_in + n_out : -1], refs[-1]
    )

    def copies_of(chunk, flag):
        base = sum(len(c) for c in cuts[:chunk])
        out = []
        for n, (piece, place, part) in enumerate(plans[flag]):
            src = pieces[piece] if part is None else pieces[piece].at[part]
            src = src.at[chunk]
            rows = pl.ds(pl.multiple_of(scal[1 + place], 16), src.shape[0])
            for j, (low, high) in enumerate(cuts[chunk]):
                out.append(
                    pltpu.make_async_copy(
                        src.at[:, low:high], straight[base + j].at[rows, :], sems.at[chunk, n, j]
                    )
                )
        return out

    for flag in range(2):

        @pl.when(scal[0] == flag)
        def _():
            for chunk in range(len(cuts)):
                for copy in copies_of(chunk, flag):
                    copy.start()

    base = 0
    for chunk, cut in enumerate(cuts):
        for flag in range(2):

            @pl.when(scal[0] == flag)
            def _():
                for copy in copies_of(chunk, flag):
                    copy.wait()

        for j in range(base, base + len(cut)):
            step = 256

            def turn(index, carry):
                here = pl.ds(pl.multiple_of(index * step, step), step)
                turned[j][:, here] = straight[j][here, :].T
                return carry

            lax.fori_loop(0, straight[j].shape[0] // step, turn, 0)
        base += len(cut)


def load_weights(pieces, plans, scal, cuts, rows):
    sizes = [high - low for cut in cuts for low, high in cut]
    most = max(len(plan) for plan in plans)
    return pl.pallas_call(
        functools.partial(load_body, cuts, plans),
        out_shape=[pltpu.VMEM((rows, n), BF) for n in sizes] + [pltpu.VMEM((n, rows), BF) for n in sizes],
        in_specs=[pl.BlockSpec(memory_space=pltpu.SMEM)]
        + [pl.BlockSpec(memory_space=pl.ANY)] * len(pieces),
        out_specs=[spec_vmem()] * (2 * len(sizes)),
        scratch_shapes=[pltpu.SemaphoreType.DMA((len(cuts), most, 2))],
        compiler_params=pltpu.CompilerParams(vmem_limit_bytes=8 << 20),
        name="load_weights",
    )(scal, *[in_hbm(piece) for piece in pieces])


def weight_grads_body(shape, order, *refs):
    rows, micro, tok = shape
    lefts, rights, outs = refs[:4], refs[4:8], refs[8:11]
    turned, ordered, grad, left_v, hid_v, sin, sout = refs[11:]
    loads = [pltpu.make_async_copy(lefts[n], left_v.at[n], sin.at[n]) for n in range(3)]
    wide = pltpu.make_async_copy(rights[3], hid_v, sin.at[3])
    for copy in loads:
        copy.start()
    wide.start()
    taken = ordered.shape[0]
    cuts = (slice(0, rows), slice(rows, taken // 2), slice(taken // 2, taken))
    step = 768
    copies = []
    attn_cols = rights[1].shape[2]
    for chunk, n, col in ((1, 0, 0), (0, 1, 0), (0, 2, attn_cols), (2, 3, 0)):
        if n < 3:
            loads[n].wait()
            left, right = left_v.at[n], rights[n]
        else:
            wide.wait()
            left, right = lefts[3], hid_v
        for p in range(micro):
            turned[:, p * tok : (p + 1) * tok] = left[p].T
        for k in range(taken // rows):
            here = pl.ds(pl.multiple_of(order[k] * rows, 16), rows)
            ordered[k * rows : (k + 1) * rows, :] = turned[here, :]
        for start in range(0, right.shape[2], step):
            block = right[:, :, start : start + step].reshape(micro * tok, step)
            for low in range(0, taken, taken // 2):
                grad[chunk, low : low + taken // 2, col + start : col + start + step] = mm(
                    ordered[low : low + taken // 2, :], block
                ).astype(BF)
        if n == 1:
            continue
        for m, cut in enumerate(cuts):
            copy = pltpu.make_async_copy(grad.at[chunk, cut], outs[m].at[chunk], sout.at[chunk, m])
            copy.start()
            copies.append(copy)
    for copy in copies:
        copy.wait()


def weight_grads(order, lefts, rights, rows):
    micro, tok, width = lefts[0].shape
    cols = rights[0].shape[2]
    taken = order.shape[0] * rows
    return pl.pallas_call(
        functools.partial(weight_grads_body, (rows, micro, tok)),
        out_shape=[pltpu.HBM((3, n, cols), BF) for n in (rows, taken // 2 - rows, taken // 2)],
        in_specs=[pl.BlockSpec(memory_space=pltpu.SMEM)]
        + [spec_any()] * 3 + [spec_vmem()] * 4 + [spec_any()],
        out_specs=[spec_any()] * 3,
        scratch_shapes=[
            pltpu.VMEM((width, micro * tok), BF), pltpu.VMEM((taken, micro * tok), BF),
            pltpu.VMEM((3, taken, cols), BF), pltpu.VMEM((3, micro, tok, width), BF),
            pltpu.VMEM((micro, tok, cols), BF),
            pltpu.SemaphoreType.DMA((4,)), pltpu.SemaphoreType.DMA((3, 3)),
        ],
        compiler_params=pltpu.CompilerParams(vmem_limit_bytes=34 << 20),
        cost_estimate=pl.CostEstimate(
            flops=6 * micro * tok * taken * cols, bytes_accessed=12 * taken * cols, transcendentals=0
        ),
        name="weight_grads",
    )(
        order, *[in_hbm(v) for v in lefts[:3]], resident(lefts[3]),
        *[resident(v) for v in rights[:3]], in_hbm(rights[3]),
    )


def forward_call(heads, slides, shrink, scal, ids, gain, fgain, head_w, known, label, x0, received, lm, weights, bufs):
    micro, tok, width = x0.shape
    ff = weights[2].shape[1]
    rows = known.shape[1]
    shapes = [
        ((tok, width), BF), ((tok, 3 * width), BF), ((heads, tok), F32), ((tok, width), BF),
        ((tok, width), F32), ((tok, ff), F32), ((tok, ff), BF), ((tok, width), BF), ((tok, width), BF),
        ((tok, width), F32), ((rows, width), BF), ((rows, LANES), BF), ((8, width), F32),
    ]
    fresh = bufs is None
    given = [] if fresh else list(bufs)
    vm = lambda index: pltpu.VMEM(*shapes[index])
    n_in = 18
    out = pl.pallas_call(
        functools.partial(forward_body, heads, slides, shrink, fresh),
        out_shape=[pltpu.VMEM((tok, width), BF)]
        + [pltpu.HBM((micro,) + s, d) for s, d in shapes],
        in_specs=[pl.BlockSpec(memory_space=pltpu.SMEM)]
        + [spec_vmem()] * 17
        + [spec_any()] * len(given),
        out_specs=[spec_vmem()] + [spec_any()] * len(shapes),
        input_output_aliases={n_in + i: 1 + i for i in range(len(given))},
        scratch_shapes=[
            vm(0), vm(1), vm(2), vm(3), vm(4), vm(5), vm(6), vm(7), vm(8),
            pltpu.VMEM((tok, width), F32),
            pltpu.VMEM((width, tok), BF), pltpu.VMEM((width, tok), BF), pltpu.VMEM((width, tok), F32),
            pltpu.VMEM((rows, width), F32), vm(10), vm(11), vm(12),
            pltpu.SemaphoreType.DMA((4,)), pltpu.SemaphoreType.DMA((9,)),
        ],
        compiler_params=pltpu.CompilerParams(vmem_limit_bytes=14 << 20),
        cost_estimate=pl.CostEstimate(flops=7 << 30, bytes_accessed=8 << 20, transcendentals=1 << 20),
        name="layer_forward",
    )(
        scal, ids, gain, fgain, head_w, known, label, resident(x0), received, resident(lm),
        *[resident(w) for w in weights], *[in_hbm(b) for b in given],
    )
    return out[0], out[1:]


def backward_call(heads, scal, ids, gain, received, records, lm, weights, bufs):
    x_b, qkv_b, lse_b, mid_b, gp_b, dl_b = records
    micro, tok, width = x_b.shape
    ff = weights[3].shape[1]
    shapes = [((tok, width), BF), ((tok, ff), BF), ((tok, width), BF), ((tok, 3 * width), BF), ((8, width), F32)]
    fresh = bufs is None
    given = [] if fresh else list(bufs)
    n_in = 15
    out = pl.pallas_call(
        functools.partial(backward_body, heads, fresh),
        out_shape=[pltpu.VMEM((tok, width), BF)]
        + [pltpu.VMEM((micro,) + s, d) for s, d in shapes],
        in_specs=[pl.BlockSpec(memory_space=pltpu.SMEM)] + [spec_vmem()] * 3 + [spec_any()]
        + [spec_vmem()] * 5 + [spec_any()] * 5 + [spec_vmem()] * len(given),
        out_specs=[spec_vmem()] * (1 + len(shapes)),
        input_output_aliases={n_in + i: 1 + i for i in range(len(given))},
        scratch_shapes=[
            pltpu.VMEM((tok, width), F32),
            pltpu.VMEM((tok, width), BF), pltpu.VMEM((tok, 3 * width), BF), pltpu.VMEM((heads, tok), F32),
            pltpu.VMEM((tok, width), F32), pltpu.VMEM((tok, ff), F32),
        ]
        + [
            pltpu.VMEM((tok, width), F32),
            pltpu.VMEM((width, tok), BF), pltpu.VMEM((width, tok), BF),
            pltpu.VMEM((tok, width), BF), pltpu.VMEM((width, tok), BF), pltpu.VMEM((width, tok), F32),
            pltpu.VMEM((tok, 8 * tok), BF), pltpu.VMEM((tok, 8 * tok), BF),
            pltpu.SemaphoreType.DMA((6,)),
        ],
        compiler_params=pltpu.CompilerParams(vmem_limit_bytes=14 << 20),
        cost_estimate=pl.CostEstimate(flops=10 << 30, bytes_accessed=8 << 20, transcendentals=1 << 20),
        name="layer_backward",
    )(
        scal, ids, gain, received, in_hbm(dl_b), resident(lm), *[resident(w) for w in weights],
        *[in_hbm(b) for b in (x_b, qkv_b, lse_b, mid_b, gp_b)], *[resident(b) for b in given],
    )
    return out[0], out[1:]


def forward_body(heads, slides, shrink, fresh, *refs):
    forward_kernel(heads, slides, shrink, *refs[:18], fresh, *refs[18:])


def backward_body(heads, fresh, *refs):
    backward_kernel(heads, *refs[:15], fresh, *refs[15:])


def adam(weight, grad, first, second, rate, decay):
    first = BETA_ONE * first + (1.0 - BETA_ONE) * grad
    second = BETA_TWO * second + (1.0 - BETA_TWO) * grad * grad
    mhat = first / (1.0 - BETA_ONE**STEP)
    vhat = second / (1.0 - BETA_TWO**STEP)
    return (first, second, weight - rate * (mhat / (jnp.sqrt(vhat) + ADAM_EPS) + decay * weight))


def per_device(
    tiles,
    slide_ids,
    coords,
    known,
    labels,
    mats,
    mats_m,
    mats_v,
    gains,
    gains_m,
    gains_v,
    final_gain,
    fgain_m,
    fgain_v,
    w_in,
    win_m,
    win_v,
    head,
    head_m,
    head_v,
):
    sections = lax.axis_size("section")
    dp = lax.axis_size("dp")
    section = lax.axis_index("section")
    dp_index = lax.axis_index("dp")
    near = dp // 2
    side_of, place = dp_index // near, dp_index % near
    row_of, core = section // 2, section % 2
    stage = 2 * row_of + (side_of ^ row_of)
    micro, tok = slide_ids.shape
    heads = HEADS
    slides, genes = known.shape[1:]
    width = w_in.shape[1]
    rows, wide_cols = mats.shape[2:]
    direct = dp == 8 and sections == 4 and rows % 32 == 0

    def join(side, place, row, core):
        return side * near + place, row * 2 + core

    def layer_turn(d, s):
        side, at, row, c = d // near, d % near, s // 2, s % 2
        target = join(c ^ row, at, row, side ^ row)
        return None if target == (d, s) else target

    def pack_turn(d, s):
        side, at, row, c = d // near, d % near, s // 2, s % 2
        target = join(c, at, row, side)
        return None if target == (d, s) else target

    own_layer = side_of == (core ^ row_of)
    own_packs = side_of == core

    def slot(flip_c, flip_m):
        return (core ^ flip_c ^ row_of) * near + (place ^ flip_m)

    groups = [
        [
            (side * near + m) * sections + row * 2 + (half ^ row)
            for half in range(2)
            for m in range(near)
        ]
        for side in range(2)
        for row in range(sections // 2)
    ]

    def to_next(distance):
        def route(d, s):
            side, at, row, c = d // near, d % near, s // 2, s % 2
            goal = 2 * row + (side ^ row) + distance
            if not 0 <= goal < sections:
                return None
            return join((goal % 2) ^ (goal // 2), at, goal // 2, c)

        return route

    def some(route, kind):
        def limited(d, s):
            own = d // near == ((s % 2) ^ (s // 2))
            target = route(d, s)
            return target if kind is None or own == kind else None

        return limited

    def gather_all(low, early, late):
        if not direct:
            own = jnp.where(own_layer, low, moved(low, layer_turn))
            full = lax.all_gather(
                own, ("dp", "section"), axis=1, tiled=True, axis_index_groups=groups
            )
            table = early(())
            marks = late(table[0])
            return [full], ([(0, 0, None)], [(0, 0, None)]), jnp.zeros((2,), jnp.int32), table, marks
        half = rows // 2

        def routes(kind):
            return [some(f, kind) for f in (flip_dp(1), flip_dp(2), flip_section(1))]

        x_own, z_own, c_own = routes(True)
        x_got, z_got, c_got = routes(False)
        together = lax.optimization_barrier
        low = low.reshape(3, 2, half, wide_cols).transpose(1, 0, 2, 3)
        got, side, over = together(
            (moved(low, layer_turn), moved(low, x_own), moved(low, z_own))
        )
        table = early(())
        marks = late(got)
        side_got, over_got, far_low, far_high, sent, sent_got, table = together(
            (
                moved(got, x_got), moved(got, z_got), moved(over[0], x_own), moved(side[1], z_own),
                moved(low, c_own), moved(got, c_got), table,
            )
        )
        far_low_got, far_high_got, sent_side, sent_over, sent_low, sent_high, sent_side_got, sent_over_got = together(
            (
                moved(over_got[0], x_got), moved(side_got[1], z_got),
                moved(side, c_own), moved(over, c_own),
                moved(far_low, c_own), moved(far_high, c_own),
                moved(side_got, c_got), moved(over_got, c_got),
            )
        )
        mine_own = [low, side, over, far_low, far_high]
        sent_own = [sent, sent_side, sent_over, sent_low, sent_high]
        mine_got = [got, side_got, over_got, far_low_got, far_high_got]
        sent_got = [
            sent_got, sent_side_got, sent_over_got, moved(far_low_got, c_got), moved(far_high_got, c_got),
        ]
        pieces = mine_own + sent_own + mine_got + sent_got
        def listed(first, place):
            out = []
            for n in range(3):
                out += [(first + n, place + 2 * n + h, h) for h in range(2)]
            return out + [(first + 3 + h, place + 6 + h, None) for h in range(2)]

        plans = (listed(10, 0) + listed(5, 8), listed(0, 0) + listed(15, 8))
        starts = [
            slot(flip_c, m) * rows + start
            for flip_c in range(2)
            for m in range(4)
            for start in (0, half)
        ]
        place_at = jnp.stack([own_layer.astype(jnp.int32)] + starts).astype(jnp.int32)
        return pieces, plans, place_at, table, marks

    def scatter_all(lefts, rights):
        order = jnp.stack([slot(1 - k // 4, (k + 3) % 4) for k in range(8)]).astype(jnp.int32)
        if not direct:
            flat = lambda v: v.reshape((-1, v.shape[-1]))
            grads = [inner(flat(l), flat(r)).astype(BF) for l, r in zip(lefts, rights)]
            outs = []
            for grad in (grads[0], jnp.concatenate(grads[1:3], axis=1), grads[3]):
                own = lax.psum_scatter(
                    grad, ("dp", "section"), scatter_dimension=0, tiled=True, axis_index_groups=groups
                )
                outs.append((own, jnp.where(own_layer, own, moved(own, layer_turn)).astype(F32)))
            squares = sum(jnp.sum(jnp.square(own.astype(F32))) for own, _ in outs)
            mark = outs[0][0]
            held = beside_z(beside_x(beside_early(mark), mark), mark)
            return jnp.stack([outs[n][1] for n in (1, 0, 2)]), settled(*beside_last(held, mark), squares)
        half = rows // 2
        send_far, send_rest, kept = weight_grads(order, lefts, rights, rows)
        got_far = moved(send_far, flip_section(1))
        got_rest = moved(after(send_rest, got_far), flip_section(1))
        kept = kept.reshape(3, 4, rows, wide_cols)
        got_rest = got_rest.reshape(3, 3, rows, wide_cols)

        def both(m, cut=slice(None)):
            other = got_far[:, cut] if m == 0 else got_rest[:, m - 1, cut]
            return kept[:, m, cut].astype(F32) + other.astype(F32)

        far_low, far_high = lax.optimization_barrier(
            (both(0, slice(0, half)).astype(BF), both(0, slice(half, rows)).astype(BF))
        )
        first = beside_early(far_low)
        from_side, from_over = moved(far_low, flip_dp(1)), moved(far_high, flip_dp(2))
        from_side, from_over = lax.optimization_barrier((from_side, from_over))
        low_rows = ((0, 0), (0, rows - half), (0, 0))
        high_rows = ((0, 0), (half, 0), (0, 0))
        side = both(2) + jnp.pad(from_over, high_rows).astype(F32)
        over = both(3) + jnp.pad(from_side, low_rows).astype(F32)
        side, over = lax.optimization_barrier((side.astype(BF), over.astype(BF)))

        def totalled(kind, mark):
            one, two = lax.optimization_barrier(
                (moved(side, some(flip_dp(1), kind)), moved(over, some(flip_dp(2), kind)), mark)
            )[:2]
            return after((both(1) + one.astype(F32) + two.astype(F32)).astype(BF))

        second = beside_x(first, side)
        total_far = totalled(False, second)
        away = moved(total_far, layer_turn)
        side, over = lax.optimization_barrier((side, over, total_far))[:2]
        total_own = totalled(True, ())
        small, piece = beside_last(beside_z(second, total_own), ())
        squares = jnp.where(
            own_layer,
            jnp.sum(jnp.square(total_own.astype(F32))),
            jnp.sum(jnp.square(total_far.astype(F32))),
        )
        ends = settled(small, piece, squares)
        away, ends = lax.optimization_barrier((away, ends))
        return jnp.where(own_layer, total_own, away).astype(F32), ends

    def over_section(block):
        other_row = moved(block, flip_section(3))
        pair = jnp.stack([block, other_row])
        other_core = moved(pair, flip_section(1))
        whole = jnp.zeros((sections,) + block.shape, block.dtype)
        for part, flip in ((block, 0), (other_row, 3), (other_core[0], 1), (other_core[1], 2)):
            whole = lax.dynamic_update_slice(
                whole, part[None], (section ^ flip,) + (0,) * block.ndim
            )
        return whole.reshape((sections * block.shape[0],) + block.shape[1:])

    slots = micro * dp * slides * genes
    shrink = 0.5 ** (slots - 1).bit_length()
    def to_first(d, s):
        return (d - near, s) if d >= near and s < 2 else None

    def to_home(d, s):
        return (d + near, s) if d < near and s < 2 else None

    in_rows = w_in.shape[0]

    def embedded(mark):
        own_part, in_rows = final_gain.shape[0], w_in.shape[0]
        gain_high = final_gain.astype(BF)
        gain_low = (final_gain - gain_high.astype(F32)).astype(BF)
        own_ends = jnp.concatenate([head.astype(BF), gain_high[:, None], gain_low[:, None]], axis=1)
        own_ends = jnp.pad(own_ends, ((0, 0), (0, LANES - genes - 2)))
        extra = own_part * LANES // width
        packed = over_section(
            after(jnp.concatenate([w_in.astype(BF), own_ends.reshape(extra, width)])[None], mark)
        )
        in_low = packed[:, :in_rows].reshape(sections * in_rows, width)
        head_p = packed[:, in_rows:].reshape(sections * own_part, LANES)
        full_fgain = (head_p[:, genes].astype(F32) + head_p[:, genes + 1].astype(F32))[None, :]
        table = jax.vmap(lambda c: position_table(c, width), in_axes=1)(after(coords, mark))
        x0 = (
            jnp.dot(tiles.reshape(micro * tok, -1), in_low, preferred_element_type=F32).reshape(
                micro, tok, width
            )
            + table
        ).astype(BF)

        return x0, head_p, full_fgain

    cuts = (((0, 3 * width), (3 * width, wide_cols)), ((0, wide_cols),), ((0, wide_cols),))
    half_packs = micro // 2

    def mine_of(value):
        return lax.dynamic_slice_in_dim(value, core * half_packs, half_packs, 0)

    def exchanged(x0):
        first, known_in, labels_in = lax.optimization_barrier((slide_ids, known, labels, x0))[:3]
        home = mine_of(
            jnp.concatenate(
                [first, known_in.reshape(micro, -1), labels_in.reshape(micro, -1)], axis=1
            )
        )
        other = moved(home, flip_dp(near))
        lower = side_of == 0
        home = jnp.concatenate([jnp.where(lower, home, other), jnp.where(lower, other, home)])
        gain = jnp.where(own_layer, gains[0], moved(gains[0], flip_section(1)))
        return home, gain

    pieces, plans, place_at, (x0, head_p, full_fgain), (home, gain) = gather_all(
        mats[0].astype(BF), embedded, exchanged
    )
    near_packs = mine_of(x0)
    far_packs = moved(near_packs, to_first)
    x0_near = jnp.concatenate([near_packs, near_packs])
    ids = home[:, :tok]
    marks = home[:, tok:].reshape(micro, 2, slides, genes).astype(F32)
    pad = ((0, 0), (0, 16 - slides), (0, LANES - genes))
    known_p = jnp.pad(marks[:, 0], pad)
    labels_p = jnp.pad(marks[:, 1], pad)
    x0_near, lm, ids, gain, pieces, full_fgain, head_p, known_p, labels_p = lax.optimization_barrier(
        (x0_near, log_mult(heads, tok), ids, gain, pieces, full_fgain, head_p, known_p, labels_p)
    )
    wqkv, wo, w1, w2, wqkv_t, wo_t, w1_t, w2_t = load_weights(pieces, plans, place_at, cuts, width)
    ticks = micro + 2 * (sections - 1)
    late = 2 * (sections - 1)
    def scalars(index):
        valid = (index >= 0) & (index < micro)
        return jnp.stack(
            [valid, jnp.clip(index, 0, micro - 1), stage == 0, stage == sections - 1]
        ).astype(jnp.int32)

    arrived = [jnp.zeros((tok, width), BF)] * 2
    bufs = None
    for tick in range(ticks):
        if tick == half_packs:
            x0_near = jnp.concatenate([near_packs, after(far_packs, send)])
        end_args = (full_fgain, head_p, known_p, labels_p)
        send, bufs = forward_call(
            heads, slides, shrink, scalars(tick - 2 * stage), ids, gain, *end_args, x0_near, arrived[tick], lm,
            (wqkv, wo, w1, w2_t, wqkv_t, wo_t, w1_t, w2), bufs,
        )
        arrived.append(moved(send, to_next(1)) if tick + 2 < ticks else None)
    (x_b, qkv_b, lse_b, att_b, mid_b, gp_b, hid_b, a_b, b_b, dl_b, nl_b, dlog_b, side_b) = bufs
    records = (x_b, qkv_b, lse_b, mid_b, gp_b, dl_b)
    arrived = [jnp.zeros((tok, width), BF)] * 2
    bufs = None
    sends = []
    for tick in range(ticks):
        send, bufs = backward_call(
            heads, scalars(tick - 2 * (sections - 1 - stage)), ids, gain, arrived[tick], records,
            lm, (wqkv_t, wo_t, w1_t, w2), bufs,
        )
        sends.append(send)
        arrived.append(moved(send, to_next(-1)) if tick + 2 < ticks else None)
    dbr_b, dup_b, dat_b, dqkv_b, gg_b = bufs
    nl_b, dlog_b, side_b = lax.optimization_barrier((nl_b, dlog_b, side_b, sends[-1]))[:3]
    flat = lambda v: v.reshape((-1, v.shape[-1]))
    bits = [1 << k for k in range(dp.bit_length() - 1)]
    on_last = stage == sections - 1

    def halved(piece, bit):
        size = piece.shape[0] // 2
        up = (dp_index // bit) % 2
        keep = lax.dynamic_slice_in_dim(piece, up * size, size, 0)
        away = lax.dynamic_slice_in_dim(piece, (1 - up) * size, size, 0)
        return (keep.astype(F32) + moved(away, flip_dp(bit)).astype(F32)).astype(BF)

    d_near = jnp.stack(sends[late : late + half_packs])
    d_far = jnp.stack([moved(send, to_home) for send in sends[late + half_packs :]])
    d_rows = jnp.where(stage == 0, d_near, jnp.where(row_of == 0, d_far, jnp.zeros((), BF)))

    def beside_early(mark):
        rows_in = after(d_rows, mark)
        rows_in = rows_in + moved(rows_in, lambda d, s: (d, s ^ 2) if s < 2 else None)
        other = moved(rows_in, flip_section(1))
        rows_in = jnp.concatenate(
            [jnp.where(core == 0, rows_in, other), jnp.where(core == 0, other, rows_in)]
        )
        mine = lax.dynamic_slice_in_dim(flat(tiles), section * in_rows, in_rows, 1)
        piece = inner(mine, flat(rows_in)).astype(BF)
        grad_head = jnp.where(on_last, inner(flat(dlog_b), flat(nl_b)), 0.0)[:genes]
        side = jnp.where(on_last, jnp.sum(side_b, 0), 0.0)[:2]
        seen = jnp.pad(jnp.sum(marks[:, 0]).reshape(1, 1), ((0, 0), (0, width - 1)))
        fill = jnp.zeros((-(5 + genes) % 8, width), F32)
        small = jnp.concatenate([side, grad_head, jnp.sum(gg_b, 0)[:2], seen, fill])
        return small + moved(small, flip_section(1)), piece

    def folded(held, bit, mark):
        small, piece = lax.optimization_barrier((*held, mark))[:2]
        return small + moved(small, flip_dp(bit)), halved(piece, bit)

    def beside_x(held, mark):
        return folded(held, bits[0], mark)

    def beside_z(held, mark):
        for bit in bits[1:-1]:
            held = folded(held, bit, mark)
        return held

    def beside_last(held, mark):
        small, piece = lax.optimization_barrier((*held, mark))[:2]
        return small, (piece.astype(F32) + moved(piece, flip_dp(bits[-1])).astype(F32)).astype(BF)

    lead = (place == 0) & (core == 0)

    def settled(small, piece, squares):
        layer_gain = small[2 + genes : 4 + genes]
        count = jnp.maximum(small[4 + genes, 0], 1.0)
        own_ends = jnp.where(on_last, small[: 2 + genes], 0.0)
        kind = jnp.arange(small.shape[0])[:, None]
        counted = (kind == 0) | ((kind >= 2) & (kind < 4 + genes))
        squares = (
            squares
            + 0.5 * jnp.sum(jnp.square(piece.astype(F32)))
            + jnp.where(lead, jnp.sum(jnp.where(counted, small * small, 0.0)), 0.0)
        )
        sum_gain = jnp.where(own_layer, layer_gain, moved(layer_gain, flip_dp(near)))
        ends = own_ends + moved(own_ends, flip_section(2))
        ends = ends + moved(ends, flip_dp(near))
        loss_sum = jnp.sum(ends[1, :LANES])
        part = width // sections
        mine = lax.dynamic_slice_in_dim(ends, section * part, part, 1)
        return squares.reshape(1, 1), piece, count, loss_sum, sum_gain, mine

    shards, (squares, piece, count, loss_sum, sum_gain, mine) = scatter_all(
        (b_b, a_b, att_b, dbr_b), (dup_b, dqkv_b, dat_b, hid_b)
    )
    part_head, part_fgain = mine[2:].T, mine[0]
    total_sq = spread_sum(squares)
    part_in = after(piece, total_sq)
    for bit in reversed(bits[:-1]):
        up = (dp_index // bit) % 2 == 1
        other = moved(part_in, flip_dp(bit))
        part_in = jnp.concatenate([jnp.where(up, other, part_in), jnp.where(up, part_in, other)])
    part_in = part_in.astype(F32)
    total_sq = total_sq[0, 0]
    shard_wide = shards[None]
    grow = 1.0 / (shrink * count)
    grad_norm = jnp.sqrt(total_sq) * grow
    factor = CLIP / jnp.maximum(grad_norm, CLIP) * grow
    mats_out = adam(mats, shard_wide * factor, mats_m, mats_v, RATE, DECAY)
    gains_out = adam(gains, sum_gain[None] * factor, gains_m, gains_v, RATE_GAIN, 0.0)
    fgain_out = adam(final_gain, part_fgain * factor, fgain_m, fgain_v, RATE_GAIN, 0.0)
    in_out = adam(w_in, part_in * factor, win_m, win_v, RATE, DECAY)
    head_out = adam(head, part_head * factor, head_m, head_v, RATE, DECAY)
    return (
        grad_norm,
        loss_sum,
        count,
        mats_out[0],
        mats_out[1],
        mats_out[2],
        gains_out[0],
        gains_out[1],
        gains_out[2],
        fgain_out[0],
        fgain_out[1],
        fgain_out[2],
        in_out[0],
        in_out[1],
        in_out[2],
        head_out[0],
        head_out[1],
        head_out[2],
    )


def solution(mesh):
    placed = (
        P("dp", None, None),
        P("dp", None),
        P(None, "dp", None),
        P("dp", None, None),
        P("dp", None, None),
        P("section", None, "dp", None),
        P("section", None, "dp", None),
        P("section", None, "dp", None),
        P("section", None, None),
        P("section", None, None),
        P("section", None, None),
        P("section"),
        P("section"),
        P("section"),
        P("section", None),
        P("section", None),
        P("section", None),
        P("section", None),
        P("section", None),
        P("section", None),
    )
    return jax.shard_map(
        per_device,
        mesh=mesh,
        in_specs=placed,
        out_specs=(
            P(),
            P(),
            P(),
            P("section", None, "dp", None),
            P("section", None, "dp", None),
            P("section", None, "dp", None),
            P("section", None, None),
            P("section", None, None),
            P("section", None, None),
            P("section"),
            P("section"),
            P("section"),
            P("section", None),
            P("section", None),
            P("section", None),
            P("section", None),
            P("section", None),
            P("section", None),
        ),
        check_vma=False,
    )
```

```python
import functools

import jax
import jax.numpy as jnp
from jax import lax
from jax.experimental import pallas as pl
from jax.experimental.pallas import tpu as pltpu
from jax.sharding import PartitionSpec as P

HEADS = 16
STEP = 10


EPS_NORM = 1e-05
CLIP = 0.05
BETA_ONE = 0.9
BETA_TWO = 0.95
ADAM_EPS = 1e-08
RATE = 0.06
RATE_GAIN = 1.0
DECAY = 0.1
RATIOS = (1, 2, 4, 8, 16)

def moved(block, route):
    dp, sections = lax.axis_size("dp"), lax.axis_size("section")
    pairs = []
    for d in range(dp):
        for s in range(sections):
            target = route(d, s)
            if target is not None:
                pairs.append((d * sections + s, target[0] * sections + target[1]))
    return lax.ppermute(block, ("dp", "section"), pairs)


def flip_dp(bit):
    return lambda d, s: (d ^ bit, s)


def flip_section(bit):
    return lambda d, s: (d, s ^ bit)


def spread_sum(value):
    dp, sections = lax.axis_size("dp"), lax.axis_size("section")
    for k in range(sections.bit_length() - 1):
        value = value + moved(value, flip_section(1 << k))
    for k in range(dp.bit_length() - 1):
        value = value + moved(value, flip_dp(1 << k))
    return value


def inner(left, right):
    return lax.dot_general(
        left, right, (((0,), (0,)), ((), ())), preferred_element_type=jnp.float32
    )


def position_table(coord, width):
    quarter = width // 4
    freq = jnp.exp(-jnp.log(10000.0) * jnp.arange(quarter, dtype=jnp.float32) / quarter)
    along = coord[0].astype(jnp.float32)[:, None] * freq
    across = coord[1].astype(jnp.float32)[:, None] * freq
    return jnp.concatenate(
        [jnp.sin(along), jnp.cos(along), jnp.sin(across), jnp.cos(across)], axis=1
    )


def log_mult(heads, tok):
    place = jnp.arange(tok, dtype=jnp.int32)
    head_idx = jnp.arange(heads, dtype=jnp.int32)
    mult = jnp.zeros((heads, tok, tok), jnp.float32)
    for ratio in RATIOS:
        hit = (place[None, :] % ratio == head_idx[:, None] % ratio).astype(jnp.float32)
        mult = mult + hit[:, :, None] * hit[:, None, :]
    return jnp.log(mult)


NN = (((1,), (0,)), ((), ()))
NT = (((1,), (1,)), ((), ()))
TN = (((0,), (0,)), ((), ()))
LANES = 128
BF = jnp.bfloat16
F32 = jnp.float32


def mm(left, right, dims=NN):
    return lax.dot_general(left, right, dims, preferred_element_type=F32)


def norm_parts(value):
    mean = jnp.mean(value, -1, keepdims=True)
    centred = value - mean
    var = jnp.mean(centred * centred, -1, keepdims=True)
    inv = lax.rsqrt(var + EPS_NORM)
    return centred * inv, inv


def norm_back(dvalue, gain, hat, inv):
    dhat = dvalue * gain
    return inv * (
        dhat
        - jnp.mean(dhat, -1, keepdims=True)
        - hat * jnp.mean(dhat * hat, -1, keepdims=True)
    )


def window(head, size):
    low = head * size // LANES * LANES
    high = -(-(head + 1) * size // LANES) * LANES
    return low, high


def placed_rows(ref, head, size):
    low, high = window(head, size)
    before, after = head * size - low, high - (head + 1) * size
    tok = ref.shape[1]
    parts = [ref[head * size : (head + 1) * size, :]]
    if before:
        parts = [jnp.zeros((before, tok), ref.dtype)] + parts
    if after:
        parts = parts + [jnp.zeros((after, tok), ref.dtype)]
    return jnp.concatenate(parts, axis=0) if len(parts) > 1 else parts[0]


def same_slide(ids_ref, pick):
    tok = ids_ref.shape[1]
    row = jnp.broadcast_to(ids_ref[pl.ds(pick, 1), :].astype(F32), (tok, tok))
    return row, row.T


def forward_kernel(
    heads, slides, shrink, scal, ids, gain, fgain, head_w, known, label,
    x0, rc, lm_v, wqkv, wo, w1, w2t, wqkv_t, wo_t, w1_t, w2, *rest
):
    fresh = rest[0]
    n_buf = 13
    rest = rest[1:] if fresh else rest[1 + n_buf :]
    send_h = rest[0]
    (x_b, qkv_b, lse_b, att_b, mid_b, gp_b, hid_b, a_b, b_b, dl_b, nl_b, dlog_b, side_b) = rest[1 : 1 + n_buf]
    (x_v, qkv_v, lse_v, att_v, mid_v, gp_v, hid_v, a_v, b_v, o_v,
     q_t, v_t, o_t, pool_v, nl_v, dlog_v, side_v, sin, sout) = rest[1 + n_buf :]
    valid, pick, first, last = scal[0], scal[1], scal[2], scal[3]
    tok, width = x_v.shape
    size = width // heads
    scale = size ** (-0.5)

    @pl.when(valid == 1)
    def _():
        @pl.when(first == 1)
        def _():
            x_v[...] = x0[pick]

        @pl.when(first != 1)
        def _():
            x_v[...] = rc[...]

        outs = []

        def emit(src, dst):
            c = pltpu.make_async_copy(src, dst, sout.at[len(outs)])
            c.start()
            outs.append(c)

        row, col = same_slide(ids, pick)
        same = row == col

        emit(x_v, x_b.at[pick])
        x = x_v[...].astype(F32)
        hat, _ = norm_parts(x)
        a_v[...] = (hat * gain[0:1, :]).astype(BF)
        emit(a_v, a_b.at[pick])
        qkv_v[...] = mm(a_v[...], wqkv[...]).astype(BF)
        emit(qkv_v, qkv_b.at[pick])
        q_t[...] = qkv_v[:, :width].T
        v_t[...] = qkv_v[:, 2 * width :].T
        for h in range(heads):
            low, high = window(h, size)
            s = mm(qkv_v[:, width + low : width + high], placed_rows(q_t, h, size)) * scale
            s = s + jnp.where(same, lm_v[h], -1000000000.0)
            top = jnp.max(s, 0, keepdims=True)
            e = jnp.exp(s - top)
            total = jnp.sum(e, 0, keepdims=True)
            lse_v[h : h + 1, :] = top + jnp.log(total)
            o = mm(v_t[h * size : (h + 1) * size, :], e.astype(BF))
            o_t[h * size : (h + 1) * size, :] = o * (1.0 / total)
        att_v[...] = o_t[...].T.astype(BF)
        emit(lse_v, lse_b.at[pick])
        emit(att_v, att_b.at[pick])
        middle = x + mm(att_v[...], wo[...])
        mid_v[...] = middle
        emit(mid_v, mid_b.at[pick])
        hat, _ = norm_parts(middle)
        b_v[...] = (hat * gain[1:2, :]).astype(BF)
        emit(b_v, b_b.at[pick])
        ff = w1.shape[1]
        part = ff // 4
        for j in range(4):
            cols = slice(j * part, (j + 1) * part)
            up = mm(b_v[...], w1[:, cols])
            square = up * up
            sig = 1.0 / (1.0 + jnp.exp(up * (-1.5957691216057308 - 0.07135481627159852 * square)))
            act = up * sig
            hid_v[:, cols] = act.astype(BF)
            slope = 1.5957691216057308 + 0.21406444881478 * square
            gp_v[:, cols] = sig + act * (1.0 - sig) * slope
            emit(gp_v.at[:, cols], gp_b.at[pick, :, cols])
            emit(hid_v.at[:, cols], hid_b.at[pick, :, cols])
        out = mid_v[...] + mm(hid_v[...], w2t[...])
        send_h[...] = out.astype(BF)

        @pl.when(last == 1)
        def _():
            o_v[...] = out
            pool_v[...] = jnp.zeros_like(pool_v)
            inverse = []
            for s in range(slides):
                inside = (col == float(s)).astype(F32)
                inverse.append(1.0 / jnp.sum(inside, 0, keepdims=True))
                parts = []
                for j in range(width // LANES):
                    parts.append(
                        jnp.sum(o_v[:, j * LANES : (j + 1) * LANES] * inside, 0, keepdims=True) * inverse[s]
                    )
                pool_v[s : s + 1, :] = jnp.concatenate(parts, axis=1)
            hat, inv = norm_parts(pool_v[...])
            low_n = (hat * fgain[...]).astype(BF)
            nl_v[...] = low_n
            logits = mm(low_n, head_w[...])
            kn = known[pick]
            lb = label[pick]
            tail = jnp.exp(-jnp.abs(logits))
            soft = jnp.maximum(logits, 0.0) + jnp.log(1.0 + tail)
            terms = kn * (soft - lb * logits)
            gate = jnp.where(logits >= 0.0, 1.0, tail) / (1.0 + tail)
            dlog = (kn * (gate - lb) * shrink).astype(BF)
            dlog_v[...] = dlog
            d_n = mm(dlog, head_w[...], NT)
            side_v[...] = jnp.zeros_like(side_v)
            side_v[0:1, :] = jnp.sum(d_n * hat, 0, keepdims=True)
            side_v[1:2, 0:LANES] = jnp.sum(terms, 0, keepdims=True)
            d_pool = norm_back(d_n, fgain[...], hat, inv)
            pool_v[...] = d_pool
            for j in range(width // LANES):
                lanes = slice(j * LANES, (j + 1) * LANES)
                acc = jnp.zeros((tok, LANES), F32)
                for s in range(slides):
                    acc = acc + jnp.where(col == float(s), pool_v[s : s + 1, lanes] * inverse[s], 0.0)
                o_v[:, lanes] = acc
            tails = [
                pltpu.make_async_copy(o_v, dl_b.at[pick], sin.at[0]),
                pltpu.make_async_copy(nl_v, nl_b.at[pick], sin.at[1]),
                pltpu.make_async_copy(dlog_v, dlog_b.at[pick], sin.at[2]),
                pltpu.make_async_copy(side_v, side_b.at[pick], sin.at[3]),
            ]
            for c in tails:
                c.start()
            for c in tails:
                c.wait()

        for c in outs:
            c.wait()


def backward_kernel(
    heads, scal, ids, gain, rc_v, dl_b, lm_v, wqkv_t, wo_t, w1_t, w2,
    x_b, qkv_b, lse_b, mid_b, gp_b, *rest
):
    fresh = rest[0]
    n_buf = 5
    rest = rest[1:] if fresh else rest[1 + n_buf :]
    send_h = rest[0]
    outs = rest[1 : 1 + n_buf]
    (dl_v, x_v, qkv_v, lse_v, mid_v, gp_v, dm_v, q_t, k_t, do_v, do_t, dq_t, p_v, ds_v, sin) = rest[1 + n_buf :]
    valid, pick, last = scal[0], scal[1], scal[3]
    dbr_v, dup_v, dat_v, dqkv_v, gg_v = [ref.at[pick] for ref in outs]
    tok, width = x_v.shape
    size = width // heads
    scale = size ** (-0.5)
    per = 8

    @pl.when(valid == 1)
    def _():
        from_head = pltpu.make_async_copy(dl_b.at[pick], dl_v, sin.at[0])

        @pl.when(last == 1)
        def _():
            from_head.start()

        loads = [
            pltpu.make_async_copy(gp_b.at[pick], gp_v, sin.at[1]),
            pltpu.make_async_copy(mid_b.at[pick], mid_v, sin.at[2]),
            pltpu.make_async_copy(qkv_b.at[pick], qkv_v, sin.at[3]),
            pltpu.make_async_copy(lse_b.at[pick], lse_v, sin.at[4]),
            pltpu.make_async_copy(x_b.at[pick], x_v, sin.at[5]),
        ]
        for c in loads:
            c.start()
        row, col = same_slide(ids, pick)
        same = row == col

        @pl.when(last == 1)
        def _():
            from_head.wait()

        @pl.when(last != 1)
        def _():
            dl_v[...] = rc_v[...].astype(F32)

        dbr_v[...] = dl_v[...].astype(BF)
        loads[0].wait()
        ff = w2.shape[1]
        part = ff // 4
        for j in range(4):
            cols = slice(j * part, (j + 1) * part)
            dup_v[:, cols] = (mm(dbr_v[...], w2[:, cols]) * gp_v[:, cols]).astype(BF)
        d_b = mm(dup_v[...], w1_t[...])
        loads[1].wait()
        hat, inv = norm_parts(mid_v[...])
        gg_v[1:2, :] = jnp.sum(d_b * hat, 0, keepdims=True)
        d_mid = dl_v[...] + norm_back(d_b, gain[1:2, :], hat, inv)
        dm_v[...] = d_mid
        dat_v[...] = d_mid.astype(BF)
        loads[2].wait()
        q_t[...] = qkv_v[:, :width].T
        k_t[...] = qkv_v[:, width : 2 * width].T
        do_v[...] = mm(dat_v[...], wo_t[...]).astype(BF)
        do_t[...] = do_v[...].T
        loads[3].wait()
        lane = lax.broadcasted_iota(jnp.int32, (tok, LANES), 1)
        for group in range(heads // per):
            for i in range(per):
                h = group * per + i
                low, high = window(h, size)
                s = mm(qkv_v[:, width + low : width + high], placed_rows(q_t, h, size)) * scale
                s = s + jnp.where(same, lm_v[h], -1000000000.0)
                p = jnp.exp(s - lse_v[h : h + 1, :])
                dp = mm(qkv_v[:, 2 * width + low : 2 * width + high], placed_rows(do_t, h, size))
                inner_sum = jnp.sum(dp * p, 0, keepdims=True)
                ds = (p * (dp - inner_sum)).astype(BF)
                p_v[:, i * tok : (i + 1) * tok] = p.astype(BF)
                ds_v[:, i * tok : (i + 1) * tok] = ds
                dq_t[h * size : (h + 1) * size, :] = mm(k_t[h * size : (h + 1) * size, :], ds) * scale
            base = group * per * size
            for block in range(base // LANES, (base + per * size) // LANES):
                left = block * LANES
                inside = [
                    i for i in range(per)
                    if (group * per + i) * size < left + LANES and (group * per + i + 1) * size > left
                ]
                spans = slice(inside[0] * tok, (inside[-1] + 1) * tok)
                q_parts, o_parts = [], []
                for i in inside:
                    start = (group * per + i) * size - left
                    keep = (lane >= start) & (lane < start + size)
                    q_parts.append(jnp.where(keep, qkv_v[:, left : left + LANES], jnp.zeros((), BF)))
                    o_parts.append(jnp.where(keep, do_v[:, left : left + LANES], jnp.zeros((), BF)))
                dk = mm(ds_v[:, spans], jnp.concatenate(q_parts, axis=0)) * scale
                dv = mm(p_v[:, spans], jnp.concatenate(o_parts, axis=0))
                dqkv_v[:, width + left : width + left + LANES] = dk.astype(BF)
                dqkv_v[:, 2 * width + left : 2 * width + left + LANES] = dv.astype(BF)
        dqkv_v[:, :width] = dq_t[...].T.astype(BF)
        d_a = mm(dqkv_v[...], wqkv_t[...])
        loads[4].wait()
        hat, inv = norm_parts(x_v[...].astype(F32))
        gg_v[0:1, :] = jnp.sum(d_a * hat, 0, keepdims=True)
        send_h[...] = (dm_v[...] + norm_back(d_a, gain[0:1, :], hat, inv)).astype(BF)


def spec_any():
    return pl.BlockSpec(memory_space=pltpu.HBM)


def spec_vmem():
    return pl.BlockSpec(memory_space=pltpu.VMEM)


def resident(value):
    return pltpu.with_memory_space_constraint(value, pltpu.VMEM)


def in_hbm(value):
    return pltpu.with_memory_space_constraint(value, pltpu.HBM)


def after(value, *others):
    return lax.optimization_barrier((value, *others))[0]


def load_body(cuts, plans, scal, *refs):
    n_out = sum(len(c) for c in cuts)
    n_in = len(refs) - 2 * n_out - 1
    pieces, straight, turned, sems = (
        refs[:n_in], refs[n_in : n_in + n_out], refs[n_in + n_out : -1], refs[-1]
    )

    def copies_of(chunk, flag):
        base = sum(len(c) for c in cuts[:chunk])
        out = []
        for n, (piece, place, part) in enumerate(plans[flag]):
            src = pieces[piece] if part is None else pieces[piece].at[part]
            src = src.at[chunk]
            rows = pl.ds(pl.multiple_of(scal[1 + place], 16), src.shape[0])
            for j, (low, high) in enumerate(cuts[chunk]):
                out.append(
                    pltpu.make_async_copy(
                        src.at[:, low:high], straight[base + j].at[rows, :], sems.at[chunk, n, j]
                    )
                )
        return out

    for flag in range(2):

        @pl.when(scal[0] == flag)
        def _():
            for chunk in range(len(cuts)):
                for copy in copies_of(chunk, flag):
                    copy.start()

    base = 0
    for chunk, cut in enumerate(cuts):
        for flag in range(2):

            @pl.when(scal[0] == flag)
            def _():
                for copy in copies_of(chunk, flag):
                    copy.wait()

        for j in range(base, base + len(cut)):
            step = 256

            def turn(index, carry):
                here = pl.ds(pl.multiple_of(index * step, step), step)
                turned[j][:, here] = straight[j][here, :].T
                return carry

            lax.fori_loop(0, straight[j].shape[0] // step, turn, 0)
        base += len(cut)


def load_weights(pieces, plans, scal, cuts, rows):
    sizes = [high - low for cut in cuts for low, high in cut]
    most = max(len(plan) for plan in plans)
    return pl.pallas_call(
        functools.partial(load_body, cuts, plans),
        out_shape=[pltpu.VMEM((rows, n), BF) for n in sizes] + [pltpu.VMEM((n, rows), BF) for n in sizes],
        in_specs=[pl.BlockSpec(memory_space=pltpu.SMEM)]
        + [pl.BlockSpec(memory_space=pl.ANY)] * len(pieces),
        out_specs=[spec_vmem()] * (2 * len(sizes)),
        scratch_shapes=[pltpu.SemaphoreType.DMA((len(cuts), most, 2))],
        compiler_params=pltpu.CompilerParams(vmem_limit_bytes=8 << 20),
        name="load_weights",
    )(scal, *[in_hbm(piece) for piece in pieces])


def weight_grads_body(shape, order, *refs):
    rows, micro, tok = shape
    lefts, rights, outs = refs[:4], refs[4:8], refs[8:11]
    turned, ordered, grad, left_v, hid_v, sin, sout = refs[11:]
    loads = [pltpu.make_async_copy(lefts[n], left_v.at[n], sin.at[n]) for n in range(3)]
    wide = pltpu.make_async_copy(rights[3], hid_v, sin.at[3])
    for copy in loads:
        copy.start()
    wide.start()
    taken = ordered.shape[0]
    cuts = (slice(0, rows), slice(rows, taken // 2), slice(taken // 2, taken))
    step = 768
    copies = []
    attn_cols = rights[1].shape[2]
    for chunk, n, col in ((1, 0, 0), (0, 1, 0), (0, 2, attn_cols), (2, 3, 0)):
        if n < 3:
            loads[n].wait()
            left, right = left_v.at[n], rights[n]
        else:
            wide.wait()
            left, right = lefts[3], hid_v
        for p in range(micro):
            turned[:, p * tok : (p + 1) * tok] = left[p].T
        for k in range(taken // rows):
            here = pl.ds(pl.multiple_of(order[k] * rows, 16), rows)
            ordered[k * rows : (k + 1) * rows, :] = turned[here, :]
        for start in range(0, right.shape[2], step):
            block = right[:, :, start : start + step].reshape(micro * tok, step)
            for low in range(0, taken, taken // 2):
                grad[chunk, low : low + taken // 2, col + start : col + start + step] = mm(
                    ordered[low : low + taken // 2, :], block
                ).astype(BF)
        if n == 1:
            continue
        for m, cut in enumerate(cuts):
            copy = pltpu.make_async_copy(grad.at[chunk, cut], outs[m].at[chunk], sout.at[chunk, m])
            copy.start()
            copies.append(copy)
    for copy in copies:
        copy.wait()


def weight_grads(order, lefts, rights, rows):
    micro, tok, width = lefts[0].shape
    cols = rights[0].shape[2]
    taken = order.shape[0] * rows
    return pl.pallas_call(
        functools.partial(weight_grads_body, (rows, micro, tok)),
        out_shape=[pltpu.HBM((3, n, cols), BF) for n in (rows, taken // 2 - rows, taken // 2)],
        in_specs=[pl.BlockSpec(memory_space=pltpu.SMEM)]
        + [spec_any()] * 3 + [spec_vmem()] * 4 + [spec_any()],
        out_specs=[spec_any()] * 3,
        scratch_shapes=[
            pltpu.VMEM((width, micro * tok), BF), pltpu.VMEM((taken, micro * tok), BF),
            pltpu.VMEM((3, taken, cols), BF), pltpu.VMEM((3, micro, tok, width), BF),
            pltpu.VMEM((micro, tok, cols), BF),
            pltpu.SemaphoreType.DMA((4,)), pltpu.SemaphoreType.DMA((3, 3)),
        ],
        compiler_params=pltpu.CompilerParams(vmem_limit_bytes=34 << 20),
        cost_estimate=pl.CostEstimate(
            flops=6 * micro * tok * taken * cols, bytes_accessed=12 * taken * cols, transcendentals=0
        ),
        name="weight_grads",
    )(
        order, *[in_hbm(v) for v in lefts[:3]], resident(lefts[3]),
        *[resident(v) for v in rights[:3]], in_hbm(rights[3]),
    )


def forward_call(heads, slides, shrink, scal, ids, gain, fgain, head_w, known, label, x0, received, lm, weights, bufs):
    micro, tok, width = x0.shape
    ff = weights[2].shape[1]
    rows = known.shape[1]
    shapes = [
        ((tok, width), BF), ((tok, 3 * width), BF), ((heads, tok), F32), ((tok, width), BF),
        ((tok, width), F32), ((tok, ff), F32), ((tok, ff), BF), ((tok, width), BF), ((tok, width), BF),
        ((tok, width), F32), ((rows, width), BF), ((rows, LANES), BF), ((8, width), F32),
    ]
    fresh = bufs is None
    given = [] if fresh else list(bufs)
    vm = lambda index: pltpu.VMEM(*shapes[index])
    n_in = 18
    out = pl.pallas_call(
        functools.partial(forward_body, heads, slides, shrink, fresh),
        out_shape=[pltpu.VMEM((tok, width), BF)]
        + [pltpu.HBM((micro,) + s, d) for s, d in shapes],
        in_specs=[pl.BlockSpec(memory_space=pltpu.SMEM)]
        + [spec_vmem()] * 17
        + [spec_any()] * len(given),
        out_specs=[spec_vmem()] + [spec_any()] * len(shapes),
        input_output_aliases={n_in + i: 1 + i for i in range(len(given))},
        scratch_shapes=[
            vm(0), vm(1), vm(2), vm(3), vm(4), vm(5), vm(6), vm(7), vm(8),
            pltpu.VMEM((tok, width), F32),
            pltpu.VMEM((width, tok), BF), pltpu.VMEM((width, tok), BF), pltpu.VMEM((width, tok), F32),
            pltpu.VMEM((rows, width), F32), vm(10), vm(11), vm(12),
            pltpu.SemaphoreType.DMA((4,)), pltpu.SemaphoreType.DMA((15,)),
        ],
        compiler_params=pltpu.CompilerParams(vmem_limit_bytes=14 << 20),
        cost_estimate=pl.CostEstimate(flops=7 << 30, bytes_accessed=8 << 20, transcendentals=1 << 20),
        name="layer_forward",
    )(
        scal, ids, gain, fgain, head_w, known, label, resident(x0), received, resident(lm),
        *[resident(w) for w in weights], *[in_hbm(b) for b in given],
    )
    return out[0], out[1:]


def backward_call(heads, scal, ids, gain, received, records, lm, weights, bufs):
    x_b, qkv_b, lse_b, mid_b, gp_b, dl_b = records
    micro, tok, width = x_b.shape
    ff = weights[3].shape[1]
    shapes = [((tok, width), BF), ((tok, ff), BF), ((tok, width), BF), ((tok, 3 * width), BF), ((8, width), F32)]
    fresh = bufs is None
    given = [] if fresh else list(bufs)
    n_in = 15
    out = pl.pallas_call(
        functools.partial(backward_body, heads, fresh),
        out_shape=[pltpu.VMEM((tok, width), BF)]
        + [pltpu.VMEM((micro,) + s, d) for s, d in shapes],
        in_specs=[pl.BlockSpec(memory_space=pltpu.SMEM)] + [spec_vmem()] * 3 + [spec_any()]
        + [spec_vmem()] * 5 + [spec_any()] * 5 + [spec_vmem()] * len(given),
        out_specs=[spec_vmem()] * (1 + len(shapes)),
        input_output_aliases={n_in + i: 1 + i for i in range(len(given))},
        scratch_shapes=[
            pltpu.VMEM((tok, width), F32),
            pltpu.VMEM((tok, width), BF), pltpu.VMEM((tok, 3 * width), BF), pltpu.VMEM((heads, tok), F32),
            pltpu.VMEM((tok, width), F32), pltpu.VMEM((tok, ff), F32),
        ]
        + [
            pltpu.VMEM((tok, width), F32),
            pltpu.VMEM((width, tok), BF), pltpu.VMEM((width, tok), BF),
            pltpu.VMEM((tok, width), BF), pltpu.VMEM((width, tok), BF), pltpu.VMEM((width, tok), F32),
            pltpu.VMEM((tok, 8 * tok), BF), pltpu.VMEM((tok, 8 * tok), BF),
            pltpu.SemaphoreType.DMA((6,)),
        ],
        compiler_params=pltpu.CompilerParams(vmem_limit_bytes=14 << 20),
        cost_estimate=pl.CostEstimate(flops=10 << 30, bytes_accessed=8 << 20, transcendentals=1 << 20),
        name="layer_backward",
    )(
        scal, ids, gain, received, in_hbm(dl_b), resident(lm), *[resident(w) for w in weights],
        *[in_hbm(b) for b in (x_b, qkv_b, lse_b, mid_b, gp_b)], *[resident(b) for b in given],
    )
    return out[0], out[1:]


def forward_body(heads, slides, shrink, fresh, *refs):
    forward_kernel(heads, slides, shrink, *refs[:18], fresh, *refs[18:])


def backward_body(heads, fresh, *refs):
    backward_kernel(heads, *refs[:15], fresh, *refs[15:])


def adam(weight, grad, first, second, rate, decay):
    first = BETA_ONE * first + (1.0 - BETA_ONE) * grad
    second = BETA_TWO * second + (1.0 - BETA_TWO) * grad * grad
    mhat = first / (1.0 - BETA_ONE**STEP)
    vhat = second / (1.0 - BETA_TWO**STEP)
    return (first, second, weight - rate * (mhat / (jnp.sqrt(vhat) + ADAM_EPS) + decay * weight))


def per_device(
    tiles,
    slide_ids,
    coords,
    known,
    labels,
    mats,
    mats_m,
    mats_v,
    gains,
    gains_m,
    gains_v,
    final_gain,
    fgain_m,
    fgain_v,
    w_in,
    win_m,
    win_v,
    head,
    head_m,
    head_v,
):
    sections = lax.axis_size("section")
    dp = lax.axis_size("dp")
    section = lax.axis_index("section")
    dp_index = lax.axis_index("dp")
    near = dp // 2
    side_of, place = dp_index // near, dp_index % near
    row_of, core = section // 2, section % 2
    stage = 2 * row_of + (side_of ^ row_of)
    micro, tok = slide_ids.shape
    heads = HEADS
    slides, genes = known.shape[1:]
    width = w_in.shape[1]
    rows, wide_cols = mats.shape[2:]
    direct = dp == 8 and sections == 4 and rows % 32 == 0

    def join(side, place, row, core):
        return side * near + place, row * 2 + core

    def layer_turn(d, s):
        side, at, row, c = d // near, d % near, s // 2, s % 2
        target = join(c ^ row, at, row, side ^ row)
        return None if target == (d, s) else target

    def pack_turn(d, s):
        side, at, row, c = d // near, d % near, s // 2, s % 2
        target = join(c, at, row, side)
        return None if target == (d, s) else target

    own_layer = side_of == (core ^ row_of)
    own_packs = side_of == core

    def slot(flip_c, flip_m):
        return (core ^ flip_c ^ row_of) * near + (place ^ flip_m)

    groups = [
        [
            (side * near + m) * sections + row * 2 + (half ^ row)
            for half in range(2)
            for m in range(near)
        ]
        for side in range(2)
        for row in range(sections // 2)
    ]

    def to_next(distance):
        def route(d, s):
            side, at, row, c = d // near, d % near, s // 2, s % 2
            goal = 2 * row + (side ^ row) + distance
            if not 0 <= goal < sections:
                return None
            return join((goal % 2) ^ (goal // 2), at, goal // 2, c)

        return route

    def some(route, kind):
        def limited(d, s):
            own = d // near == ((s % 2) ^ (s // 2))
            target = route(d, s)
            return target if kind is None or own == kind else None

        return limited

    def gather_all(low, early, late):
        if not direct:
            own = jnp.where(own_layer, low, moved(low, layer_turn))
            full = lax.all_gather(
                own, ("dp", "section"), axis=1, tiled=True, axis_index_groups=groups
            )
            table = early(())
            marks = late(table[0])
            return [full], ([(0, 0, None)], [(0, 0, None)]), jnp.zeros((2,), jnp.int32), table, marks
        half = rows // 2

        def routes(kind):
            return [some(f, kind) for f in (flip_dp(1), flip_dp(2), flip_section(1))]

        x_own, z_own, c_own = routes(True)
        x_got, z_got, c_got = routes(False)
        together = lax.optimization_barrier
        low = low.reshape(3, 2, half, wide_cols).transpose(1, 0, 2, 3)
        got, side, over = together(
            (moved(low, layer_turn), moved(low, x_own), moved(low, z_own))
        )
        table = early(())
        marks = late(got)
        side_got, over_got, far_low, far_high, sent, sent_got, table = together(
            (
                moved(got, x_got), moved(got, z_got), moved(over[0], x_own), moved(side[1], z_own),
                moved(low, c_own), moved(got, c_got), table,
            )
        )
        far_low_got, far_high_got, sent_side, sent_over, sent_low, sent_high, sent_side_got, sent_over_got = together(
            (
                moved(over_got[0], x_got), moved(side_got[1], z_got),
                moved(side, c_own), moved(over, c_own),
                moved(far_low, c_own), moved(far_high, c_own),
                moved(side_got, c_got), moved(over_got, c_got),
            )
        )
        mine_own = [low, side, over, far_low, far_high]
        sent_own = [sent, sent_side, sent_over, sent_low, sent_high]
        mine_got = [got, side_got, over_got, far_low_got, far_high_got]
        sent_got = [
            sent_got, sent_side_got, sent_over_got, moved(far_low_got, c_got), moved(far_high_got, c_got),
        ]
        pieces = mine_own + sent_own + mine_got + sent_got
        def listed(first, place):
            out = []
            for n in range(3):
                out += [(first + n, place + 2 * n + h, h) for h in range(2)]
            return out + [(first + 3 + h, place + 6 + h, None) for h in range(2)]

        plans = (listed(10, 0) + listed(5, 8), listed(0, 0) + listed(15, 8))
        starts = [
            slot(flip_c, m) * rows + start
            for flip_c in range(2)
            for m in range(4)
            for start in (0, half)
        ]
        place_at = jnp.stack([own_layer.astype(jnp.int32)] + starts).astype(jnp.int32)
        return pieces, plans, place_at, table, marks

    def scatter_all(lefts, rights):
        order = jnp.stack([slot(1 - k // 4, (k + 3) % 4) for k in range(8)]).astype(jnp.int32)
        if not direct:
            flat = lambda v: v.reshape((-1, v.shape[-1]))
            grads = [inner(flat(l), flat(r)).astype(BF) for l, r in zip(lefts, rights)]
            outs = []
            for grad in (grads[0], jnp.concatenate(grads[1:3], axis=1), grads[3]):
                own = lax.psum_scatter(
                    grad, ("dp", "section"), scatter_dimension=0, tiled=True, axis_index_groups=groups
                )
                outs.append((own, jnp.where(own_layer, own, moved(own, layer_turn)).astype(F32)))
            squares = sum(jnp.sum(jnp.square(own.astype(F32))) for own, _ in outs)
            mark = outs[0][0]
            held = beside_z(beside_x(beside_early(mark), mark), mark)
            return jnp.stack([outs[n][1] for n in (1, 0, 2)]), settled(*beside_last(held, mark), squares)
        half = rows // 2
        send_far, send_rest, kept = weight_grads(order, lefts, rights, rows)
        got_far = moved(send_far, flip_section(1))
        got_rest = moved(after(send_rest, got_far), flip_section(1))
        kept = kept.reshape(3, 4, rows, wide_cols)
        got_rest = got_rest.reshape(3, 3, rows, wide_cols)

        def both(m, cut=slice(None)):
            other = got_far[:, cut] if m == 0 else got_rest[:, m - 1, cut]
            return kept[:, m, cut].astype(F32) + other.astype(F32)

        far_low, far_high = lax.optimization_barrier(
            (both(0, slice(0, half)).astype(BF), both(0, slice(half, rows)).astype(BF))
        )
        first = beside_early(far_low)
        from_side, from_over = moved(far_low, flip_dp(1)), moved(far_high, flip_dp(2))
        from_side, from_over = lax.optimization_barrier((from_side, from_over))
        low_rows = ((0, 0), (0, rows - half), (0, 0))
        high_rows = ((0, 0), (half, 0), (0, 0))
        side = both(2) + jnp.pad(from_over, high_rows).astype(F32)
        over = both(3) + jnp.pad(from_side, low_rows).astype(F32)
        side, over = lax.optimization_barrier((side.astype(BF), over.astype(BF)))

        def totalled(kind, mark):
            one, two = lax.optimization_barrier(
                (moved(side, some(flip_dp(1), kind)), moved(over, some(flip_dp(2), kind)), mark)
            )[:2]
            return after((both(1) + one.astype(F32) + two.astype(F32)).astype(BF))

        second = beside_x(first, side)
        total_far = totalled(False, second)
        away = moved(total_far, layer_turn)
        side, over = lax.optimization_barrier((side, over, total_far))[:2]
        total_own = totalled(True, ())
        small, piece = beside_last(beside_z(second, total_own), ())
        squares = jnp.where(
            own_layer,
            jnp.sum(jnp.square(total_own.astype(F32))),
            jnp.sum(jnp.square(total_far.astype(F32))),
        )
        ends = settled(small, piece, squares)
        away, ends = lax.optimization_barrier((away, ends))
        return jnp.where(own_layer, total_own, away).astype(F32), ends

    def over_section(block):
        other_row = moved(block, flip_section(3))
        pair = jnp.stack([block, other_row])
        other_core = moved(pair, flip_section(1))
        whole = jnp.zeros((sections,) + block.shape, block.dtype)
        for part, flip in ((block, 0), (other_row, 3), (other_core[0], 1), (other_core[1], 2)):
            whole = lax.dynamic_update_slice(
                whole, part[None], (section ^ flip,) + (0,) * block.ndim
            )
        return whole.reshape((sections * block.shape[0],) + block.shape[1:])

    slots = micro * dp * slides * genes
    shrink = 0.5 ** (slots - 1).bit_length()
    def to_first(d, s):
        return (d - near, s) if d >= near and s < 2 else None

    def to_home(d, s):
        return (d + near, s) if d < near and s < 2 else None

    in_rows = w_in.shape[0]

    def embedded(mark):
        own_part, in_rows = final_gain.shape[0], w_in.shape[0]
        gain_high = final_gain.astype(BF)
        gain_low = (final_gain - gain_high.astype(F32)).astype(BF)
        own_ends = jnp.concatenate([head.astype(BF), gain_high[:, None], gain_low[:, None]], axis=1)
        own_ends = jnp.pad(own_ends, ((0, 0), (0, LANES - genes - 2)))
        extra = own_part * LANES // width
        packed = over_section(
            after(jnp.concatenate([w_in.astype(BF), own_ends.reshape(extra, width)])[None], mark)
        )
        in_low = packed[:, :in_rows].reshape(sections * in_rows, width)
        head_p = packed[:, in_rows:].reshape(sections * own_part, LANES)
        full_fgain = (head_p[:, genes].astype(F32) + head_p[:, genes + 1].astype(F32))[None, :]
        table = jax.vmap(lambda c: position_table(c, width), in_axes=1)(after(coords, mark))
        x0 = (
            jnp.dot(tiles.reshape(micro * tok, -1), in_low, preferred_element_type=F32).reshape(
                micro, tok, width
            )
            + table
        ).astype(BF)

        return x0, head_p, full_fgain

    cuts = (((0, 3 * width), (3 * width, wide_cols)), ((0, wide_cols),), ((0, wide_cols),))
    half_packs = micro // 2

    def mine_of(value):
        return lax.dynamic_slice_in_dim(value, core * half_packs, half_packs, 0)

    def exchanged(x0):
        first, known_in, labels_in = lax.optimization_barrier((slide_ids, known, labels, x0))[:3]
        home = mine_of(
            jnp.concatenate(
                [first, known_in.reshape(micro, -1), labels_in.reshape(micro, -1)], axis=1
            )
        )
        other = moved(home, flip_dp(near))
        lower = side_of == 0
        home = jnp.concatenate([jnp.where(lower, home, other), jnp.where(lower, other, home)])
        gain = jnp.where(own_layer, gains[0], moved(gains[0], flip_section(1)))
        return home, gain

    pieces, plans, place_at, (x0, head_p, full_fgain), (home, gain) = gather_all(
        mats[0].astype(BF), embedded, exchanged
    )
    near_packs = mine_of(x0)
    far_packs = moved(near_packs, to_first)
    x0_near = jnp.concatenate([near_packs, near_packs])
    ids = home[:, :tok]
    marks = home[:, tok:].reshape(micro, 2, slides, genes).astype(F32)
    pad = ((0, 0), (0, 16 - slides), (0, LANES - genes))
    known_p = jnp.pad(marks[:, 0], pad)
    labels_p = jnp.pad(marks[:, 1], pad)
    x0_near, lm, ids, gain, pieces, full_fgain, head_p, known_p, labels_p = lax.optimization_barrier(
        (x0_near, log_mult(heads, tok), ids, gain, pieces, full_fgain, head_p, known_p, labels_p)
    )
    wqkv, wo, w1, w2, wqkv_t, wo_t, w1_t, w2_t = load_weights(pieces, plans, place_at, cuts, width)
    ticks = micro + 2 * (sections - 1)
    late = 2 * (sections - 1)
    def scalars(index):
        valid = (index >= 0) & (index < micro)
        return jnp.stack(
            [valid, jnp.clip(index, 0, micro - 1), stage == 0, stage == sections - 1]
        ).astype(jnp.int32)

    arrived = [jnp.zeros((tok, width), BF)] * 2
    bufs = None
    for tick in range(ticks):
        if tick == half_packs:
            x0_near = jnp.concatenate([near_packs, after(far_packs, send)])
        end_args = (full_fgain, head_p, known_p, labels_p)
        send, bufs = forward_call(
            heads, slides, shrink, scalars(tick - 2 * stage), ids, gain, *end_args, x0_near, arrived[tick], lm,
            (wqkv, wo, w1, w2_t, wqkv_t, wo_t, w1_t, w2), bufs,
        )
        arrived.append(moved(send, to_next(1)) if tick + 2 < ticks else None)
    (x_b, qkv_b, lse_b, att_b, mid_b, gp_b, hid_b, a_b, b_b, dl_b, nl_b, dlog_b, side_b) = bufs
    records = (x_b, qkv_b, lse_b, mid_b, gp_b, dl_b)
    arrived = [jnp.zeros((tok, width), BF)] * 2
    bufs = None
    sends = []
    for tick in range(ticks):
        send, bufs = backward_call(
            heads, scalars(tick - 2 * (sections - 1 - stage)), ids, gain, arrived[tick], records,
            lm, (wqkv_t, wo_t, w1_t, w2), bufs,
        )
        sends.append(send)
        arrived.append(moved(send, to_next(-1)) if tick + 2 < ticks else None)
    dbr_b, dup_b, dat_b, dqkv_b, gg_b = bufs
    nl_b, dlog_b, side_b = lax.optimization_barrier((nl_b, dlog_b, side_b, sends[-1]))[:3]
    flat = lambda v: v.reshape((-1, v.shape[-1]))
    bits = [1 << k for k in range(dp.bit_length() - 1)]
    on_last = stage == sections - 1

    def halved(piece, bit):
        size = piece.shape[0] // 2
        up = (dp_index // bit) % 2
        keep = lax.dynamic_slice_in_dim(piece, up * size, size, 0)
        away = lax.dynamic_slice_in_dim(piece, (1 - up) * size, size, 0)
        return (keep.astype(F32) + moved(away, flip_dp(bit)).astype(F32)).astype(BF)

    d_near = jnp.stack(sends[late : late + half_packs])
    d_far = jnp.stack([moved(send, to_home) for send in sends[late + half_packs :]])
    d_rows = jnp.where(stage == 0, d_near, jnp.where(row_of == 0, d_far, jnp.zeros((), BF)))

    def beside_early(mark):
        rows_in = after(d_rows, mark)
        rows_in = rows_in + moved(rows_in, lambda d, s: (d, s ^ 2) if s < 2 else None)
        other = moved(rows_in, flip_section(1))
        rows_in = jnp.concatenate(
            [jnp.where(core == 0, rows_in, other), jnp.where(core == 0, other, rows_in)]
        )
        mine = lax.dynamic_slice_in_dim(flat(tiles), section * in_rows, in_rows, 1)
        piece = inner(mine, flat(rows_in)).astype(BF)
        grad_head = jnp.where(on_last, inner(flat(dlog_b), flat(nl_b)), 0.0)[:genes]
        side = jnp.where(on_last, jnp.sum(side_b, 0), 0.0)[:2]
        seen = jnp.pad(jnp.sum(marks[:, 0]).reshape(1, 1), ((0, 0), (0, width - 1)))
        fill = jnp.zeros((-(5 + genes) % 8, width), F32)
        small = jnp.concatenate([side, grad_head, jnp.sum(gg_b, 0)[:2], seen, fill])
        return small + moved(small, flip_section(1)), piece

    def folded(held, bit, mark):
        small, piece = lax.optimization_barrier((*held, mark))[:2]
        return small + moved(small, flip_dp(bit)), halved(piece, bit)

    def beside_x(held, mark):
        return folded(held, bits[0], mark)

    def beside_z(held, mark):
        for bit in bits[1:-1]:
            held = folded(held, bit, mark)
        return held

    def beside_last(held, mark):
        small, piece = lax.optimization_barrier((*held, mark))[:2]
        return small, (piece.astype(F32) + moved(piece, flip_dp(bits[-1])).astype(F32)).astype(BF)

    lead = (place == 0) & (core == 0)

    def settled(small, piece, squares):
        layer_gain = small[2 + genes : 4 + genes]
        count = jnp.maximum(small[4 + genes, 0], 1.0)
        own_ends = jnp.where(on_last, small[: 2 + genes], 0.0)
        kind = jnp.arange(small.shape[0])[:, None]
        counted = (kind == 0) | ((kind >= 2) & (kind < 4 + genes))
        squares = (
            squares
            + 0.5 * jnp.sum(jnp.square(piece.astype(F32)))
            + jnp.where(lead, jnp.sum(jnp.where(counted, small * small, 0.0)), 0.0)
        )
        sum_gain = jnp.where(own_layer, layer_gain, moved(layer_gain, flip_dp(near)))
        ends = own_ends + moved(own_ends, flip_section(2))
        ends = ends + moved(ends, flip_dp(near))
        loss_sum = jnp.sum(ends[1, :LANES])
        part = width // sections
        mine = lax.dynamic_slice_in_dim(ends, section * part, part, 1)
        return squares.reshape(1, 1), piece, count, loss_sum, sum_gain, mine

    shards, (squares, piece, count, loss_sum, sum_gain, mine) = scatter_all(
        (b_b, a_b, att_b, dbr_b), (dup_b, dqkv_b, dat_b, hid_b)
    )
    part_head, part_fgain = mine[2:].T, mine[0]
    total_sq = spread_sum(squares)
    part_in = after(piece, total_sq)
    for bit in reversed(bits[:-1]):
        up = (dp_index // bit) % 2 == 1
        other = moved(part_in, flip_dp(bit))
        part_in = jnp.concatenate([jnp.where(up, other, part_in), jnp.where(up, part_in, other)])
    part_in = part_in.astype(F32)
    total_sq = total_sq[0, 0]
    shard_wide = shards[None]
    grow = 1.0 / (shrink * count)
    grad_norm = jnp.sqrt(total_sq) * grow
    factor = CLIP / jnp.maximum(grad_norm, CLIP) * grow
    mats_out = adam(mats, shard_wide * factor, mats_m, mats_v, RATE, DECAY)
    gains_out = adam(gains, sum_gain[None] * factor, gains_m, gains_v, RATE_GAIN, 0.0)
    fgain_out = adam(final_gain, part_fgain * factor, fgain_m, fgain_v, RATE_GAIN, 0.0)
    in_out = adam(w_in, part_in * factor, win_m, win_v, RATE, DECAY)
    head_out = adam(head, part_head * factor, head_m, head_v, RATE, DECAY)
    return (
        grad_norm,
        loss_sum,
        count,
        mats_out[0],
        mats_out[1],
        mats_out[2],
        gains_out[0],
        gains_out[1],
        gains_out[2],
        fgain_out[0],
        fgain_out[1],
        fgain_out[2],
        in_out[0],
        in_out[1],
        in_out[2],
        head_out[0],
        head_out[1],
        head_out[2],
    )


def solution(mesh):
    placed = (
        P("dp", None, None),
        P("dp", None),
        P(None, "dp", None),
        P("dp", None, None),
        P("dp", None, None),
        P("section", None, "dp", None),
        P("section", None, "dp", None),
        P("section", None, "dp", None),
        P("section", None, None),
        P("section", None, None),
        P("section", None, None),
        P("section"),
        P("section"),
        P("section"),
        P("section", None),
        P("section", None),
        P("section", None),
        P("section", None),
        P("section", None),
        P("section", None),
    )
    return jax.shard_map(
        per_device,
        mesh=mesh,
        in_specs=placed,
        out_specs=(
            P(),
            P(),
            P(),
            P("section", None, "dp", None),
            P("section", None, "dp", None),
            P("section", None, "dp", None),
            P("section", None, None),
            P("section", None, None),
            P("section", None, None),
            P("section"),
            P("section"),
            P("section"),
            P("section", None),
            P("section", None),
            P("section", None),
            P("section", None),
            P("section", None),
            P("section", None),
        ),
        check_vma=False,
    )
```
